256 devices in a mesh: shard: 32 (over z_hi, x, y), rep: 8 (over z_lo, core).
Axes of the slice: x: 4, y: 4, z: 8 (z_hi: 2, z_lo: 4; z = z_hi * 4 + z_lo), core: 2. Of those that a mesh axis runs over, the one named last changes fastest.
Arguments:
- tokens: bfloat16 [8, 4096, 2048], P('rep', 'shard'), may hold values from -8 to 8, as said below
- qkv_weight: bfloat16 [2048, 1536], P('shard'), may hold values from -0.125 to 0.125
- out_weight: bfloat16 [1024, 2048], P('shard'), may hold values from -0.1875 to 0.1875
- cotangent: bfloat16 [8, 4096, 2048], P('rep', 'shard'), may hold values from -6 to 6
Outputs:
- block_output: bfloat16 [8, 4096, 2048], P('rep', 'shard')
- tokens_grad: bfloat16 [8, 4096, 2048], P('rep', 'shard')
- qkv_grad: float32 [2048, 1536], P('shard')
- out_grad: float32 [1024, 2048], P('shard')
The draws below stay inside these ranges and needn't reach their ends.
Inputs may be any that keep to these rules, and one draw needn't show every extreme that they name: `tokens`: each token's activations carry a scale of their own.
All inputs are finite; a program needn't handle non-finite values.
Results may differ from the reference program's by a relative error of at most 0.034.
Values may be sent and summed in bfloat16 or wider, within the bound.
A program may use at most 128 MiB of HBM per device.

```python
import math
import jax
import jax.numpy as jnp
from jax import lax

D = 2048
HEADS = 16
KV_HEADS = 4
HEAD_DIM = 64
TOK_DEV = 128
SEQ = 4096
SEQS = 8
INNER = 1024
QKV = 1536
N_SHARD = 32


def draw_tokens(key, part):
    key = jax.random.fold_in(key, 11)
    base_key, scale_key = jax.random.split(key)
    base = jnp.clip(jax.random.normal(base_key, (SEQS, SEQ, D), jnp.float32), -4.0, 4.0)
    row_scale = jnp.exp(jax.random.uniform(scale_key, (SEQS, SEQ, 1), jnp.float32, math.log(0.5), math.log(2.0)))
    return (base * row_scale).astype(jnp.bfloat16)


def levels(key, dims, cuts, least, largest):
    gain = 1.0
    for position, blocks in cuts:
        heights = jax.random.uniform(jax.random.fold_in(jax.random.fold_in(key, 6), position), (blocks,), jnp.float32, least / len(cuts), largest / len(cuts))
        gain = gain * jnp.repeat(jnp.exp(heights), dims[position] // blocks).reshape((-1,) + (1,) * (len(dims) - 1 - position))
    return gain


def gaussian(stream_key, extent, width, bound, cuts=(), kind=jnp.bfloat16):
    entries = width * jax.random.normal(stream_key, extent, jnp.float32)
    if cuts:
        entries = entries * levels(stream_key, extent, cuts, -0.22, 0.18)
    return jnp.clip(entries, -bound, bound).astype(kind)


def setup_inputs(seed: int = 0) -> dict:
    keys = jax.random.split(jax.random.key(seed), 5)
    return {
        "tokens": draw_tokens(jax.random.fold_in(keys[4], 71), 0),
        "qkv_weight": gaussian(keys[1], (D, QKV), D ** -0.5, 0.125, ((0, 32),)),
        "out_weight": gaussian(keys[2], (INNER, D), INNER ** -0.5, 0.1875, ((0, 32),)),
        "cotangent": gaussian(keys[3], (SEQS, SEQ, D), 1.0, 6.0, ((0, 8), (1, 32))),
    }


ROPE_BASE = 500000.0
NEG_FILL = -1e+30

def tables(positions, head_size):
    halves = head_size // 2
    frequency = ROPE_BASE ** (-(jnp.arange(halves, dtype=jnp.float32) * 2.0) / head_size)
    angles = positions.astype(jnp.float32)[:, None] * frequency[None, :]
    return (jnp.cos(angles), jnp.sin(angles))

def rotate(matrix, cos_rows, sin_rows, head_count):
    row_count = matrix.shape[0]
    head_size = matrix.shape[1] // head_count
    halves = head_size // 2
    pieces = matrix.reshape(row_count, head_count, 2, halves)
    lower_half = pieces[:, :, 0]
    upper_half = pieces[:, :, 1]
    cos_part = cos_rows[:, None, :]
    sin_part = sin_rows[:, None, :]
    turned = jnp.stack([lower_half * cos_part - upper_half * sin_part, upper_half * cos_part + lower_half * sin_part], axis=2)
    return turned.reshape(row_count, head_count * head_size)

def reference(tokens, qkv_weight, out_weight, cotangent):
    inner_width = HEADS * HEAD_DIM
    kv_width = KV_HEADS * HEAD_DIM
    groups = HEADS // KV_HEADS
    logit_scale = HEAD_DIM ** (-0.5)
    positions = jnp.arange(SEQ, dtype=jnp.int32)
    cosine, sine = tables(positions, HEAD_DIM)
    token_pos = positions.reshape(N_SHARD, TOK_DEV)
    block_ids = jnp.arange(N_SHARD, dtype=jnp.int32)

    def sequence(carried, operands):
        inputs, grad_output = operands
        projected = jnp.dot(inputs, qkv_weight, preferred_element_type=jnp.float32)
        queries = rotate(projected[:, :inner_width], cosine, sine, HEADS).astype(jnp.bfloat16)
        key_rows = rotate(projected[:, inner_width:inner_width + kv_width], cosine, sine, KV_HEADS).astype(jnp.bfloat16)
        value_rows = projected[:, inner_width + kv_width:].astype(jnp.bfloat16)
        key_single_precision = key_rows.astype(jnp.float32).reshape(SEQ, KV_HEADS, HEAD_DIM)
        value_single_precision = value_rows.astype(jnp.float32).reshape(SEQ, KV_HEADS, HEAD_DIM)
        query_block_list = queries.reshape(N_SHARD, TOK_DEV, KV_HEADS, groups, HEAD_DIM)

        def block_scores(current_block_index):
            attention_logits = jnp.einsum('nifc,zic->ifnz', query_block_list[current_block_index].astype(jnp.float32), key_single_precision) * logit_scale
            visible = positions[None, :] <= token_pos[current_block_index][:, None]
            return (attention_logits, visible)

        def forward_block(current_block_index):
            attention_logits, visible = block_scores(current_block_index)
            row_peak = lax.optimization_barrier(jnp.max(jnp.where(visible, attention_logits, NEG_FILL), axis=-1, keepdims=True))
            summed = lax.optimization_barrier(jnp.sum(jnp.where(visible, jnp.exp(attention_logits - row_peak), 0.0), axis=-1, keepdims=True))
            log_total = row_peak + jnp.log(summed)
            attention_probabilities = jnp.where(visible, jnp.exp(attention_logits - log_total), 0.0).astype(jnp.bfloat16)
            attention_probabilities = lax.optimization_barrier(attention_probabilities).astype(jnp.float32)
            attended_values = jnp.einsum('ezhm,meo->hezo', attention_probabilities, value_single_precision)
            return (attended_values.reshape(TOK_DEV, inner_width).astype(jnp.bfloat16), log_total)
        attended_values, log_totals = lax.map(forward_block, block_ids)
        flat_attended = attended_values.reshape(SEQ, inner_width)
        block_output = jnp.dot(flat_attended, out_weight, preferred_element_type=jnp.float32).astype(jnp.bfloat16)
        grad_attended = jnp.dot(grad_output, out_weight.T, preferred_element_type=jnp.float32).astype(jnp.bfloat16)
        grad_blocks = grad_attended.reshape(N_SHARD, TOK_DEV, KV_HEADS, groups, HEAD_DIM)
        attn_blocks = attended_values.reshape(N_SHARD, TOK_DEV, KV_HEADS, groups, HEAD_DIM)

        def backward_block(kv_sum, current_block_index):
            attention_logits, visible = block_scores(current_block_index)
            probability = jnp.where(visible, jnp.exp(attention_logits - log_totals[current_block_index]), 0.0)
            gradient_local_block = grad_blocks[current_block_index].astype(jnp.float32)
            row_dots = jnp.einsum('tkgd,tkgd->kgt', gradient_local_block, attn_blocks[current_block_index].astype(jnp.float32))[..., None]
            gradient_probabilities = jnp.einsum('nifc,zic->ifnz', gradient_local_block, value_single_precision)
            score_gradient = lax.optimization_barrier((probability * (gradient_probabilities - row_dots)).astype(jnp.bfloat16)).astype(jnp.float32)
            attention_probabilities = lax.optimization_barrier(probability.astype(jnp.bfloat16)).astype(jnp.float32)
            query_gradient = jnp.einsum('ezhm,meo->hezo', score_gradient, key_single_precision) * logit_scale
            key_contribution = jnp.einsum('jmua,ujmf->ajf', score_gradient, query_block_list[current_block_index].astype(jnp.float32)) * logit_scale
            value_contribution = jnp.einsum('jmua,ujmf->ajf', attention_probabilities, gradient_local_block)
            block_term = jnp.concatenate([key_contribution.reshape(SEQ, kv_width), value_contribution.reshape(SEQ, kv_width)], axis=1)
            block_term = lax.optimization_barrier(block_term.astype(jnp.bfloat16)).astype(jnp.float32)
            return (kv_sum + block_term, query_gradient.reshape(TOK_DEV, inner_width))
        kv_grad, query_gradient = lax.scan(backward_block, jnp.zeros((SEQ, 2 * kv_width), jnp.float32), block_ids)
        query_gradient = rotate(query_gradient.reshape(SEQ, inner_width), cosine, -sine, HEADS).astype(jnp.bfloat16)
        grad_keys = rotate(kv_grad[:, :kv_width], cosine, -sine, KV_HEADS).astype(jnp.bfloat16)
        grad_values = kv_grad[:, kv_width:].astype(jnp.bfloat16)
        grad_proj = jnp.concatenate([query_gradient, grad_keys, grad_values], axis=1)
        tokens_grad = jnp.dot(grad_proj, qkv_weight.T, preferred_element_type=jnp.float32).astype(jnp.bfloat16)
        input_blocks = inputs.reshape(N_SHARD, TOK_DEV, D)
        proj_blocks = grad_proj.reshape(N_SHARD, TOK_DEV, QKV)
        cot_blocks = grad_output.reshape(N_SHARD, TOK_DEV, D)

        def weight_block(sums, current_block_index):
            qkv_term = jnp.dot(input_blocks[current_block_index].T, proj_blocks[current_block_index], preferred_element_type=jnp.float32)
            out_term = jnp.dot(attended_values[current_block_index].T, cot_blocks[current_block_index], preferred_element_type=jnp.float32)
            qkv_term = lax.optimization_barrier(qkv_term.astype(jnp.bfloat16)).astype(jnp.float32)
            out_term = lax.optimization_barrier(out_term.astype(jnp.bfloat16)).astype(jnp.float32)
            return ((sums[0] + qkv_term, sums[1] + out_term), None)
        block_sums, unused_rows = lax.scan(weight_block, carried, block_ids)
        return (block_sums, (block_output, tokens_grad))
    start_sums = (jnp.zeros((D, QKV), jnp.float32), jnp.zeros((INNER, D), jnp.float32))
    totals, results = lax.scan(sequence, start_sums, (tokens, cotangent))
    norm_factor = 1.0 / math.sqrt(SEQS * SEQ)
    return (results[0], results[1], totals[0] * norm_factor, totals[1] * norm_factor)
```

```python
import functools
import math

import jax
import jax.numpy as jnp
from jax import lax
from jax.experimental import pallas as pl
from jax.experimental.pallas import tpu as pltpu
from jax.sharding import PartitionSpec as P

HEADS = 16
KV_HEADS = 4
HEAD_DIM = 64

ROPE_BASE = 500000.0
NEG_FILL = -1e30
MESH = pl.DeviceIdType.MESH
BF16 = jnp.bfloat16
F32 = jnp.float32
VMEM_BYTES = 60 * 1024 * 1024


class Net:
    def __init__(self):
        self.s = lax.axis_index("shard")
        self.r = lax.axis_index("rep")
        self.zh = self.s // 16
        self.x = lax.rem(self.s // 4, 4)
        self.y = lax.rem(self.s, 4)
        self.zl = self.r // 2
        self.core = lax.rem(self.r, 2)
        self.z = self.zh * 4 + self.zl

    def at(self, h, da, db):
        dx, dy = (da, db) if h == 0 else (db, da)
        return lax.rem(self.x + (dx + 4), 4), lax.rem(self.y + (dy + 4), 4)

    def dev(self, h, da, db):
        gx, gy = self.at(h, da, db)
        return (self.zh * 16 + gx * 4 + gy, self.r)

    def sibling(self):
        return (self.s, self.zl * 2 + 1 - self.core)

    def partner(self):
        return (lax.rem(self.s + 16, 32), self.r)

    def up(self, k):
        z = lax.rem(self.z + k, 8)
        return ((z // 4) * 16 + self.x * 4 + self.y, lax.rem(z, 4) * 2 + self.core)

    def xy_neighbours(self):
        return [self.dev(0, 1, 0), self.dev(0, -1, 0), self.dev(0, 0, 1), self.dev(0, 0, -1)]


def greet(devices):
    barrier = pltpu.get_barrier_semaphore()
    for device in devices:
        pl.semaphore_signal(barrier, inc=1, device_id=device, device_id_type=MESH)
    pl.semaphore_wait(barrier, len(devices))


class Wire:
    def __init__(self, send_sems, recv_sems):
        self.send_sems, self.recv_sems = send_sems, recv_sems
        self.used = 0
        self.sent = []

    def new(self, count=1):
        first = self.used
        self.used += count
        return first

    def copy(self, src, dst, key, device):
        return pltpu.make_async_remote_copy(
            src_ref=src,
            dst_ref=dst,
            send_sem=self.send_sems.at[key],
            recv_sem=self.recv_sems.at[key],
            device_id=device,
            device_id_type=MESH,
        )

    def send(self, src, dst, key, device):
        made = self.copy(src, dst, key, device)
        made.start()
        self.sent.append(made)

    def recv(self, ref, key, device):
        self.copy(ref, ref, key, device).wait_recv()

    def drain(self):
        for made in self.sent:
            made.wait_send()
        self.sent = []


SIDES = (1, -1)
RING = (0, 1, -1, 2)
AG_KEYS = 40


def side(d):
    return 0 if d == 1 else 1


def gather_stages(net, wire, own, piece):
    base = wire.new(AG_KEYS)

    def s1(h, d):
        return base + h * 2 + side(d)

    def s2(h, d):
        return base + 4 + h * 2 + side(d)

    def t1(h, da, d):
        return base + 8 + (h * 4 + RING.index(da)) * 2 + side(d)

    def t2(h, da, d):
        return base + 24 + (h * 4 + RING.index(da)) * 2 + side(d)

    def at(h, da, db, part=None):
        return piece(*net.at(h, da, db), h, part)

    def spread(h, da, src):
        for d in SIDES:
            wire.send(src, at(h, da, 0), t1(h, da, d), net.dev(h, 0, d))

    def pass_on(h, da):
        for d in SIDES:
            wire.recv(at(h, da, -d), t1(h, da, d), net.dev(h, 0, -d))
            part = side(d)
            wire.send(at(h, da, -d, part), at(h, da, -d, part), t2(h, da, d), net.dev(h, 0, d))

    def stage_a():
        for h in (0, 1):
            for d in SIDES:
                wire.send(own(h), at(h, 0, 0), s1(h, d), net.dev(h, d, 0))
        for h in (0, 1):
            spread(h, 0, own(h))

    def stage_b():
        for d in SIDES:
            for h in (0, 1):
                wire.recv(at(h, -d, 0), s1(h, d), net.dev(h, -d, 0))
                part = side(d)
                wire.send(at(h, -d, 0, part), at(h, -d, 0, part), s2(h, d), net.dev(h, d, 0))
        for d in SIDES:
            for h in (0, 1):
                spread(h, -d, at(h, -d, 0))

    def stage_c():
        for h in (0, 1):
            pass_on(h, 0)

    def stage_d():
        for h in (0, 1):
            for d in SIDES:
                wire.recv(at(h, 2, 0, side(d)), s2(h, d), net.dev(h, -d, 0))
            spread(h, 2, at(h, 2, 0))

    def stage_e():
        for da in (-1, 1):
            for h in (0, 1):
                pass_on(h, da)

    def stage_f():
        for h in (0, 1):
            pass_on(h, 2)

    def stage_g():
        for da in (0, -1, 1, 2):
            for h in (0, 1):
                for d in SIDES:
                    wire.recv(at(h, da, 2, side(d)), t2(h, da, d), net.dev(h, 0, -d))

    return [stage_a, stage_b, stage_c, stage_d, stage_e, stage_f, stage_g]


def scatter_scratch(rows, cols):
    return [
        pltpu.VMEM((2, 4, 2, rows // 2, cols), BF16),
        pltpu.VMEM((2, 4, 2, rows, cols), BF16),
        pltpu.VMEM((2, 4, 2, rows, cols), BF16),
        pltpu.VMEM((2, 3, rows, cols), F32),
        pltpu.VMEM((2, rows, cols), BF16),
        pltpu.VMEM((2, 2, rows // 2, cols), BF16),
        pltpu.VMEM((2, 2, rows, cols), BF16),
        pltpu.VMEM((2, 2, rows, cols), BF16),
    ]


def scatter_stages(net, wire, own, bufs, emit):
    t2b, t1s, t1b, row_sum, s2s, s2b, s1s, s1b = bufs
    rows = row_sum.shape[2]
    half = rows // 2
    base = wire.new(AG_KEYS)

    def s1(h, d):
        return base + h * 2 + side(d)

    def s2(h, d):
        return base + 4 + h * 2 + side(d)

    def t1(h, i, d):
        return base + 8 + (h * 4 + i) * 2 + side(d)

    def t2(h, i, d):
        return base + 24 + (h * 4 + i) * 2 + side(d)

    def load(h, da, db, part=None):
        return own(*net.at(h, da, db), h, part)[...].astype(F32)

    order = (2, 1, -1, 0)

    def stage_a():
        for da in order:
            i = RING.index(da)
            for h in (0, 1):
                for d in SIDES:
                    p = side(d)
                    wire.send(own(*net.at(h, da, 2), h, p), t2b.at[h, i, p], t2(h, i, d), net.dev(h, 0, d))

    def stage_b():
        for da in order:
            i = RING.index(da)
            for h in (0, 1):
                for d in SIDES:
                    p = side(d)
                    wire.recv(t2b.at[h, i, p], t2(h, i, d), net.dev(h, 0, -d))
                    t1s[h, i, p, pl.ds(p * half, half)] = (
                        load(h, da, d, p) + t2b[h, i, p].astype(F32)
                    ).astype(BF16)
                    t1s[h, i, p, pl.ds((1 - p) * half, half)] = load(h, da, d, 1 - p).astype(BF16)
                    wire.send(t1s.at[h, i, p], t1b.at[h, i, p], t1(h, i, d), net.dev(h, 0, d))

    def stage_c():
        for da in order:
            i = RING.index(da)
            for h in (0, 1):
                for d in SIDES:
                    wire.recv(t1b.at[h, i, side(d)], t1(h, i, d), net.dev(h, 0, -d))
                total = load(h, da, 0) + t1b[h, i, 0].astype(F32) + t1b[h, i, 1].astype(F32)
                if da == 2:
                    s2s[h] = total.astype(BF16)
                    for d in SIDES:
                        p = side(d)
                        wire.send(s2s.at[h, pl.ds(p * half, half)], s2b.at[h, p], s2(h, d), net.dev(h, d, 0))
                else:
                    row_sum[h, i] = total

    def stage_d():
        for h in (0, 1):
            for d in SIDES:
                p = side(d)
                i = RING.index(d)
                wire.recv(s2b.at[h, p], s2(h, d), net.dev(h, -d, 0))
                s1s[h, p, pl.ds(p * half, half)] = (
                    row_sum[h, i, pl.ds(p * half, half)] + s2b[h, p].astype(F32)
                ).astype(BF16)
                s1s[h, p, pl.ds((1 - p) * half, half)] = row_sum[h, i, pl.ds((1 - p) * half, half)].astype(BF16)
                wire.send(s1s.at[h, p], s1b.at[h, p], s1(h, d), net.dev(h, d, 0))

    def stage_e():
        for h in (0, 1):
            for d in SIDES:
                wire.recv(s1b.at[h, side(d)], s1(h, d), net.dev(h, -d, 0))
            emit(h, row_sum[h, 0] + s1b[h, 0].astype(F32) + s1b[h, 1].astype(F32))

    return [stage_a, stage_b, stage_c, stage_d, stage_e]


def weight_gather_kernel(qkv_in, out_in, qkv_full, out_full, send_sems, recv_sems, local_sems):
    net = Net()
    wire = Wire(send_sems, recv_sems)
    core, s = net.core, net.s
    other = 1 - net.zh
    qcols = pl.ds(pl.multiple_of(core * 768, 128), 768)

    def ocols(h):
        return pl.ds(pl.multiple_of(core * 1024 + h * 512, 128), 512)

    def qkv_piece(group):
        def piece(gx, gy, h, part):
            row = (group * 16 + gx * 4 + gy) * 64 + h * 32
            if part is None:
                return qkv_full.at[pl.ds(pl.multiple_of(row, 16), 32), qcols]
            return qkv_full.at[pl.ds(pl.multiple_of(row + part * 16, 16), 16), qcols]

        return piece

    def out_piece(group):
        def piece(gx, gy, h, part):
            row = (group * 16 + gx * 4 + gy) * 32
            if part is None:
                return out_full.at[pl.ds(pl.multiple_of(row, 16), 32), ocols(h)]
            return out_full.at[pl.ds(pl.multiple_of(row + part * 16, 16), 16), ocols(h)]

        return piece

    greet(net.xy_neighbours() + [net.sibling(), net.partner()])

    ohalf = pl.ds(pl.multiple_of(core * 1024, 128), 1024)
    qrow = pl.ds(pl.multiple_of(s * 64, 64), 64)
    orow = pl.ds(pl.multiple_of(s * 32, 32), 32)
    zkey = wire.new(2)
    wire.send(qkv_in.at[:, qcols], qkv_full.at[qrow, qcols], zkey, net.partner())
    wire.send(out_in.at[:, ohalf], out_full.at[orow, ohalf], zkey + 1, net.partner())
    own_q = gather_stages(net, wire, lambda h: qkv_in.at[pl.ds(h * 32, 32), qcols], qkv_piece(net.zh))
    own_o = gather_stages(net, wire, lambda h: out_in.at[:, ocols(h)], out_piece(net.zh))
    for a, b in zip(own_q[:1], own_o[:1]):
        a()
        b()
    keep_q = pltpu.make_async_copy(qkv_in.at[:, qcols], qkv_full.at[qrow, qcols], local_sems.at[0])
    keep_o = pltpu.make_async_copy(out_in.at[:, ohalf], out_full.at[orow, ohalf], local_sems.at[1])
    keep_q.start()
    keep_o.start()
    for a, b in zip(own_q[1:6], own_o[1:6]):
        a()
        b()
    far = lax.rem(s + 16, 32)
    far_q = qkv_full.at[pl.ds(pl.multiple_of(far * 64, 64), 64), qcols]
    far_o = out_full.at[pl.ds(pl.multiple_of(far * 32, 32), 32), ohalf]
    wire.recv(far_q, zkey, net.partner())
    wire.recv(far_o, zkey + 1, net.partner())
    far_qp, far_op = qkv_piece(other), out_piece(other)
    two_q = gather_stages(net, wire, lambda h: far_qp(net.x, net.y, h, None), far_qp)
    two_o = gather_stages(net, wire, lambda h: far_op(net.x, net.y, h, None), far_op)
    two_q[0]()
    two_o[0]()
    own_q[6]()
    own_o[6]()
    keep_q.wait()
    keep_o.wait()

    dkey = wire.new(4)

    def sides_of(group, which):
        cols = pl.ds(pl.multiple_of(which * 768, 128), 768)
        cols_o = pl.ds(pl.multiple_of(which * 1024, 128), 1024)
        return (
            qkv_full.at[pl.ds(pl.multiple_of(group * 1024, 64), 1024), cols],
            out_full.at[pl.ds(pl.multiple_of(group * 512, 32), 512), cols_o],
        )

    def share(group, key):
        for i, ref in enumerate(sides_of(group, core)):
            wire.send(ref, ref, key + i, net.sibling())

    share(net.zh, dkey)
    for a, b in zip(two_q[1:], two_o[1:]):
        a()
        b()
    share(other, dkey + 2)
    for group, key in ((net.zh, dkey), (other, dkey + 2)):
        for i, ref in enumerate(sides_of(group, 1 - core)):
            wire.recv(ref, key + i, net.sibling())
    wire.drain()


def gather_weights(qkv_weight, out_weight):
    keys = 4 * AG_KEYS + 6
    return pl.pallas_call(
        weight_gather_kernel,
        out_shape=(
            jax.ShapeDtypeStruct((2048, 1536), BF16),
            jax.ShapeDtypeStruct((1024, 2048), BF16),
        ),
        in_specs=[pl.BlockSpec(memory_space=pl.ANY)] * 2,
        out_specs=[pl.BlockSpec(memory_space=pl.ANY)] * 2,
        scratch_shapes=[
            pltpu.SemaphoreType.DMA((keys,)),
            pltpu.SemaphoreType.DMA((keys,)),
            pltpu.SemaphoreType.DMA((2,)),
        ],
        compiler_params=pltpu.CompilerParams(collective_id=0, has_side_effects=True),
        name="gather_weights",
    )(qkv_weight, out_weight)


def kv_gather_kernel(kv_in, kv_full, send_sems, recv_sems, local_sems):
    net = Net()
    wire = Wire(send_sems, recv_sems)
    other = 1 - net.zh

    def kv_piece(group):
        def piece(gx, gy, h, part):
            row = (group * 16 + gx * 4 + gy) * 128 + h * 64
            if part is None:
                return kv_full.at[pl.ds(pl.multiple_of(row, 32), 64)]
            return kv_full.at[pl.ds(pl.multiple_of(row + part * 32, 32), 32)]

        return piece

    greet(net.xy_neighbours() + [net.partner()])
    mine = kv_full.at[pl.ds(pl.multiple_of(net.s * 128, 128), 128)]
    zkey = wire.new(1)
    wire.send(kv_in, mine, zkey, net.partner())
    near = gather_stages(net, wire, lambda h: kv_in.at[pl.ds(h * 64, 64)], kv_piece(net.zh))
    near[0]()
    keep = pltpu.make_async_copy(kv_in, mine, local_sems.at[0])
    keep.start()
    for stage in near[1:6]:
        stage()
    far = lax.rem(net.s + 16, 32)
    wire.recv(kv_full.at[pl.ds(pl.multiple_of(far * 128, 128), 128)], zkey, net.partner())
    far_piece = kv_piece(other)
    rest = gather_stages(net, wire, lambda h: far_piece(net.x, net.y, h, None), far_piece)
    rest[0]()
    near[6]()
    for stage in rest[1:]:
        stage()
    keep.wait()
    wire.drain()


def gather_kv(stacked):
    keys = 2 * AG_KEYS + 1
    return pl.pallas_call(
        kv_gather_kernel,
        out_shape=jax.ShapeDtypeStruct((4096, 512), BF16),
        in_specs=[pl.BlockSpec(memory_space=pl.ANY)],
        out_specs=pl.BlockSpec(memory_space=pl.ANY),
        scratch_shapes=[
            pltpu.SemaphoreType.DMA((keys,)),
            pltpu.SemaphoreType.DMA((keys,)),
            pltpu.SemaphoreType.DMA((1,)),
        ],
        compiler_params=pltpu.CompilerParams(collective_id=1, has_side_effects=True),
        name="gather_kv",
    )(stacked)


def kv_scatter_kernel(terms, result, far_out, far_in, send_sems, recv_sems, *bufs):
    net = Net()
    wire = Wire(send_sems, recv_sems)
    far_bufs, near_bufs = bufs[:8], bufs[8:]

    def own(group):
        def piece(gx, gy, h, part):
            row = (group * 16 + gx * 4 + gy) * 128 + h * 64
            if part is None:
                return terms.at[pl.ds(pl.multiple_of(row, 32), 64)]
            return terms.at[pl.ds(pl.multiple_of(row + part * 32, 32), 32)]

        return piece

    greet(net.xy_neighbours() + [net.partner()])
    zkey = wire.new(2)

    def emit_far(h, total):
        far_out[h] = total.astype(BF16)
        wire.send(far_out.at[h], far_in.at[h], zkey + h, net.partner())

    def emit_near(h, total):
        result[pl.ds(h * 64, 64)] = total

    far = scatter_stages(net, wire, own(1 - net.zh), far_bufs, emit_far)
    near = scatter_stages(net, wire, own(net.zh), near_bufs, emit_near)
    far[0]()
    far[1]()
    near[0]()
    far[2]()
    near[1]()
    far[3]()
    near[2]()
    far[4]()
    near[3]()
    near[4]()
    for h in (0, 1):
        wire.recv(far_in.at[h], zkey + h, net.partner())
        result[pl.ds(h * 64, 64)] += far_in[h].astype(F32)
    wire.drain()


def scatter_kv(terms):
    keys = 2 * AG_KEYS + 2
    return pl.pallas_call(
        kv_scatter_kernel,
        out_shape=jax.ShapeDtypeStruct((128, 512), F32),
        in_specs=[pl.BlockSpec(memory_space=pltpu.VMEM)],
        out_specs=pl.BlockSpec(memory_space=pltpu.VMEM),
        scratch_shapes=[
            pltpu.VMEM((2, 64, 512), BF16),
            pltpu.VMEM((2, 64, 512), BF16),
            pltpu.SemaphoreType.DMA((keys,)),
            pltpu.SemaphoreType.DMA((keys,)),
            *scatter_scratch(64, 512),
            *scatter_scratch(64, 512),
        ],
        compiler_params=pltpu.CompilerParams(
            collective_id=2, has_side_effects=True, vmem_limit_bytes=VMEM_BYTES
        ),
        name="scatter_kv",
    )(terms)


def weight_scatter_kernel(
    scale,
    dq,
    do,
    out_q,
    out_o,
    sib_q,
    sib_o,
    sum_q,
    sum_o,
    zs_q,
    zs_o,
    zr_q,
    zr_o,
    keep_q,
    keep_o,
    fin_q,
    fin_o,
    send_sems,
    recv_sems,
    local_sems,
    *bufs,
):
    net = Net()
    wire = Wire(send_sems, recv_sems)
    core = net.core
    cols_q = [pl.ds(pl.multiple_of(c * 768, 128), 768) for c in (core, 1 - core)]
    cols_o = [pl.ds(pl.multiple_of(c * 1024, 128), 1024) for c in (core, 1 - core)]
    greet(net.xy_neighbours() + [net.sibling()] + [net.up(k) for k in range(1, 8)])

    ckey = wire.new(4)
    for g in (0, 1):
        rq, ro = pl.ds(g * 1024, 1024), pl.ds(g * 512, 512)
        wire.send(dq.at[rq, cols_q[1]], sib_q.at[rq], ckey + 2 * g, net.sibling())
        wire.send(do.at[ro, cols_o[1]], sib_o.at[ro], ckey + 2 * g + 1, net.sibling())

    def add_cores(g):
        rq, ro = pl.ds(g * 1024, 1024), pl.ds(g * 512, 512)
        wire.recv(sib_q.at[rq], ckey + 2 * g, net.sibling())
        wire.recv(sib_o.at[ro], ckey + 2 * g + 1, net.sibling())

        def step(i, carry):
            rows = pl.ds(pl.multiple_of(g * 1024 + i * 64, 64), 64)
            sum_q[rows] = (dq[rows, cols_q[0]].astype(F32) + sib_q[rows].astype(F32)).astype(BF16)
            rows = pl.ds(pl.multiple_of(g * 512 + i * 32, 32), 32)
            sum_o[rows] = (do[rows, cols_o[0]].astype(F32) + sib_o[rows].astype(F32)).astype(BF16)
            return carry

        lax.fori_loop(0, 16, step, 0)

    def own_q(g):
        def piece(gx, gy, h, part):
            row = (g * 16 + gx * 4 + gy) * 64 + h * 32
            if part is None:
                return sum_q.at[pl.ds(pl.multiple_of(row, 16), 32)]
            return sum_q.at[pl.ds(pl.multiple_of(row + part * 16, 16), 16)]

        return piece

    def own_o(g):
        def piece(gx, gy, h, part):
            row = (g * 16 + gx * 4 + gy) * 32
            if part is None:
                return sum_o.at[pl.ds(pl.multiple_of(row, 16), 32), pl.ds(h * 512, 512)]
            return sum_o.at[pl.ds(pl.multiple_of(row + part * 16, 16), 16), pl.ds(h * 512, 512)]

        return piece

    def emit_q(g):
        def emit(h, total):
            for part in (0, 1):
                rows = total[part * 16 : part * 16 + 16]
                keep_q[g, 2 * h + part] = rows
                zs_q[g, 2 * h + part] = rows.astype(BF16)

        return emit

    def emit_o(g):
        def emit(h, total):
            for part in (0, 1):
                columns = total[:, part * 256 : part * 256 + 256]
                keep_o[g, 2 * h + part] = columns
                zs_o[g, 2 * h + part] = columns.astype(BF16)

        return emit

    runs = []
    for g in (0, 1):
        runs.append(
            (
                scatter_stages(net, wire, own_q(g), bufs[16 * g : 16 * g + 8], emit_q(g)),
                scatter_stages(net, wire, own_o(g), bufs[16 * g + 8 : 16 * g + 16], emit_o(g)),
            )
        )

    def run(g, stage):
        for stages in runs[g]:
            stages[stage]()

    add_cores(0)
    run(0, 0)
    add_cores(1)
    run(1, 0)
    run(0, 1)
    run(1, 1)
    run(0, 2)
    run(1, 2)
    run(0, 3)
    run(1, 3)
    run(0, 4)
    run(1, 4)

    z1 = wire.new(14)
    for k in range(1, 8):
        target = lax.rem(net.z + k, 8)
        g, l = target // 4, lax.rem(target, 4)
        wire.send(zs_q.at[g, l], zr_q.at[k - 1], z1 + 2 * (k - 1), net.up(k))
        wire.send(zs_o.at[g, l], zr_o.at[k - 1], z1 + 2 * (k - 1) + 1, net.up(k))
    total_q, total_o = keep_q[net.zh, net.zl], keep_o[net.zh, net.zl]
    for k in range(1, 8):
        wire.recv(zr_q.at[k - 1], z1 + 2 * (k - 1), net.up(8 - k))
        wire.recv(zr_o.at[k - 1], z1 + 2 * (k - 1) + 1, net.up(8 - k))
        total_q = total_q + zr_q[k - 1].astype(F32)
        total_o = total_o + zr_o[k - 1].astype(F32)
    fin_q[...] = total_q * scale
    fin_o[...] = total_o * scale

    def place(l):
        return (
            out_q.at[pl.ds(pl.multiple_of(l * 16, 16), 16), cols_q[0]],
            out_o.at[:, pl.ds(pl.multiple_of(core * 1024 + l * 256, 128), 256)],
        )

    def level(k):
        l = lax.rem(net.zl + k, 4)
        return l, (net.s, l * 2 + core)

    z2 = wire.new(6)
    mine = place(net.zl)
    for k in (1, 2, 3):
        device = level(k)[1]
        wire.send(fin_q, mine[0], z2 + 2 * (k - 1), device)
        wire.send(fin_o, mine[1], z2 + 2 * (k - 1) + 1, device)
    own_copies = [
        pltpu.make_async_copy(fin_q, mine[0], local_sems.at[0]),
        pltpu.make_async_copy(fin_o, mine[1], local_sems.at[1]),
    ]
    for made in own_copies:
        made.start()
    for k in (1, 2, 3):
        l, device = level(4 - k)
        there = place(l)
        wire.recv(there[0], z2 + 2 * (k - 1), device)
        wire.recv(there[1], z2 + 2 * (k - 1) + 1, device)
    for made in own_copies:
        made.wait()
    last = wire.new(2)
    wire.send(out_q.at[:, cols_q[0]], out_q.at[:, cols_q[0]], last, net.sibling())
    wire.send(out_o.at[:, cols_o[0]], out_o.at[:, cols_o[0]], last + 1, net.sibling())
    wire.recv(out_q.at[:, cols_q[1]], last, net.sibling())
    wire.recv(out_o.at[:, cols_o[1]], last + 1, net.sibling())
    wire.drain()


def scatter_weights(dq, do, scale):
    keys = 4 * AG_KEYS + 4 + 14 + 6 + 2
    return pl.pallas_call(
        functools.partial(weight_scatter_kernel, scale),
        out_shape=(
            jax.ShapeDtypeStruct((64, 1536), F32),
            jax.ShapeDtypeStruct((32, 2048), F32),
        ),
        in_specs=[pl.BlockSpec(memory_space=pltpu.VMEM)] * 2,
        out_specs=[pl.BlockSpec(memory_space=pltpu.VMEM)] * 2,
        scratch_shapes=[
            pltpu.VMEM((2048, 768), BF16),
            pltpu.VMEM((1024, 1024), BF16),
            pltpu.VMEM((2048, 768), BF16),
            pltpu.VMEM((1024, 1024), BF16),
            pltpu.VMEM((2, 4, 16, 768), BF16),
            pltpu.VMEM((2, 4, 32, 256), BF16),
            pltpu.VMEM((7, 16, 768), BF16),
            pltpu.VMEM((7, 32, 256), BF16),
            pltpu.VMEM((2, 4, 16, 768), F32),
            pltpu.VMEM((2, 4, 32, 256), F32),
            pltpu.VMEM((16, 768), F32),
            pltpu.VMEM((32, 256), F32),
            pltpu.SemaphoreType.DMA((keys,)),
            pltpu.SemaphoreType.DMA((keys,)),
            pltpu.SemaphoreType.DMA((2,)),
            *scatter_scratch(32, 768),
            *scatter_scratch(32, 512),
            *scatter_scratch(32, 768),
            *scatter_scratch(32, 512),
        ],
        compiler_params=pltpu.CompilerParams(
            collective_id=3, has_side_effects=True, vmem_limit_bytes=VMEM_BYTES
        ),
        name="scatter_weights",
    )(dq, do)


def tables(positions, head_size):
    halves = head_size // 2
    frequency = ROPE_BASE ** (-(jnp.arange(halves, dtype=jnp.float32) * 2.0) / head_size)
    angles = positions.astype(jnp.float32)[:, None] * frequency[None, :]
    return (jnp.cos(angles), jnp.sin(angles))


def rotate(matrix, cos_rows, sin_rows, head_count):
    row_count = matrix.shape[0]
    head_size = matrix.shape[1] // head_count
    halves = head_size // 2
    pieces = matrix.reshape(row_count, head_count, 2, halves)
    lower_half = pieces[:, :, 0]
    upper_half = pieces[:, :, 1]
    cos_part = cos_rows[:, None, :]
    sin_part = sin_rows[:, None, :]
    turned = jnp.stack(
        [
            lower_half * cos_part - upper_half * sin_part,
            upper_half * cos_part + lower_half * sin_part,
        ],
        axis=2,
    )
    return turned.reshape(row_count, head_count * head_size)


def body(tokens, qkv_weight, out_weight, cotangent):
    inner_width = HEADS * HEAD_DIM
    kv_width = KV_HEADS * HEAD_DIM
    groups = HEADS // KV_HEADS
    logit_scale = HEAD_DIM ** (-0.5)
    inputs = tokens[0]
    grad_output = cotangent[0]
    tok_count = inputs.shape[0]
    shard_index = lax.axis_index("shard")
    qkv_full, out_full = gather_weights(qkv_weight, out_weight)
    positions = shard_index * tok_count + jnp.arange(tok_count, dtype=jnp.int32)
    cosine, sine = tables(positions, HEAD_DIM)
    projected = jnp.dot(inputs, qkv_full, preferred_element_type=jnp.float32)
    queries = rotate(projected[:, :inner_width], cosine, sine, HEADS).astype(jnp.bfloat16)
    key_rows = rotate(
        projected[:, inner_width : inner_width + kv_width], cosine, sine, KV_HEADS
    ).astype(jnp.bfloat16)
    value_rows = projected[:, inner_width + kv_width :].astype(jnp.bfloat16)
    stacked = jnp.concatenate([key_rows, value_rows], axis=1)
    gathered = gather_kv(stacked)
    seq_len = gathered.shape[0]
    block_len = min(512, seq_len)
    visible_blocks = (shard_index * tok_count + tok_count - 1) // block_len + 1
    grouped_heads = queries.reshape(tok_count, KV_HEADS, groups, HEAD_DIM)

    def key_block(current_block_index):
        block_rows = lax.dynamic_slice_in_dim(
            gathered, current_block_index * block_len, block_len, 0
        )
        key_portion = block_rows[:, :kv_width].reshape(block_len, KV_HEADS, HEAD_DIM)
        value_portion = block_rows[:, kv_width:].reshape(block_len, KV_HEADS, HEAD_DIM)
        return (key_portion, value_portion)

    def block_scores(current_block_index, key_portion):
        attention_logits = (
            jnp.einsum(
                "nifc,zic->ifnz", grouped_heads, key_portion, preferred_element_type=jnp.float32
            )
            * logit_scale
        )
        key_pos = current_block_index * block_len + jnp.arange(block_len, dtype=jnp.int32)
        visible = key_pos[None, :] <= positions[:, None]
        return (attention_logits, visible)

    def first_pass(current_block_index, carried):
        running, summed = carried
        key_portion, value_portion = key_block(current_block_index)
        attention_logits, visible = block_scores(current_block_index, key_portion)
        row_peak = jnp.maximum(
            running, jnp.max(jnp.where(visible, attention_logits, NEG_FILL), axis=-1, keepdims=True)
        )
        fresh = jnp.sum(
            jnp.where(visible, jnp.exp(attention_logits - row_peak), 0.0), axis=-1, keepdims=True
        )
        return (row_peak, summed * jnp.exp(running - row_peak) + fresh)

    start_peak = jnp.full((KV_HEADS, groups, tok_count, 1), NEG_FILL, jnp.float32)
    start_sum = jnp.zeros((KV_HEADS, groups, tok_count, 1), jnp.float32)
    row_peak, summed = lax.fori_loop(0, visible_blocks, first_pass, (start_peak, start_sum))
    log_total = row_peak + jnp.log(summed)

    def second_pass(current_block_index, carried):
        key_portion, value_portion = key_block(current_block_index)
        attention_logits, visible = block_scores(current_block_index, key_portion)
        attention_probabilities = jnp.where(
            visible, jnp.exp(attention_logits - log_total), 0.0
        ).astype(jnp.bfloat16)
        update = jnp.einsum(
            "ezhm,meo->hezo",
            attention_probabilities,
            value_portion,
            preferred_element_type=jnp.float32,
        )
        return carried + update

    empty_out = jnp.zeros((tok_count, KV_HEADS, groups, HEAD_DIM), jnp.float32)
    attended_sum = lax.fori_loop(0, visible_blocks, second_pass, empty_out)
    attended_values = attended_sum.reshape(tok_count, inner_width).astype(jnp.bfloat16)
    block_output = jnp.dot(attended_values, out_full, preferred_element_type=jnp.float32).astype(
        jnp.bfloat16
    )
    grad_attended = lax.dot_general(
        grad_output, out_full, (((1,), (1,)), ((), ())), preferred_element_type=jnp.float32
    ).astype(jnp.bfloat16)
    out_term = lax.dot_general(
        attended_values, grad_output, (((0,), (0,)), ((), ())), preferred_element_type=jnp.float32
    ).astype(jnp.bfloat16)
    gradient_grouped_heads = grad_attended.reshape(tok_count, KV_HEADS, groups, HEAD_DIM)
    attn_grouped = attended_values.reshape(tok_count, KV_HEADS, groups, HEAD_DIM)
    row_dots = jnp.einsum(
        "tkgd,tkgd->kgt", gradient_grouped_heads, attn_grouped, preferred_element_type=jnp.float32
    )[..., None]

    def backward_pass(current_block_index, carried):
        query_sum, term_rows = carried
        key_portion, value_portion = key_block(current_block_index)
        attention_logits, visible = block_scores(current_block_index, key_portion)
        probability = jnp.where(visible, jnp.exp(attention_logits - log_total), 0.0)
        gradient_probabilities = jnp.einsum(
            "nifc,zic->ifnz",
            gradient_grouped_heads,
            value_portion,
            preferred_element_type=jnp.float32,
        )
        score_gradient = (probability * (gradient_probabilities - row_dots)).astype(jnp.bfloat16)
        attention_probabilities = probability.astype(jnp.bfloat16)
        query_sum = query_sum + jnp.einsum(
            "ezhm,meo->hezo", score_gradient, key_portion, preferred_element_type=jnp.float32
        )
        key_contribution = (
            jnp.einsum(
                "jmua,ujmf->ajf", score_gradient, grouped_heads, preferred_element_type=jnp.float32
            )
            * logit_scale
        )
        value_contribution = jnp.einsum(
            "jmua,ujmf->ajf",
            attention_probabilities,
            gradient_grouped_heads,
            preferred_element_type=jnp.float32,
        )
        block_term = jnp.concatenate(
            [
                key_contribution.reshape(block_len, kv_width),
                value_contribution.reshape(block_len, kv_width),
            ],
            axis=1,
        )
        term_rows = lax.dynamic_update_slice_in_dim(
            term_rows, block_term, current_block_index * block_len, 0
        )
        return (query_sum, term_rows)

    empty_terms = jnp.zeros((seq_len, 2 * kv_width), jnp.float32)
    grad_query_sum, key_terms = lax.fori_loop(
        0, visible_blocks, backward_pass, (empty_out, empty_terms)
    )
    kv_grad = scatter_kv(key_terms.astype(jnp.bfloat16))
    query_gradient = rotate(
        grad_query_sum.reshape(tok_count, inner_width) * logit_scale, cosine, -sine, HEADS
    ).astype(jnp.bfloat16)
    grad_keys = rotate(kv_grad[:, :kv_width], cosine, -sine, KV_HEADS).astype(jnp.bfloat16)
    grad_values = kv_grad[:, kv_width:].astype(jnp.bfloat16)
    grad_proj = jnp.concatenate([query_gradient, grad_keys, grad_values], axis=1)
    tokens_grad = lax.dot_general(
        grad_proj, qkv_full, (((1,), (1,)), ((), ())), preferred_element_type=jnp.float32
    ).astype(jnp.bfloat16)
    qkv_term = lax.dot_general(
        inputs, grad_proj, (((0,), (0,)), ((), ())), preferred_element_type=jnp.float32
    ).astype(jnp.bfloat16)
    norm_factor = 1.0 / math.sqrt(lax.axis_size("rep") * seq_len)
    qkv_grad, out_grad = scatter_weights(qkv_term, out_term, norm_factor)
    return (block_output[None], tokens_grad[None], qkv_grad, out_grad)


def solution(mesh):
    return jax.shard_map(
        body,
        mesh=mesh,
        in_specs=(
            P("rep", "shard", None),
            P("shard", None),
            P("shard", None),
            P("rep", "shard", None),
        ),
        out_specs=(
            P("rep", "shard", None),
            P("rep", "shard", None),
            P("shard", None),
            P("shard", None),
        ),
        check_vma=False,
    )
```

```python
import functools
import math

import jax
import jax.numpy as jnp
from jax import lax
from jax.experimental import pallas as pl
from jax.experimental.pallas import tpu as pltpu
from jax.sharding import PartitionSpec as P

HEADS = 16
KV_HEADS = 4
HEAD_DIM = 64

ROPE_BASE = 500000.0
NEG_FILL = -1e30
MESH = pl.DeviceIdType.MESH
BF16 = jnp.bfloat16
F32 = jnp.float32
VMEM_BYTES = 60 * 1024 * 1024


class Net:
    def __init__(self):
        self.s = lax.axis_index("shard")
        self.r = lax.axis_index("rep")
        self.zh = self.s // 16
        self.x = lax.rem(self.s // 4, 4)
        self.y = lax.rem(self.s, 4)
        self.zl = self.r // 2
        self.core = lax.rem(self.r, 2)
        self.z = self.zh * 4 + self.zl

    def at(self, h, da, db):
        dx, dy = (da, db) if h == 0 else (db, da)
        return lax.rem(self.x + (dx + 4), 4), lax.rem(self.y + (dy + 4), 4)

    def dev(self, h, da, db):
        gx, gy = self.at(h, da, db)
        return (self.zh * 16 + gx * 4 + gy, self.r)

    def sibling(self):
        return (self.s, self.zl * 2 + 1 - self.core)

    def partner(self):
        return (lax.rem(self.s + 16, 32), self.r)

    def up(self, k):
        z = lax.rem(self.z + k, 8)
        return ((z // 4) * 16 + self.x * 4 + self.y, lax.rem(z, 4) * 2 + self.core)

    def xy_neighbours(self):
        return [self.dev(0, 1, 0), self.dev(0, -1, 0), self.dev(0, 0, 1), self.dev(0, 0, -1)]


def greet(devices):
    barrier = pltpu.get_barrier_semaphore()
    for device in devices:
        pl.semaphore_signal(barrier, inc=1, device_id=device, device_id_type=MESH)
    pl.semaphore_wait(barrier, len(devices))


class Wire:
    def __init__(self, send_sems, recv_sems):
        self.send_sems, self.recv_sems = send_sems, recv_sems
        self.used = 0
        self.sent = []

    def new(self, count=1):
        first = self.used
        self.used += count
        return first

    def copy(self, src, dst, key, device):
        return pltpu.make_async_remote_copy(
            src_ref=src,
            dst_ref=dst,
            send_sem=self.send_sems.at[key],
            recv_sem=self.recv_sems.at[key],
            device_id=device,
            device_id_type=MESH,
        )

    def send(self, src, dst, key, device):
        made = self.copy(src, dst, key, device)
        made.start()
        self.sent.append(made)

    def recv(self, ref, key, device):
        self.copy(ref, ref, key, device).wait_recv()

    def drain(self):
        for made in self.sent:
            made.wait_send()
        self.sent = []


SIDES = (1, -1)
RING = (0, 1, -1, 2)
AG_KEYS = 40


def side(d):
    return 0 if d == 1 else 1


def gather_stages(net, wire, own, piece):
    base = wire.new(AG_KEYS)

    def s1(h, d):
        return base + h * 2 + side(d)

    def s2(h, d):
        return base + 4 + h * 2 + side(d)

    def t1(h, da, d):
        return base + 8 + (h * 4 + RING.index(da)) * 2 + side(d)

    def t2(h, da, d):
        return base + 24 + (h * 4 + RING.index(da)) * 2 + side(d)

    def at(h, da, db, part=None):
        return piece(*net.at(h, da, db), h, part)

    def spread(h, da, src):
        for d in SIDES:
            wire.send(src, at(h, da, 0), t1(h, da, d), net.dev(h, 0, d))

    def pass_on(h, da):
        for d in SIDES:
            wire.recv(at(h, da, -d), t1(h, da, d), net.dev(h, 0, -d))
            part = side(d)
            wire.send(at(h, da, -d, part), at(h, da, -d, part), t2(h, da, d), net.dev(h, 0, d))

    def stage_a():
        for h in (0, 1):
            for d in SIDES:
                wire.send(own(h), at(h, 0, 0), s1(h, d), net.dev(h, d, 0))
        for h in (0, 1):
            spread(h, 0, own(h))

    def stage_b():
        for d in SIDES:
            for h in (0, 1):
                wire.recv(at(h, -d, 0), s1(h, d), net.dev(h, -d, 0))
                part = side(d)
                wire.send(at(h, -d, 0, part), at(h, -d, 0, part), s2(h, d), net.dev(h, d, 0))
        for d in SIDES:
            for h in (0, 1):
                spread(h, -d, at(h, -d, 0))

    def stage_c():
        for h in (0, 1):
            pass_on(h, 0)

    def stage_d():
        for h in (0, 1):
            for d in SIDES:
                wire.recv(at(h, 2, 0, side(d)), s2(h, d), net.dev(h, -d, 0))
            spread(h, 2, at(h, 2, 0))

    def stage_e():
        for da in (-1, 1):
            for h in (0, 1):
                pass_on(h, da)

    def stage_f():
        for h in (0, 1):
            pass_on(h, 2)

    def stage_g():
        for da in (0, -1, 1, 2):
            for h in (0, 1):
                for d in SIDES:
                    wire.recv(at(h, da, 2, side(d)), t2(h, da, d), net.dev(h, 0, -d))

    return [stage_a, stage_b, stage_c, stage_d, stage_e, stage_f, stage_g]


def scatter_scratch(rows, cols):
    return [
        pltpu.VMEM((2, 4, 2, rows // 2, cols), BF16),
        pltpu.VMEM((2, 4, 2, rows, cols), BF16),
        pltpu.VMEM((2, 4, 2, rows, cols), BF16),
        pltpu.VMEM((2, 3, rows, cols), F32),
        pltpu.VMEM((2, rows, cols), BF16),
        pltpu.VMEM((2, 2, rows // 2, cols), BF16),
        pltpu.VMEM((2, 2, rows, cols), BF16),
        pltpu.VMEM((2, 2, rows, cols), BF16),
    ]


def scatter_stages(net, wire, own, bufs, emit):
    t2b, t1s, t1b, row_sum, s2s, s2b, s1s, s1b = bufs
    rows = row_sum.shape[2]
    half = rows // 2
    base = wire.new(AG_KEYS)

    def s1(h, d):
        return base + h * 2 + side(d)

    def s2(h, d):
        return base + 4 + h * 2 + side(d)

    def t1(h, i, d):
        return base + 8 + (h * 4 + i) * 2 + side(d)

    def t2(h, i, d):
        return base + 24 + (h * 4 + i) * 2 + side(d)

    def load(h, da, db, part=None):
        return own(*net.at(h, da, db), h, part)[...].astype(F32)

    order = (2, 1, -1, 0)

    def stage_a():
        for da in order:
            i = RING.index(da)
            for h in (0, 1):
                for d in SIDES:
                    p = side(d)
                    wire.send(own(*net.at(h, da, 2), h, p), t2b.at[h, i, p], t2(h, i, d), net.dev(h, 0, d))

    def stage_b():
        for da in order:
            i = RING.index(da)
            for h in (0, 1):
                for d in SIDES:
                    p = side(d)
                    wire.recv(t2b.at[h, i, p], t2(h, i, d), net.dev(h, 0, -d))
                    t1s[h, i, p, pl.ds(p * half, half)] = (
                        load(h, da, d, p) + t2b[h, i, p].astype(F32)
                    ).astype(BF16)
                    t1s[h, i, p, pl.ds((1 - p) * half, half)] = load(h, da, d, 1 - p).astype(BF16)
                    wire.send(t1s.at[h, i, p], t1b.at[h, i, p], t1(h, i, d), net.dev(h, 0, d))

    def stage_c():
        for da in order:
            i = RING.index(da)
            for h in (0, 1):
                for d in SIDES:
                    wire.recv(t1b.at[h, i, side(d)], t1(h, i, d), net.dev(h, 0, -d))
                total = load(h, da, 0) + t1b[h, i, 0].astype(F32) + t1b[h, i, 1].astype(F32)
                if da == 2:
                    s2s[h] = total.astype(BF16)
                    for d in SIDES:
                        p = side(d)
                        wire.send(s2s.at[h, pl.ds(p * half, half)], s2b.at[h, p], s2(h, d), net.dev(h, d, 0))
                else:
                    row_sum[h, i] = total

    def stage_d():
        for h in (0, 1):
            for d in SIDES:
                p = side(d)
                i = RING.index(d)
                wire.recv(s2b.at[h, p], s2(h, d), net.dev(h, -d, 0))
                s1s[h, p, pl.ds(p * half, half)] = (
                    row_sum[h, i, pl.ds(p * half, half)] + s2b[h, p].astype(F32)
                ).astype(BF16)
                s1s[h, p, pl.ds((1 - p) * half, half)] = row_sum[h, i, pl.ds((1 - p) * half, half)].astype(BF16)
                wire.send(s1s.at[h, p], s1b.at[h, p], s1(h, d), net.dev(h, d, 0))

    def stage_e():
        for h in (0, 1):
            for d in SIDES:
                wire.recv(s1b.at[h, side(d)], s1(h, d), net.dev(h, -d, 0))
            emit(h, row_sum[h, 0] + s1b[h, 0].astype(F32) + s1b[h, 1].astype(F32))

    return [stage_a, stage_b, stage_c, stage_d, stage_e]


def weight_gather_kernel(qkv_in, out_in, qkv_full, out_full, send_sems, recv_sems, local_sems):
    net = Net()
    wire = Wire(send_sems, recv_sems)
    core, s = net.core, net.s
    other = 1 - net.zh
    qcols = pl.ds(pl.multiple_of(core * 768, 128), 768)

    def ocols(h):
        return pl.ds(pl.multiple_of(core * 1024 + h * 512, 128), 512)

    def qkv_piece(group):
        def piece(gx, gy, h, part):
            row = (group * 16 + gx * 4 + gy) * 64 + h * 32
            if part is None:
                return qkv_full.at[pl.ds(pl.multiple_of(row, 16), 32), qcols]
            return qkv_full.at[pl.ds(pl.multiple_of(row + part * 16, 16), 16), qcols]

        return piece

    def out_piece(group):
        def piece(gx, gy, h, part):
            row = (group * 16 + gx * 4 + gy) * 32
            if part is None:
                return out_full.at[pl.ds(pl.multiple_of(row, 16), 32), ocols(h)]
            return out_full.at[pl.ds(pl.multiple_of(row + part * 16, 16), 16), ocols(h)]

        return piece

    greet(net.xy_neighbours() + [net.sibling(), net.partner()])

    ohalf = pl.ds(pl.multiple_of(core * 1024, 128), 1024)
    qrow = pl.ds(pl.multiple_of(s * 64, 64), 64)
    orow = pl.ds(pl.multiple_of(s * 32, 32), 32)
    zkey = wire.new(2)
    wire.send(qkv_in.at[:, qcols], qkv_full.at[qrow, qcols], zkey, net.partner())
    wire.send(out_in.at[:, ohalf], out_full.at[orow, ohalf], zkey + 1, net.partner())
    own_q = gather_stages(net, wire, lambda h: qkv_in.at[pl.ds(h * 32, 32), qcols], qkv_piece(net.zh))
    own_o = gather_stages(net, wire, lambda h: out_in.at[:, ocols(h)], out_piece(net.zh))
    for a, b in zip(own_q[:1], own_o[:1]):
        a()
        b()
    keep_q = pltpu.make_async_copy(qkv_in.at[:, qcols], qkv_full.at[qrow, qcols], local_sems.at[0])
    keep_o = pltpu.make_async_copy(out_in.at[:, ohalf], out_full.at[orow, ohalf], local_sems.at[1])
    keep_q.start()
    keep_o.start()
    for a, b in zip(own_q[1:6], own_o[1:6]):
        a()
        b()
    far = lax.rem(s + 16, 32)
    far_q = qkv_full.at[pl.ds(pl.multiple_of(far * 64, 64), 64), qcols]
    far_o = out_full.at[pl.ds(pl.multiple_of(far * 32, 32), 32), ohalf]
    wire.recv(far_q, zkey, net.partner())
    wire.recv(far_o, zkey + 1, net.partner())
    far_qp, far_op = qkv_piece(other), out_piece(other)
    two_q = gather_stages(net, wire, lambda h: far_qp(net.x, net.y, h, None), far_qp)
    two_o = gather_stages(net, wire, lambda h: far_op(net.x, net.y, h, None), far_op)
    two_q[0]()
    two_o[0]()
    own_q[6]()
    own_o[6]()
    keep_q.wait()
    keep_o.wait()

    dkey = wire.new(4)

    def sides_of(group, which):
        cols = pl.ds(pl.multiple_of(which * 768, 128), 768)
        cols_o = pl.ds(pl.multiple_of(which * 1024, 128), 1024)
        return (
            qkv_full.at[pl.ds(pl.multiple_of(group * 1024, 64), 1024), cols],
            out_full.at[pl.ds(pl.multiple_of(group * 512, 32), 512), cols_o],
        )

    def share(group, key):
        for i, ref in enumerate(sides_of(group, core)):
            wire.send(ref, ref, key + i, net.sibling())

    share(net.zh, dkey)
    for a, b in zip(two_q[1:], two_o[1:]):
        a()
        b()
    share(other, dkey + 2)
    for group, key in ((net.zh, dkey), (other, dkey + 2)):
        for i, ref in enumerate(sides_of(group, 1 - core)):
            wire.recv(ref, key + i, net.sibling())
    wire.drain()


def gather_weights(qkv_weight, out_weight):
    keys = 4 * AG_KEYS + 6
    return pl.pallas_call(
        weight_gather_kernel,
        out_shape=(
            jax.ShapeDtypeStruct((2048, 1536), BF16),
            jax.ShapeDtypeStruct((1024, 2048), BF16),
        ),
        in_specs=[pl.BlockSpec(memory_space=pl.ANY)] * 2,
        out_specs=[pl.BlockSpec(memory_space=pl.ANY)] * 2,
        scratch_shapes=[
            pltpu.SemaphoreType.DMA((keys,)),
            pltpu.SemaphoreType.DMA((keys,)),
            pltpu.SemaphoreType.DMA((2,)),
        ],
        compiler_params=pltpu.CompilerParams(collective_id=0, has_side_effects=True),
        name="gather_weights",
    )(qkv_weight, out_weight)


def kv_gather_kernel(kv_in, kv_full, send_sems, recv_sems, local_sems):
    net = Net()
    wire = Wire(send_sems, recv_sems)
    other = 1 - net.zh

    def kv_piece(group):
        def piece(gx, gy, h, part):
            row = (group * 16 + gx * 4 + gy) * 128 + h * 64
            if part is None:
                return kv_full.at[pl.ds(pl.multiple_of(row, 32), 64)]
            return kv_full.at[pl.ds(pl.multiple_of(row + part * 32, 32), 32)]

        return piece

    greet(net.xy_neighbours() + [net.partner()])
    mine = kv_full.at[pl.ds(pl.multiple_of(net.s * 128, 128), 128)]
    zkey = wire.new(1)
    wire.send(kv_in, mine, zkey, net.partner())
    near = gather_stages(net, wire, lambda h: kv_in.at[pl.ds(h * 64, 64)], kv_piece(net.zh))
    near[0]()
    keep = pltpu.make_async_copy(kv_in, mine, local_sems.at[0])
    keep.start()
    for stage in near[1:6]:
        stage()
    far = lax.rem(net.s + 16, 32)
    wire.recv(kv_full.at[pl.ds(pl.multiple_of(far * 128, 128), 128)], zkey, net.partner())
    far_piece = kv_piece(other)
    rest = gather_stages(net, wire, lambda h: far_piece(net.x, net.y, h, None), far_piece)
    rest[0]()
    near[6]()
    for stage in rest[1:]:
        stage()
    keep.wait()
    wire.drain()


def gather_kv(stacked):
    keys = 2 * AG_KEYS + 1
    return pl.pallas_call(
        kv_gather_kernel,
        out_shape=jax.ShapeDtypeStruct((4096, 512), BF16),
        in_specs=[pl.BlockSpec(memory_space=pl.ANY)],
        out_specs=pl.BlockSpec(memory_space=pl.ANY),
        scratch_shapes=[
            pltpu.SemaphoreType.DMA((keys,)),
            pltpu.SemaphoreType.DMA((keys,)),
            pltpu.SemaphoreType.DMA((1,)),
        ],
        compiler_params=pltpu.CompilerParams(collective_id=1, has_side_effects=True),
        name="gather_kv",
    )(stacked)


def kv_scatter_kernel(terms, result, far_out, far_in, send_sems, recv_sems, *bufs):
    net = Net()
    wire = Wire(send_sems, recv_sems)
    far_bufs, near_bufs = bufs[:8], bufs[8:]

    def own(group):
        def piece(gx, gy, h, part):
            row = (group * 16 + gx * 4 + gy) * 128 + h * 64
            if part is None:
                return terms.at[pl.ds(pl.multiple_of(row, 32), 64)]
            return terms.at[pl.ds(pl.multiple_of(row + part * 32, 32), 32)]

        return piece

    greet(net.xy_neighbours() + [net.partner()])
    zkey = wire.new(2)

    def emit_far(h, total):
        far_out[h] = total.astype(BF16)
        wire.send(far_out.at[h], far_in.at[h], zkey + h, net.partner())

    def emit_near(h, total):
        result[pl.ds(h * 64, 64)] = total

    far = scatter_stages(net, wire, own(1 - net.zh), far_bufs, emit_far)
    near = scatter_stages(net, wire, own(net.zh), near_bufs, emit_near)
    far[0]()
    far[1]()
    near[0]()
    far[2]()
    near[1]()
    far[3]()
    near[2]()
    far[4]()
    near[3]()
    near[4]()
    for h in (0, 1):
        wire.recv(far_in.at[h], zkey + h, net.partner())
        result[pl.ds(h * 64, 64)] += far_in[h].astype(F32)
    wire.drain()


def scatter_kv(terms):
    keys = 2 * AG_KEYS + 2
    return pl.pallas_call(
        kv_scatter_kernel,
        out_shape=jax.ShapeDtypeStruct((128, 512), F32),
        in_specs=[pl.BlockSpec(memory_space=pltpu.VMEM)],
        out_specs=pl.BlockSpec(memory_space=pltpu.VMEM),
        scratch_shapes=[
            pltpu.VMEM((2, 64, 512), BF16),
            pltpu.VMEM((2, 64, 512), BF16),
            pltpu.SemaphoreType.DMA((keys,)),
            pltpu.SemaphoreType.DMA((keys,)),
            *scatter_scratch(64, 512),
            *scatter_scratch(64, 512),
        ],
        compiler_params=pltpu.CompilerParams(
            collective_id=2, has_side_effects=True, vmem_limit_bytes=VMEM_BYTES
        ),
        name="scatter_kv",
    )(terms)


def weight_scatter_kernel(
    scale,
    dq,
    do,
    out_q,
    out_o,
    sib_q,
    sib_o,
    sum_q,
    sum_o,
    zs_q,
    zs_o,
    zr_q,
    zr_o,
    keep_q,
    keep_o,
    fin_q,
    fin_o,
    send_sems,
    recv_sems,
    local_sems,
    *bufs,
):
    net = Net()
    wire = Wire(send_sems, recv_sems)
    core = net.core
    cols_q = [pl.ds(pl.multiple_of(c * 768, 128), 768) for c in (core, 1 - core)]
    cols_o = [pl.ds(pl.multiple_of(c * 1024, 128), 1024) for c in (core, 1 - core)]
    greet(net.xy_neighbours() + [net.sibling()] + [net.up(k) for k in range(1, 8)])

    ckey = wire.new(4)
    for g in (0, 1):
        rq, ro = pl.ds(g * 1024, 1024), pl.ds(g * 512, 512)
        wire.send(dq.at[rq, cols_q[1]], sib_q.at[rq], ckey + 2 * g, net.sibling())
        wire.send(do.at[ro, cols_o[1]], sib_o.at[ro], ckey + 2 * g + 1, net.sibling())

    def add_cores(g):
        rq, ro = pl.ds(g * 1024, 1024), pl.ds(g * 512, 512)
        wire.recv(sib_q.at[rq], ckey + 2 * g, net.sibling())
        wire.recv(sib_o.at[ro], ckey + 2 * g + 1, net.sibling())

        def step(i, carry):
            rows = pl.ds(pl.multiple_of(g * 1024 + i * 64, 64), 64)
            sum_q[rows] = (dq[rows, cols_q[0]].astype(F32) + sib_q[rows].astype(F32)).astype(BF16)
            rows = pl.ds(pl.multiple_of(g * 512 + i * 32, 32), 32)
            sum_o[rows] = (do[rows, cols_o[0]].astype(F32) + sib_o[rows].astype(F32)).astype(BF16)
            return carry

        lax.fori_loop(0, 16, step, 0)

    def own_q(g):
        def piece(gx, gy, h, part):
            row = (g * 16 + gx * 4 + gy) * 64 + h * 32
            if part is None:
                return sum_q.at[pl.ds(pl.multiple_of(row, 16), 32)]
            return sum_q.at[pl.ds(pl.multiple_of(row + part * 16, 16), 16)]

        return piece

    def own_o(g):
        def piece(gx, gy, h, part):
            row = (g * 16 + gx * 4 + gy) * 32
            if part is None:
                return sum_o.at[pl.ds(pl.multiple_of(row, 16), 32), pl.ds(h * 512, 512)]
            return sum_o.at[pl.ds(pl.multiple_of(row + part * 16, 16), 16), pl.ds(h * 512, 512)]

        return piece

    def emit_q(g):
        def emit(h, total):
            for part in (0, 1):
                rows = total[part * 16 : part * 16 + 16]
                keep_q[g, 2 * h + part] = rows
                zs_q[g, 2 * h + part] = rows.astype(BF16)

        return emit

    def emit_o(g):
        def emit(h, total):
            for part in (0, 1):
                columns = total[:, part * 256 : part * 256 + 256]
                keep_o[g, 2 * h + part] = columns
                zs_o[g, 2 * h + part] = columns.astype(BF16)

        return emit

    runs = []
    for g in (0, 1):
        runs.append(
            (
                scatter_stages(net, wire, own_q(g), bufs[16 * g : 16 * g + 8], emit_q(g)),
                scatter_stages(net, wire, own_o(g), bufs[16 * g + 8 : 16 * g + 16], emit_o(g)),
            )
        )

    def run(g, stage):
        for stages in runs[g]:
            stages[stage]()

    add_cores(0)
    run(0, 0)
    add_cores(1)
    run(1, 0)
    run(0, 1)
    run(1, 1)
    run(0, 2)
    run(1, 2)
    run(0, 3)
    run(1, 3)
    run(0, 4)
    run(1, 4)

    z1 = wire.new(14)
    for k in range(1, 8):
        target = lax.rem(net.z + k, 8)
        g, l = target // 4, lax.rem(target, 4)
        wire.send(zs_q.at[g, l], zr_q.at[k - 1], z1 + 2 * (k - 1), net.up(k))
        wire.send(zs_o.at[g, l], zr_o.at[k - 1], z1 + 2 * (k - 1) + 1, net.up(k))
    total_q, total_o = keep_q[net.zh, net.zl], keep_o[net.zh, net.zl]
    for k in range(1, 8):
        wire.recv(zr_q.at[k - 1], z1 + 2 * (k - 1), net.up(8 - k))
        wire.recv(zr_o.at[k - 1], z1 + 2 * (k - 1) + 1, net.up(8 - k))
        total_q = total_q + zr_q[k - 1].astype(F32)
        total_o = total_o + zr_o[k - 1].astype(F32)
    fin_q[...] = total_q * scale
    fin_o[...] = total_o * scale

    def place(l):
        return (
            out_q.at[pl.ds(pl.multiple_of(l * 16, 16), 16), cols_q[0]],
            out_o.at[:, pl.ds(pl.multiple_of(core * 1024 + l * 256, 128), 256)],
        )

    def level(k):
        l = lax.rem(net.zl + k, 4)
        return l, (net.s, l * 2 + core)

    z2 = wire.new(6)
    mine = place(net.zl)
    for k in (1, 2, 3):
        device = level(k)[1]
        wire.send(fin_q, mine[0], z2 + 2 * (k - 1), device)
        wire.send(fin_o, mine[1], z2 + 2 * (k - 1) + 1, device)
    own_copies = [
        pltpu.make_async_copy(fin_q, mine[0], local_sems.at[0]),
        pltpu.make_async_copy(fin_o, mine[1], local_sems.at[1]),
    ]
    for made in own_copies:
        made.start()
    for k in (1, 2, 3):
        l, device = level(4 - k)
        there = place(l)
        wire.recv(there[0], z2 + 2 * (k - 1), device)
        wire.recv(there[1], z2 + 2 * (k - 1) + 1, device)
    for made in own_copies:
        made.wait()
    last = wire.new(2)
    wire.send(out_q.at[:, cols_q[0]], out_q.at[:, cols_q[0]], last, net.sibling())
    wire.send(out_o.at[:, cols_o[0]], out_o.at[:, cols_o[0]], last + 1, net.sibling())
    wire.recv(out_q.at[:, cols_q[1]], last, net.sibling())
    wire.recv(out_o.at[:, cols_o[1]], last + 1, net.sibling())
    wire.drain()


def scatter_weights(dq, do, scale):
    keys = 4 * AG_KEYS + 4 + 14 + 6 + 2
    return pl.pallas_call(
        functools.partial(weight_scatter_kernel, scale),
        out_shape=(
            jax.ShapeDtypeStruct((64, 1536), F32),
            jax.ShapeDtypeStruct((32, 2048), F32),
        ),
        in_specs=[pl.BlockSpec(memory_space=pltpu.VMEM)] * 2,
        out_specs=[pl.BlockSpec(memory_space=pltpu.VMEM)] * 2,
        scratch_shapes=[
            pltpu.VMEM((2048, 768), BF16),
            pltpu.VMEM((1024, 1024), BF16),
            pltpu.VMEM((2048, 768), BF16),
            pltpu.VMEM((1024, 1024), BF16),
            pltpu.VMEM((2, 4, 16, 768), BF16),
            pltpu.VMEM((2, 4, 32, 256), BF16),
            pltpu.VMEM((7, 16, 768), BF16),
            pltpu.VMEM((7, 32, 256), BF16),
            pltpu.VMEM((2, 4, 16, 768), F32),
            pltpu.VMEM((2, 4, 32, 256), F32),
            pltpu.VMEM((16, 768), F32),
            pltpu.VMEM((32, 256), F32),
            pltpu.SemaphoreType.DMA((keys,)),
            pltpu.SemaphoreType.DMA((keys,)),
            pltpu.SemaphoreType.DMA((2,)),
            *scatter_scratch(32, 768),
            *scatter_scratch(32, 512),
            *scatter_scratch(32, 768),
            *scatter_scratch(32, 512),
        ],
        compiler_params=pltpu.CompilerParams(
            collective_id=3, has_side_effects=True, vmem_limit_bytes=VMEM_BYTES
        ),
        name="scatter_weights",
    )(dq, do)


BLOCK = 512


def spread_heads(rows_t, padded, natural):
    padded[...] = jnp.zeros_like(padded)
    for g in range(4):
        for k in range(4):
            head = 4 * g + k
            padded[g, g * 64 : g * 64 + 64, k * 128 : k * 128 + 128] = rows_t[head * 64 : head * 64 + 64]
        natural[g * 512 : g * 512 + 512] = padded[g].T


def attention_kernel(
    shard_of,
    q_ref,
    do_ref,
    kv_ref,
    att_ref,
    dq_ref,
    terms_ref,
    qt,
    qn,
    dot_,
    don,
    probs,
    peaks,
    peak,
    total,
    acc,
    dqt,
    dots,
    pcat,
    dcat,
):
    s = shard_of()
    blocks = s // 4 + 1
    spread_heads(q_ref[...].T, qt, qn)
    spread_heads(do_ref[...].T, dot_, don)
    peak[...] = jnp.full_like(peak, NEG_FILL)
    total[...] = jnp.zeros_like(total)
    acc[...] = jnp.zeros_like(acc)
    dqt[...] = jnp.zeros_like(dqt)

    def rows_of(j):
        return pl.ds(pl.multiple_of(j * BLOCK, BLOCK), BLOCK)

    def forward(j, masked):
        keys = kv_ref[rows_of(j), 0:256]
        values_t = kv_ref[rows_of(j), 256:512].T
        if masked:
            key_at = lax.broadcasted_iota(jnp.int32, (BLOCK, 512), 0) + j * BLOCK
            query_at = lax.rem(lax.broadcasted_iota(jnp.int32, (BLOCK, 512), 1), 128) + s * 128
            visible = key_at <= query_at
        for g in range(4):
            scores = jnp.dot(keys, qt[g], preferred_element_type=F32)
            if masked:
                scores = jnp.where(visible, scores, NEG_FILL)
            before = peak[g]
            now = jnp.maximum(before, jnp.max(scores, axis=0, keepdims=True))
            fade = jnp.exp(before - now)
            e = jnp.exp(scores - now)
            total[g] = total[g] * fade + jnp.sum(e, axis=0, keepdims=True)
            e = e.astype(BF16)
            probs[g, j] = e
            peaks[g, j] = now
            peak[g] = now
            acc[g] = acc[g] * fade + jnp.dot(values_t[g * 64 : g * 64 + 64], e, preferred_element_type=F32)

    def forward_step(j, carry):
        forward(j, False)
        return carry

    lax.fori_loop(0, blocks - 1, forward_step, 0)
    forward(blocks - 1, True)

    pieces = []
    for g in range(4):
        attended = (acc[g] / total[g]).astype(BF16)
        grads = dot_[g, g * 64 : g * 64 + 64].astype(F32)
        dots[g] = jnp.sum(attended.astype(F32) * grads, axis=0, keepdims=True)
        peak[g] = peak[g] + jnp.log(total[g])
        for k in range(4):
            pieces.append(attended[:, k * 128 : k * 128 + 128])
    att_ref[...] = jnp.concatenate(pieces, axis=0).T

    def backward_step(j, carry):
        keys_t = kv_ref[rows_of(j), 0:256].T
        values = kv_ref[rows_of(j), 256:512]
        for g in range(4):
            p = probs[g, j].astype(F32) * jnp.exp(peaks[g, j] - peak[g])
            grads = jnp.dot(values, dot_[g], preferred_element_type=F32)
            ds = (p * (grads - dots[g])).astype(BF16)
            pcat[:, g * 512 : g * 512 + 512] = p.astype(BF16)
            dcat[:, g * 512 : g * 512 + 512] = ds
            dqt[g] += jnp.dot(keys_t[g * 64 : g * 64 + 64], ds, preferred_element_type=F32)
        terms_ref[rows_of(j), 0:256] = jnp.dot(dcat[...], qn[...], preferred_element_type=F32).astype(BF16)
        terms_ref[rows_of(j), 256:512] = jnp.dot(pcat[...], don[...], preferred_element_type=F32).astype(BF16)
        return carry

    lax.fori_loop(0, blocks, backward_step, 0)

    def blank_step(j, carry):
        terms_ref[rows_of(j)] = jnp.zeros((BLOCK, 512), BF16)
        return carry

    lax.fori_loop(blocks, 8, blank_step, 0)
    pieces = []
    for g in range(4):
        for k in range(4):
            pieces.append(dqt[g, :, k * 128 : k * 128 + 128])
    dq_ref[...] = jnp.concatenate(pieces, axis=0).T


ATTENTION_SCRATCH = [
    pltpu.VMEM((4, 256, 512), BF16),
    pltpu.VMEM((2048, 256), BF16),
    pltpu.VMEM((4, 256, 512), BF16),
    pltpu.VMEM((2048, 256), BF16),
    pltpu.VMEM((4, 8, BLOCK, 512), BF16),
    pltpu.VMEM((4, 8, 1, 512), F32),
    pltpu.VMEM((4, 1, 512), F32),
    pltpu.VMEM((4, 1, 512), F32),
    pltpu.VMEM((4, 64, 512), F32),
    pltpu.VMEM((4, 64, 512), F32),
    pltpu.VMEM((4, 1, 512), F32),
    pltpu.VMEM((BLOCK, 2048), BF16),
    pltpu.VMEM((BLOCK, 2048), BF16),
]


def attention(queries, grads, kv, shard_of=lambda: lax.axis_index("shard")):
    return pl.pallas_call(
        functools.partial(attention_kernel, shard_of),
        out_shape=(
            jax.ShapeDtypeStruct((128, 1024), BF16),
            jax.ShapeDtypeStruct((128, 1024), F32),
            jax.ShapeDtypeStruct((4096, 512), BF16),
        ),
        in_specs=[pl.BlockSpec(memory_space=pltpu.VMEM)] * 3,
        out_specs=[pl.BlockSpec(memory_space=pltpu.VMEM)] * 3,
        scratch_shapes=ATTENTION_SCRATCH,
        compiler_params=pltpu.CompilerParams(vmem_limit_bytes=VMEM_BYTES),
        name="attention",
    )(queries, grads, kv)


def tables(positions, head_size):
    halves = head_size // 2
    frequency = ROPE_BASE ** (-(jnp.arange(halves, dtype=jnp.float32) * 2.0) / head_size)
    angles = positions.astype(jnp.float32)[:, None] * frequency[None, :]
    return (jnp.cos(angles), jnp.sin(angles))


def rotate(matrix, cos_rows, sin_rows, head_count):
    row_count = matrix.shape[0]
    head_size = matrix.shape[1] // head_count
    halves = head_size // 2
    pieces = matrix.reshape(row_count, head_count, 2, halves)
    lower_half = pieces[:, :, 0]
    upper_half = pieces[:, :, 1]
    cos_part = cos_rows[:, None, :]
    sin_part = sin_rows[:, None, :]
    turned = jnp.stack(
        [
            lower_half * cos_part - upper_half * sin_part,
            upper_half * cos_part + lower_half * sin_part,
        ],
        axis=2,
    )
    return turned.reshape(row_count, head_count * head_size)


def body(tokens, qkv_weight, out_weight, cotangent):
    inner_width = HEADS * HEAD_DIM
    kv_width = KV_HEADS * HEAD_DIM
    logit_scale = HEAD_DIM ** (-0.5)
    inputs = tokens[0]
    grad_output = cotangent[0]
    tok_count = inputs.shape[0]
    qkv_full, out_full = gather_weights(qkv_weight, out_weight)
    positions = lax.axis_index("shard") * tok_count + jnp.arange(tok_count, dtype=jnp.int32)
    cosine, sine = tables(positions, HEAD_DIM)
    projected = jnp.dot(inputs, qkv_full, preferred_element_type=F32)
    queries = rotate(projected[:, :inner_width], cosine, sine, HEADS).astype(BF16)
    key_rows = rotate(projected[:, inner_width : inner_width + kv_width], cosine, sine, KV_HEADS).astype(BF16)
    value_rows = projected[:, inner_width + kv_width :].astype(BF16)
    kv = gather_kv(jnp.concatenate([key_rows, value_rows], axis=1))
    grad_attended = lax.dot_general(
        grad_output, out_full, (((1,), (1,)), ((), ())), preferred_element_type=F32
    ).astype(BF16)
    attended, query_sum, kv_terms = attention(queries * BF16(logit_scale), grad_attended, kv)
    block_output = jnp.dot(attended, out_full, preferred_element_type=F32).astype(BF16)
    out_term = lax.dot_general(
        attended, grad_output, (((0,), (0,)), ((), ())), preferred_element_type=F32
    ).astype(BF16)
    kv_grad = scatter_kv(kv_terms)
    query_gradient = rotate(query_sum * logit_scale, cosine, -sine, HEADS).astype(BF16)
    grad_keys = rotate(kv_grad[:, :kv_width], cosine, -sine, KV_HEADS).astype(BF16)
    grad_values = kv_grad[:, kv_width:].astype(BF16)
    grad_proj = jnp.concatenate([query_gradient, grad_keys, grad_values], axis=1)
    tokens_grad = lax.dot_general(
        grad_proj, qkv_full, (((1,), (1,)), ((), ())), preferred_element_type=F32
    ).astype(BF16)
    qkv_term = lax.dot_general(
        inputs, grad_proj, (((0,), (0,)), ((), ())), preferred_element_type=F32
    ).astype(BF16)
    norm_factor = 1.0 / math.sqrt(lax.axis_size("rep") * lax.axis_size("shard") * tok_count)
    qkv_grad, out_grad = scatter_weights(qkv_term, out_term, norm_factor)
    return (block_output[None], tokens_grad[None], qkv_grad, out_grad)


def solution(mesh):
    return jax.shard_map(
        body,
        mesh=mesh,
        in_specs=(
            P("rep", "shard", None),
            P("shard", None),
            P("shard", None),
            P("rep", "shard", None),
        ),
        out_specs=(
            P("rep", "shard", None),
            P("rep", "shard", None),
            P("shard", None),
            P("shard", None),
        ),
        check_vma=False,
    )
```

```python
import functools
import math

import jax
import jax.numpy as jnp
from jax import lax
from jax.experimental import pallas as pl
from jax.experimental.pallas import tpu as pltpu
from jax.sharding import PartitionSpec as P

HEADS = 16
KV_HEADS = 4
HEAD_DIM = 64

ROPE_BASE = 500000.0
NEG_FILL = -1e30
MESH = pl.DeviceIdType.MESH
BF16 = jnp.bfloat16
F32 = jnp.float32
VMEM_BYTES = 60 * 1024 * 1024


class Net:
    def __init__(self):
        self.s = lax.axis_index("shard")
        self.r = lax.axis_index("rep")
        self.zh = self.s // 16
        self.x = lax.rem(self.s // 4, 4)
        self.y = lax.rem(self.s, 4)
        self.zl = self.r // 2
        self.core = lax.rem(self.r, 2)
        self.z = self.zh * 4 + self.zl

    def at(self, h, da, db):
        dx, dy = (da, db) if h == 0 else (db, da)
        return lax.rem(self.x + (dx + 4), 4), lax.rem(self.y + (dy + 4), 4)

    def dev(self, h, da, db):
        gx, gy = self.at(h, da, db)
        return (self.zh * 16 + gx * 4 + gy, self.r)

    def sibling(self):
        return (self.s, self.zl * 2 + 1 - self.core)

    def partner(self):
        return (lax.rem(self.s + 16, 32), self.r)

    def up(self, k):
        z = lax.rem(self.z + k, 8)
        return ((z // 4) * 16 + self.x * 4 + self.y, lax.rem(z, 4) * 2 + self.core)

    def xy_neighbours(self):
        return [self.dev(0, 1, 0), self.dev(0, -1, 0), self.dev(0, 0, 1), self.dev(0, 0, -1)]


def greet(devices):
    barrier = pltpu.get_barrier_semaphore()
    for device in devices:
        pl.semaphore_signal(barrier, inc=1, device_id=device, device_id_type=MESH)
    pl.semaphore_wait(barrier, len(devices))


class Wire:
    def __init__(self, send_sems, recv_sems, canvas, device):
        self.send_sems, self.recv_sems = send_sems, recv_sems
        self.canvas, self.device = canvas, device
        self.used = 0
        self.sent = []

    def new(self, count=1):
        first = self.used
        self.used += count
        return first

    def copy(self, src, dst, key, device):
        return pltpu.make_async_remote_copy(
            src_ref=src,
            dst_ref=dst,
            send_sem=self.send_sems.at[key],
            recv_sem=self.recv_sems.at[key],
            device_id=device,
            device_id_type=MESH,
        )

    def send(self, src, dst, key, device):
        self.copy(src, dst, key, device).start()
        self.sent.append((src.shape, src.dtype, key))

    def recv(self, ref, key, device):
        self.copy(ref, ref, key, device).wait_recv()

    def drain(self):
        for (rows, cols), dtype, key in self.sent:
            ref = self.canvas[dtype == F32].at[pl.ds(0, rows), pl.ds(0, cols)]
            self.copy(ref, ref, key, self.device).wait_send()
        self.sent = []


SIDES = (1, -1)
RING = (0, 1, -1, 2)
AG_KEYS = 40


def side(d):
    return 0 if d == 1 else 1


def gather_stages(net, wire, own, piece):
    base = wire.new(AG_KEYS)

    def s1(h, d):
        return base + h * 2 + side(d)

    def s2(h, d):
        return base + 4 + h * 2 + side(d)

    def t1(h, da, d):
        return base + 8 + (h * 4 + RING.index(da)) * 2 + side(d)

    def t2(h, da, d):
        return base + 24 + (h * 4 + RING.index(da)) * 2 + side(d)

    def at(h, da, db, part=None):
        return piece(*net.at(h, da, db), h, part)

    def spread(h, da, src):
        for d in SIDES:
            wire.send(src, at(h, da, 0), t1(h, da, d), net.dev(h, 0, d))

    def pass_on(h, da):
        for d in SIDES:
            wire.recv(at(h, da, -d), t1(h, da, d), net.dev(h, 0, -d))
            part = side(d)
            wire.send(at(h, da, -d, part), at(h, da, -d, part), t2(h, da, d), net.dev(h, 0, d))

    def stage_a():
        for h in (0, 1):
            for d in SIDES:
                wire.send(own(h), at(h, 0, 0), s1(h, d), net.dev(h, d, 0))
        for h in (0, 1):
            spread(h, 0, own(h))

    def stage_b():
        for d in SIDES:
            for h in (0, 1):
                wire.recv(at(h, -d, 0), s1(h, d), net.dev(h, -d, 0))
                part = side(d)
                wire.send(at(h, -d, 0, part), at(h, -d, 0, part), s2(h, d), net.dev(h, d, 0))
        for d in SIDES:
            for h in (0, 1):
                spread(h, -d, at(h, -d, 0))

    def stage_c():
        for h in (0, 1):
            pass_on(h, 0)

    def stage_d():
        for h in (0, 1):
            for d in SIDES:
                wire.recv(at(h, 2, 0, side(d)), s2(h, d), net.dev(h, -d, 0))
            spread(h, 2, at(h, 2, 0))

    def stage_e():
        for da in (-1, 1):
            for h in (0, 1):
                pass_on(h, da)

    def stage_f():
        for h in (0, 1):
            pass_on(h, 2)

    def stage_g():
        for da in (0, -1, 1, 2):
            for h in (0, 1):
                for d in SIDES:
                    wire.recv(at(h, da, 2, side(d)), t2(h, da, d), net.dev(h, 0, -d))

    return [stage_a, stage_b, stage_c, stage_d, stage_e, stage_f, stage_g]


def scatter_scratch(rows, cols):
    return [
        pltpu.VMEM((2, 4, 2, rows // 2, cols), BF16),
        pltpu.VMEM((2, 4, 2, rows, cols), BF16),
        pltpu.VMEM((2, 4, 2, rows, cols), BF16),
        pltpu.VMEM((2, 3, rows, cols), F32),
        pltpu.VMEM((2, rows, cols), BF16),
        pltpu.VMEM((2, 2, rows // 2, cols), BF16),
        pltpu.VMEM((2, 2, rows, cols), BF16),
        pltpu.VMEM((2, 2, rows, cols), BF16),
    ]


class Scatter:
    ORDER = (2, 1, -1, 0)

    def __init__(self, net, wire, own, bufs, emit):
        self.net, self.wire, self.own, self.emit = net, wire, own, emit
        self.t2b, self.t1s, self.t1b, self.row_sum, self.s2s, self.s2b, self.s1s, self.s1b = bufs
        self.rows = self.row_sum.shape[2]
        self.half = self.rows // 2
        self.base = wire.new(AG_KEYS)

    def s1(self, h, d):
        return self.base + h * 2 + side(d)

    def s2(self, h, d):
        return self.base + 4 + h * 2 + side(d)

    def t1(self, h, i, d):
        return self.base + 8 + (h * 4 + i) * 2 + side(d)

    def t2(self, h, i, d):
        return self.base + 24 + (h * 4 + i) * 2 + side(d)

    def part(self, p):
        return pl.ds(p * self.half, self.half)

    def load(self, h, da, db, part=None):
        return self.own(*self.net.at(h, da, db), h, part)[...].astype(F32)

    def a(self, h, da):
        i, net = RING.index(da), self.net
        for d in SIDES:
            p = side(d)
            src = self.own(*net.at(h, da, 2), h, p)
            self.wire.send(src, self.t2b.at[h, i, p], self.t2(h, i, d), net.dev(h, 0, d))

    def b(self, h, da, d):
        i, p, net = RING.index(da), side(d), self.net
        self.wire.recv(self.t2b.at[h, i, p], self.t2(h, i, d), net.dev(h, 0, -d))
        added = self.load(h, da, d, p) + self.t2b[h, i, p].astype(F32)
        self.t1s[h, i, p, self.part(p)] = added.astype(BF16)
        self.t1s[h, i, p, self.part(1 - p)] = self.load(h, da, d, 1 - p).astype(BF16)
        self.wire.send(self.t1s.at[h, i, p], self.t1b.at[h, i, p], self.t1(h, i, d), net.dev(h, 0, d))

    def c(self, h, da):
        i, net = RING.index(da), self.net
        for d in SIDES:
            self.wire.recv(self.t1b.at[h, i, side(d)], self.t1(h, i, d), net.dev(h, 0, -d))
        total = self.load(h, da, 0) + self.t1b[h, i, 0].astype(F32) + self.t1b[h, i, 1].astype(F32)
        if da != 2:
            self.row_sum[h, i] = total
            return
        self.s2s[h] = total.astype(BF16)
        for d in SIDES:
            p = side(d)
            self.wire.send(self.s2s.at[h, self.part(p)], self.s2b.at[h, p], self.s2(h, d), net.dev(h, d, 0))

    def d(self, h, d):
        i, p, net = RING.index(d), side(d), self.net
        self.wire.recv(self.s2b.at[h, p], self.s2(h, d), net.dev(h, -d, 0))
        added = self.row_sum[h, i, self.part(p)] + self.s2b[h, p].astype(F32)
        self.s1s[h, p, self.part(p)] = added.astype(BF16)
        self.s1s[h, p, self.part(1 - p)] = self.row_sum[h, i, self.part(1 - p)].astype(BF16)
        self.wire.send(self.s1s.at[h, p], self.s1b.at[h, p], self.s1(h, d), net.dev(h, d, 0))

    def e(self, h):
        for d in SIDES:
            self.wire.recv(self.s1b.at[h, side(d)], self.s1(h, d), self.net.dev(h, -d, 0))
        self.emit(h, self.row_sum[h, 0] + self.s1b[h, 0].astype(F32) + self.s1b[h, 1].astype(F32))

    def all_a(self):
        for da in self.ORDER:
            for h in (0, 1):
                self.a(h, da)

    def all_b(self):
        for da in self.ORDER:
            for h in (0, 1):
                for d in SIDES:
                    self.b(h, da, d)

    def all_c(self):
        for da in self.ORDER:
            for h in (0, 1):
                self.c(h, da)

    def all_d(self):
        for h in (0, 1):
            for d in SIDES:
                self.d(h, d)

    def all_e(self):
        for h in (0, 1):
            self.e(h)


def qkv_gather_kernel(qkv_in, qkv_full, send_sems, recv_sems, local_sems):
    net = Net()
    wire = Wire(send_sems, recv_sems, (qkv_full, None), net.sibling())
    core, s = net.core, net.s
    other = 1 - net.zh
    cols = pl.ds(pl.multiple_of(core * 768, 128), 768)

    def place(group):
        def piece(gx, gy, h, part):
            row = (group * 16 + gx * 4 + gy) * 64 + h * 32
            if part is None:
                return qkv_full.at[pl.ds(pl.multiple_of(row, 16), 32), cols]
            return qkv_full.at[pl.ds(pl.multiple_of(row + part * 16, 16), 16), cols]

        return piece

    greet(net.xy_neighbours() + [net.sibling(), net.partner()])
    mine = qkv_full.at[pl.ds(pl.multiple_of(s * 64, 64), 64), cols]
    zkey = wire.new(1)
    wire.send(qkv_in.at[:, cols], mine, zkey, net.partner())
    near = gather_stages(net, wire, lambda h: qkv_in.at[pl.ds(h * 32, 32), cols], place(net.zh))
    near[0]()
    keep = pltpu.make_async_copy(qkv_in.at[:, cols], mine, local_sems.at[0])
    keep.start()
    for stage in near[1:6]:
        stage()
    far_row = pl.multiple_of(lax.rem(s + 16, 32) * 64, 64)
    wire.recv(qkv_full.at[pl.ds(far_row, 64), cols], zkey, net.partner())
    far_place = place(other)
    far = gather_stages(net, wire, lambda h: far_place(net.x, net.y, h, None), far_place)
    far[0]()
    near[6]()
    keep.wait()

    def half_of(group, which):
        columns = pl.ds(pl.multiple_of(which * 768, 128), 768)
        return qkv_full.at[pl.ds(pl.multiple_of(group * 1024, 64), 1024), columns]

    share = wire.new(2)
    wire.send(half_of(net.zh, core), half_of(net.zh, core), share, net.sibling())
    for stage in far[1:]:
        stage()
    wire.send(half_of(other, core), half_of(other, core), share + 1, net.sibling())
    wire.recv(half_of(net.zh, 1 - core), share, net.sibling())
    wire.recv(half_of(other, 1 - core), share + 1, net.sibling())
    wire.drain()


def gather_qkv(qkv_weight):
    keys = 2 * AG_KEYS + 3
    return pl.pallas_call(
        qkv_gather_kernel,
        out_shape=jax.ShapeDtypeStruct((2048, 1536), BF16),
        in_specs=[pl.BlockSpec(memory_space=pl.ANY)],
        out_specs=pl.BlockSpec(memory_space=pl.ANY),
        scratch_shapes=[
            pltpu.SemaphoreType.DMA((keys,)),
            pltpu.SemaphoreType.DMA((keys,)),
            pltpu.SemaphoreType.DMA((1,)),
        ],
        compiler_params=pltpu.CompilerParams(collective_id=0, has_side_effects=True),
        name="gather_qkv",
    )(qkv_weight)


BLOCK = 512


def spread_heads(rows_t, padded, natural):
    padded[...] = jnp.zeros_like(padded)
    for g in range(4):
        for k in range(4):
            head = 4 * g + k
            padded[g, g * 64 : g * 64 + 64, k * 128 : k * 128 + 128] = rows_t[head * 64 : head * 64 + 64]
        natural[g * 512 : g * 512 + 512] = padded[g].T


def attend_kernel(
    q_ref,
    kv_in,
    cot_ref,
    out_in,
    att_ref,
    dq_ref,
    kvg_ref,
    block_ref,
    parts_o,
    kv_ref,
    out_full,
    terms,
    qt,
    qn,
    dot_,
    don,
    probs,
    peaks,
    peak,
    total,
    acc,
    dqt,
    dots,
    att_t,
    do_sib,
    sib_o,
    sum_o,
    far_out,
    far_in,
    send_sems,
    recv_sems,
    *bufs,
):
    net = Net()
    wire = Wire(send_sems, recv_sems, (out_full, None), net.sibling())
    s, x, zh, core = net.s, net.x, net.zh, net.core
    other = 1 - zh

    def kv_place(ref, group):
        def piece(gx, gy, h, part):
            row = (group * 16 + gx * 4 + gy) * 128 + h * 64
            if part is None:
                return ref.at[pl.ds(pl.multiple_of(row, 32), 64)]
            return ref.at[pl.ds(pl.multiple_of(row + part * 32, 32), 32)]

        return piece

    def out_cols(h):
        return pl.ds(pl.multiple_of(core * 1024 + h * 512, 128), 512)

    def out_place(group):
        def piece(gx, gy, h, part):
            row = (group * 16 + gx * 4 + gy) * 32
            if part is None:
                return out_full.at[pl.ds(pl.multiple_of(row, 16), 32), out_cols(h)]
            return out_full.at[pl.ds(pl.multiple_of(row + part * 16, 16), 16), out_cols(h)]

        return piece

    def out_half(group, which):
        columns = pl.ds(pl.multiple_of(which * 1024, 128), 1024)
        return out_full.at[pl.ds(pl.multiple_of(group * 512, 32), 512), columns]

    def kv_rows(shard):
        return kv_ref.at[pl.ds(pl.multiple_of(shard * 128, 128), 128)]

    far_shard = lax.rem(s + 16, 32)
    half_cols = pl.ds(pl.multiple_of(core * 1024, 128), 1024)

    def out_rows(shard):
        return out_full.at[pl.ds(pl.multiple_of(shard * 32, 32), 32), half_cols]

    greet(net.xy_neighbours() + [net.sibling(), net.partner()])

    zkey = wire.new(2)
    wire.send(kv_in, kv_rows(s), zkey, net.partner())
    near = gather_stages(net, wire, lambda h: kv_in.at[pl.ds(h * 64, 64)], kv_place(kv_ref, zh))
    near[0]()
    kv_ref[pl.ds(pl.multiple_of(s * 128, 128), 128)] = kv_in[...]
    out_full[pl.ds(pl.multiple_of(s * 32, 32), 32), half_cols] = out_in[:, half_cols]
    peak[...] = jnp.full_like(peak, NEG_FILL)
    total[...] = jnp.zeros_like(total)
    acc[...] = jnp.zeros_like(acc)
    dqt[...] = jnp.zeros_like(dqt)
    near[1]()
    near[2]()
    spread_heads(q_ref[...].T, qt, qn)
    for stage in near[3:6]:
        stage()
    wire.recv(kv_rows(far_shard), zkey, net.partner())
    wire.send(out_in.at[:, half_cols], out_rows(s), zkey + 1, net.partner())
    far_place = kv_place(kv_ref, other)
    far = gather_stages(net, wire, lambda h: far_place(net.x, net.y, h, None), far_place)
    far[0]()
    near[6]()

    near_o = gather_stages(net, wire, lambda h: out_in.at[:, out_cols(h)], out_place(zh))
    far_op = out_place(other)
    far_o = gather_stages(net, wire, lambda h: far_op(net.x, net.y, h, None), far_op)
    share = wire.new(2)

    def rows_of(j):
        return pl.ds(pl.multiple_of(j * BLOCK, BLOCK), BLOCK)

    def forward(j, masked):
        keys = kv_ref[rows_of(j), 0:256]
        values_t = kv_ref[rows_of(j), 256:512].T
        if masked:
            key_at = lax.broadcasted_iota(jnp.int32, (BLOCK, 512), 0) + j * BLOCK
            query_at = lax.rem(lax.broadcasted_iota(jnp.int32, (BLOCK, 512), 1), 128) + s * 128
            visible = key_at <= query_at
        ahead = jnp.dot(keys, qt[0], preferred_element_type=F32)
        for g in range(4):
            scores = ahead
            if g < 3:
                ahead = jnp.dot(keys, qt[g + 1], preferred_element_type=F32)
            if masked:
                scores = jnp.where(visible, scores, NEG_FILL)
            before = peak[g]
            now = jnp.maximum(before, jnp.max(scores, axis=0, keepdims=True))
            fade = jnp.exp(before - now)
            e = jnp.exp(scores - now)
            total[g] = total[g] * fade + jnp.sum(e, axis=0, keepdims=True)
            e = e.astype(BF16)
            probs[g, j] = e
            peaks[g, j] = now
            peak[g] = now
            acc[g] = acc[g] * fade + jnp.dot(values_t[g * 64 : g * 64 + 64], e, preferred_element_type=F32)

    def in_turn(plans, i):
        for k, plan in enumerate(plans):

            @pl.when(i == k)
            def _():
                for stage in plan:
                    stage()

    def near_forward(i, carry):
        in_turn([[far[1]], [far[2]], [far[3], near_o[0]], [far[4]]], i)

        @pl.when(i < x)
        def _():
            forward(zh * 4 + i, False)

        @pl.when(i == x)
        def _():
            forward(zh * 4 + i, True)

        return carry

    lax.fori_loop(0, 4, near_forward, 0)
    far[5]()
    near_o[1]()
    far[6]()

    def recv_out():
        wire.recv(out_rows(far_shard), zkey + 1, net.partner())

    def share_near():
        wire.send(out_half(zh, core), out_half(zh, core), share, net.sibling())

    def far_forward(i, carry):
        in_turn(
            [
                [near_o[2], near_o[3]],
                [near_o[4], near_o[5], recv_out, far_o[0]],
                [near_o[6], share_near, far_o[1], far_o[2]],
                [far_o[3], far_o[4]],
            ],
            i,
        )

        @pl.when(zh == 1)
        def _():
            forward(i, False)

        return carry

    lax.fori_loop(0, 4, far_forward, 0)
    far_o[5]()
    far_o[6]()
    wire.send(out_half(other, core), out_half(other, core), share + 1, net.sibling())

    for g in range(4):
        attended = (acc[g] / total[g]).astype(BF16)
        for k in range(4):
            head = 4 * g + k
            att_t[head * 64 : head * 64 + 64] = attended[:, k * 128 : k * 128 + 128]
    core_key = wire.new(2)
    for g in (0, 1):
        rows = slice(g * 512, g * 512 + 512)
        sib_cols = pl.ds(pl.multiple_of((1 - core) * 1024, 128), 1024)
        do_sib[rows] = jnp.dot(att_t[rows], cot_ref[:, sib_cols], preferred_element_type=F32).astype(BF16)
        wire.send(do_sib.at[pl.ds(g * 512, 512)], sib_o.at[pl.ds(g * 512, 512)], core_key + g, net.sibling())
    att_ref[...] = att_t[...].T
    wire.recv(out_half(zh, 1 - core), share, net.sibling())
    wire.recv(out_half(other, 1 - core), share + 1, net.sibling())
    grad_t = lax.dot_general(
        out_full[...], cot_ref[...], (((1,), (1,)), ((), ())), preferred_element_type=F32
    ).astype(BF16)
    spread_heads(grad_t, dot_, don)
    for g in range(4):
        for k in range(4):
            head = 4 * g + k
            rows = slice(head * 64, head * 64 + 64)
            both = att_t[rows].astype(F32) * dot_[g, g * 64 : g * 64 + 64, k * 128 : k * 128 + 128].astype(F32)
            dots[g, :, k * 128 : k * 128 + 128] = jnp.sum(both, axis=0, keepdims=True)
        peak[g] = peak[g] + jnp.log(total[g])

    def out_own(group):
        def piece(gx, gy, h, part):
            row = (group * 16 + gx * 4 + gy) * 32
            if part is None:
                return sum_o.at[pl.ds(pl.multiple_of(row, 16), 32), pl.ds(h * 512, 512)]
            return sum_o.at[pl.ds(pl.multiple_of(row + part * 16, 16), 16), pl.ds(h * 512, 512)]

        return piece

    def out_emit(group):
        def emit(h, result):
            for part in (0, 1):
                parts_o[group, 2 * h + part] = result[:, part * 256 : part * 256 + 256]

        return emit

    scat_o = [Scatter(net, wire, out_own(g), bufs[16 + 8 * g : 24 + 8 * g], out_emit(g)) for g in (0, 1)]

    def add_cores(g):
        def run():
            rows = slice(g * 512, g * 512 + 512)
            wire.recv(sib_o.at[pl.ds(g * 512, 512)], core_key + g, net.sibling())
            own = jnp.dot(att_t[rows], cot_ref[:, half_cols], preferred_element_type=F32)
            sum_o[rows] = (own + sib_o[rows].astype(F32)).astype(BF16)
            scat_o[g].all_a()

        return run

    def backward(j):
        keys_t = kv_ref[rows_of(j), 0:256].T
        values = kv_ref[rows_of(j), 256:512]
        ahead = jnp.dot(values, dot_[0], preferred_element_type=F32)
        dk = dv = None
        for g in range(4):
            grads = ahead
            if g < 3:
                ahead = jnp.dot(values, dot_[g + 1], preferred_element_type=F32)
            p = probs[g, j].astype(F32) * jnp.exp(peaks[g, j] - peak[g])
            ds = (p * (grads - dots[g])).astype(BF16)
            p = p.astype(BF16)
            dqt[g] += jnp.dot(keys_t[g * 64 : g * 64 + 64], ds, preferred_element_type=F32)
            rows = slice(g * 512, g * 512 + 512)
            dk_g = jnp.dot(ds, qn[rows], preferred_element_type=F32)
            dv_g = jnp.dot(p, don[rows], preferred_element_type=F32)
            dk = dk_g if g == 0 else dk + dk_g
            dv = dv_g if g == 0 else dv + dv_g
        terms[rows_of(j), 0:256] = dk.astype(BF16)
        terms[rows_of(j), 256:512] = dv.astype(BF16)

    zback = wire.new(2)

    def emit_far(h, result):
        far_out[h] = result.astype(BF16)
        wire.send(far_out.at[h], far_in.at[h], zback + h, net.partner())

    def emit_near(h, result):
        kvg_ref[pl.ds(h * 64, 64)] = result

    scat_far = Scatter(net, wire, kv_place(terms, other), bufs[0:8], emit_far)
    scat_near = Scatter(net, wire, kv_place(terms, zh), bufs[8:16], emit_near)

    def after(scat):
        one = functools.partial

        def plan0():
            scat.a(0, 2)
            for da in scat.ORDER:
                scat.a(1, da)

        def plan1():
            scat.a(0, 1)
            for da in scat.ORDER:
                scat.b(1, da, 1)
            for d in SIDES:
                scat.b(0, 2, d)

        def plan2():
            scat.a(0, -1)
            for da in scat.ORDER:
                scat.b(1, da, -1)
            for d in SIDES:
                scat.b(0, 1, d)
            scat.c(0, 2)

        def plan3():
            scat.a(0, 0)
            for d in SIDES:
                scat.b(0, -1, d)
            scat.c(1, 2)
            scat.c(0, 1)

        return [[plan0], [plan1], [plan2], [plan3]]

    def late1(scat):
        def run():
            for d in SIDES:
                scat.b(0, 0, d)
            for da in (1, -1, 0):
                scat.c(1, da)
            scat.c(0, -1)

        return run

    def late2(scat):
        def run():
            scat.c(0, 0)
            scat.all_d()

        return run

    def block_loop(group, plans):
        def step(i, carry):
            turn = lax.rem(18 - i + 3 * ((i * (i - 1)) // 2), 4)
            j = group * 4 + lax.rem(x + turn, 4)

            @pl.when(j <= s // 4)
            def _():
                backward(j)

            @pl.when(j > s // 4)
            def _():
                terms[rows_of(j)] = jnp.zeros((BLOCK, 512), BF16)

            in_turn(plans, i)
            return carry

        lax.fori_loop(0, 4, step, 0)

    plans = after(scat_far)
    plans[1].append(add_cores(0))
    plans[2].append(add_cores(1))
    plans[3].append(scat_o[0].all_b)
    block_loop(other, plans)
    plans = after(scat_near)
    plans[0] = [late1(scat_far)] + plans[0] + [scat_o[1].all_b]
    plans[1] = [late2(scat_far)] + plans[1] + [scat_o[0].all_c]
    plans[2] = [scat_far.all_e] + plans[2] + [scat_o[1].all_c, scat_o[0].all_d]
    plans[3] = plans[3] + [scat_o[1].all_d, scat_o[0].all_e]
    block_loop(zh, plans)
    late1(scat_near)()
    for c in range(4):
        cols = slice(c * 512, c * 512 + 512)
        block_ref[:, cols] = jnp.dot(att_ref[...], out_full[:, cols], preferred_element_type=F32).astype(BF16)
    late2(scat_near)()
    for g in range(4):
        for k in range(0, 4, 2):
            head = 4 * g + k
            pair = jnp.concatenate([dqt[g, :, k * 128 : k * 128 + 128], dqt[g, :, k * 128 + 128 : k * 128 + 256]], axis=0)
            dq_ref[:, head * 64 : head * 64 + 128] = pair.T
    scat_o[1].all_e()
    scat_near.all_e()
    for h in (0, 1):
        wire.recv(far_in.at[h], zback + h, net.partner())
        kvg_ref[pl.ds(h * 64, 64)] += far_in[h].astype(F32)
    wire.drain()


def attend(queries, kv, cotangent, out_weight):
    keys = 8 * AG_KEYS + 8
    return pl.pallas_call(
        attend_kernel,
        out_shape=(
            jax.ShapeDtypeStruct((128, 1024), BF16),
            jax.ShapeDtypeStruct((128, 1024), F32),
            jax.ShapeDtypeStruct((128, 512), F32),
            jax.ShapeDtypeStruct((128, 2048), BF16),
            jax.ShapeDtypeStruct((2, 4, 32, 256), F32),
        ),
        in_specs=[pl.BlockSpec(memory_space=pltpu.VMEM)] * 4,
        out_specs=[pl.BlockSpec(memory_space=pltpu.VMEM)] * 5,
        scratch_shapes=[
            pltpu.VMEM((4096, 512), BF16),
            pltpu.VMEM((1024, 2048), BF16),
            pltpu.VMEM((4096, 512), BF16),
            pltpu.VMEM((4, 256, 512), BF16),
            pltpu.VMEM((2048, 256), BF16),
            pltpu.VMEM((4, 256, 512), BF16),
            pltpu.VMEM((2048, 256), BF16),
            pltpu.VMEM((4, 8, BLOCK, 512), BF16),
            pltpu.VMEM((4, 8, 1, 512), F32),
            pltpu.VMEM((4, 1, 512), F32),
            pltpu.VMEM((4, 1, 512), F32),
            pltpu.VMEM((4, 64, 512), F32),
            pltpu.VMEM((4, 64, 512), F32),
            pltpu.VMEM((4, 1, 512), F32),
            pltpu.VMEM((1024, 128), BF16),
            pltpu.VMEM((1024, 1024), BF16),
            pltpu.VMEM((1024, 1024), BF16),
            pltpu.VMEM((1024, 1024), BF16),
            pltpu.VMEM((2, 64, 512), BF16),
            pltpu.VMEM((2, 64, 512), BF16),
            pltpu.SemaphoreType.DMA((keys,)),
            pltpu.SemaphoreType.DMA((keys,)),
            *scatter_scratch(64, 512),
            *scatter_scratch(64, 512),
            *scatter_scratch(32, 512),
            *scatter_scratch(32, 512),
        ],
        compiler_params=pltpu.CompilerParams(
            collective_id=1, has_side_effects=True, vmem_limit_bytes=VMEM_BYTES
        ),
        name="attend",
    )(queries, kv, cotangent, out_weight)


def weight_grad_kernel(
    scale,
    x_ref,
    gp_ref,
    w_ref,
    parts_o,
    tg_ref,
    out_q,
    out_o,
    xt,
    do_sib,
    sib_q,
    sum_q,
    zs_q,
    zs_o,
    zr_q,
    zr_o,
    keep_q,
    fin_q,
    fin_o,
    send_sems,
    recv_sems,
    *bufs,
):
    net = Net()
    wire = Wire(send_sems, recv_sems, (sum_q, out_q), net.sibling())
    core = net.core
    cols_q = [pl.ds(pl.multiple_of(c * 768, 128), 768) for c in (core, 1 - core)]
    cols_o = [pl.ds(pl.multiple_of(c * 1024, 128), 1024) for c in (core, 1 - core)]
    greet(net.xy_neighbours() + [net.sibling()] + [net.up(k) for k in range(1, 8)])

    z1 = wire.new(14)

    def z_send(k, staged, slots, key):
        target = lax.rem(net.z + k, 8)
        wire.send(staged.at[target // 4, lax.rem(target, 4)], slots.at[k - 1], key + k - 1, net.up(k))

    for g in (0, 1):
        for l in range(4):
            zs_o[g, l] = parts_o[g, l].astype(BF16)
    for k in range(1, 8):
        z_send(k, zs_o, zr_o, z1)

    xt[...] = x_ref[...].T
    ckey = wire.new(2)

    def product(rows, cols):
        return jnp.dot(xt[rows], gp_ref[:, cols], preferred_element_type=F32)

    def make_sibling(g):
        def step(i, carry):
            rows = pl.ds(pl.multiple_of(g * 1024 + i * 256, 256), 256)
            do_sib[rows] = product(rows, cols_q[1]).astype(BF16)
            return carry

        lax.fori_loop(0, 4, step, 0)
        rows = pl.ds(g * 1024, 1024)
        wire.send(do_sib.at[rows], sib_q.at[rows], ckey + g, net.sibling())

    def add_cores(g):
        wire.recv(sib_q.at[pl.ds(g * 1024, 1024)], ckey + g, net.sibling())

        def step(i, carry):
            rows = pl.ds(pl.multiple_of(g * 1024 + i * 256, 256), 256)
            sum_q[rows] = (product(rows, cols_q[0]) + sib_q[rows].astype(F32)).astype(BF16)
            return carry

        lax.fori_loop(0, 4, step, 0)

    def own_q(g):
        def piece(gx, gy, h, part):
            row = (g * 16 + gx * 4 + gy) * 64 + h * 32
            if part is None:
                return sum_q.at[pl.ds(pl.multiple_of(row, 16), 32)]
            return sum_q.at[pl.ds(pl.multiple_of(row + part * 16, 16), 16)]

        return piece

    def emit_q(g):
        def emit(h, result):
            for part in (0, 1):
                rows = result[part * 16 : part * 16 + 16]
                keep_q[g, 2 * h + part] = rows
                zs_q[g, 2 * h + part] = rows.astype(BF16)

        return emit

    runs = [Scatter(net, wire, own_q(g), bufs[8 * g : 8 * g + 8], emit_q(g)) for g in (0, 1)]

    def tokens_grad(c):
        rows = slice(c * 512, c * 512 + 512)
        tg_ref[:, rows] = lax.dot_general(
            gp_ref[...], w_ref[rows], (((1,), (1,)), ((), ())), preferred_element_type=F32
        ).astype(BF16)

    make_sibling(0)
    make_sibling(1)
    add_cores(0)
    runs[0].all_a()
    add_cores(1)
    runs[1].all_a()
    tokens_grad(0)
    runs[0].all_b()
    runs[1].all_b()
    tokens_grad(1)
    runs[0].all_c()
    runs[1].all_c()
    tokens_grad(2)
    runs[0].all_d()
    runs[1].all_d()
    tokens_grad(3)
    runs[0].all_e()
    runs[1].all_e()

    z1q = z1 + 7
    for k in range(1, 8):
        z_send(k, zs_q, zr_q, z1q)

    def place(l):
        return (
            out_q.at[pl.ds(pl.multiple_of(l * 16, 16), 16), cols_q[0]],
            out_o.at[:, pl.ds(pl.multiple_of(core * 1024 + l * 256, 128), 256)],
        )

    def level(k):
        l = lax.rem(net.zl + k, 4)
        return l, (net.s, l * 2 + core)

    z2 = wire.new(6)
    mine = place(net.zl)

    def z_sum(first, slots, key):
        result = first
        for k in range(1, 8):
            wire.recv(slots.at[k - 1], key + k - 1, net.up(8 - k))
            result = result + slots[k - 1].astype(F32)
        return result * scale

    def z_spread(which, ref, key):
        for k in (1, 2, 3):
            wire.send(ref, mine[which], key + k - 1, level(k)[1])

    fin_o[...] = z_sum(parts_o[net.zh, net.zl], zr_o, z1)
    z_spread(1, fin_o, z2)
    out_o[:, pl.ds(pl.multiple_of(core * 1024 + net.zl * 256, 128), 256)] = fin_o[...]
    fin_q[...] = z_sum(keep_q[net.zh, net.zl], zr_q, z1q)
    z_spread(0, fin_q, z2 + 3)
    out_q[pl.ds(pl.multiple_of(net.zl * 16, 16), 16), cols_q[0]] = fin_q[...]
    last = wire.new(2)
    for k in (1, 2, 3):
        l, device = level(4 - k)
        wire.recv(place(l)[1], z2 + k - 1, device)
    wire.send(out_o.at[:, cols_o[0]], out_o.at[:, cols_o[0]], last, net.sibling())
    for k in (1, 2, 3):
        l, device = level(4 - k)
        wire.recv(place(l)[0], z2 + 3 + k - 1, device)
    wire.send(out_q.at[:, cols_q[0]], out_q.at[:, cols_q[0]], last + 1, net.sibling())
    wire.recv(out_o.at[:, cols_o[1]], last, net.sibling())
    wire.recv(out_q.at[:, cols_q[1]], last + 1, net.sibling())
    wire.drain()


def weight_grads(inputs, grad_proj, qkv_full, parts_o, scale):
    keys = 2 * AG_KEYS + 14 + 2 + 6 + 2
    return pl.pallas_call(
        functools.partial(weight_grad_kernel, scale),
        out_shape=(
            jax.ShapeDtypeStruct((128, 2048), BF16),
            jax.ShapeDtypeStruct((64, 1536), F32),
            jax.ShapeDtypeStruct((32, 2048), F32),
        ),
        in_specs=[pl.BlockSpec(memory_space=pltpu.VMEM)] * 4,
        out_specs=[pl.BlockSpec(memory_space=pltpu.VMEM)] * 3,
        scratch_shapes=[
            pltpu.VMEM((2048, 128), BF16),
            pltpu.VMEM((2048, 768), BF16),
            pltpu.VMEM((2048, 768), BF16),
            pltpu.VMEM((2048, 768), BF16),
            pltpu.VMEM((2, 4, 16, 768), BF16),
            pltpu.VMEM((2, 4, 32, 256), BF16),
            pltpu.VMEM((7, 16, 768), BF16),
            pltpu.VMEM((7, 32, 256), BF16),
            pltpu.VMEM((2, 4, 16, 768), F32),
            pltpu.VMEM((16, 768), F32),
            pltpu.VMEM((32, 256), F32),
            pltpu.SemaphoreType.DMA((keys,)),
            pltpu.SemaphoreType.DMA((keys,)),
            *scatter_scratch(32, 768),
            *scatter_scratch(32, 768),
        ],
        compiler_params=pltpu.CompilerParams(
            collective_id=2, has_side_effects=True, vmem_limit_bytes=VMEM_BYTES
        ),
        name="weight_grads",
    )(inputs, grad_proj, qkv_full, parts_o)


def tables(positions, head_size):
    halves = head_size // 2
    frequency = ROPE_BASE ** (-(jnp.arange(halves, dtype=jnp.float32) * 2.0) / head_size)
    angles = positions.astype(jnp.float32)[:, None] * frequency[None, :]
    return (jnp.cos(angles), jnp.sin(angles))


def rotate(matrix, cos_rows, sin_rows, head_count):
    row_count = matrix.shape[0]
    head_size = matrix.shape[1] // head_count
    halves = head_size // 2
    pieces = matrix.reshape(row_count, head_count, 2, halves)
    lower_half = pieces[:, :, 0]
    upper_half = pieces[:, :, 1]
    cos_part = cos_rows[:, None, :]
    sin_part = sin_rows[:, None, :]
    turned = jnp.stack(
        [
            lower_half * cos_part - upper_half * sin_part,
            upper_half * cos_part + lower_half * sin_part,
        ],
        axis=2,
    )
    return turned.reshape(row_count, head_count * head_size)


def body(tokens, qkv_weight, out_weight, cotangent):
    inner_width = HEADS * HEAD_DIM
    kv_width = KV_HEADS * HEAD_DIM
    logit_scale = HEAD_DIM ** (-0.5)
    inputs = tokens[0]
    grad_output = cotangent[0]
    tok_count = inputs.shape[0]
    qkv_full = gather_qkv(qkv_weight)
    positions = lax.axis_index("shard") * tok_count + jnp.arange(tok_count, dtype=jnp.int32)
    cosine, sine = tables(positions, HEAD_DIM)
    projected = jnp.dot(inputs, qkv_full, preferred_element_type=F32)
    queries = rotate(projected[:, :inner_width], cosine, sine, HEADS).astype(BF16)
    key_rows = rotate(projected[:, inner_width : inner_width + kv_width], cosine, sine, KV_HEADS).astype(BF16)
    value_rows = projected[:, inner_width + kv_width :].astype(BF16)
    attended, query_sum, kv_grad, block_output, parts_o = attend(
        queries * BF16(logit_scale),
        jnp.concatenate([key_rows, value_rows], axis=1),
        grad_output,
        out_weight,
    )
    query_gradient = rotate(query_sum * logit_scale, cosine, -sine, HEADS).astype(BF16)
    grad_keys = rotate(kv_grad[:, :kv_width], cosine, -sine, KV_HEADS).astype(BF16)
    grad_values = kv_grad[:, kv_width:].astype(BF16)
    grad_proj = jnp.concatenate([query_gradient, grad_keys, grad_values], axis=1)
    norm_factor = 1.0 / math.sqrt(lax.axis_size("rep") * lax.axis_size("shard") * tok_count)
    tokens_grad, qkv_grad, out_grad = weight_grads(inputs, grad_proj, qkv_full, parts_o, norm_factor)
    return (block_output[None], tokens_grad[None], qkv_grad, out_grad)


def solution(mesh):
    return jax.shard_map(
        body,
        mesh=mesh,
        in_specs=(
            P("rep", "shard", None),
            P("shard", None),
            P("shard", None),
            P("rep", "shard", None),
        ),
        out_specs=(
            P("rep", "shard", None),
            P("rep", "shard", None),
            P("shard", None),
            P("shard", None),
        ),
        check_vma=False,
    )
```

```python
import functools
import math

import jax
import jax.numpy as jnp
from jax import lax
from jax.experimental import pallas as pl
from jax.experimental.pallas import tpu as pltpu
from jax.sharding import PartitionSpec as P

HEADS = 16
KV_HEADS = 4
HEAD_DIM = 64

ROPE_BASE = 500000.0
NEG_FILL = -1e30
MESH = pl.DeviceIdType.MESH
BF16 = jnp.bfloat16
F32 = jnp.float32
VMEM_BYTES = 60 * 1024 * 1024


class Net:
    def __init__(self):
        self.s = lax.axis_index("shard")
        self.r = lax.axis_index("rep")
        self.zh = self.s // 16
        self.x = lax.rem(self.s // 4, 4)
        self.y = lax.rem(self.s, 4)
        self.zl = self.r // 2
        self.core = lax.rem(self.r, 2)
        self.z = self.zh * 4 + self.zl

    def at(self, h, da, db):
        dx, dy = (da, db) if h == 0 else (db, da)
        return lax.rem(self.x + (dx + 4), 4), lax.rem(self.y + (dy + 4), 4)

    def dev(self, h, da, db):
        gx, gy = self.at(h, da, db)
        return (self.zh * 16 + gx * 4 + gy, self.r)

    def sibling(self):
        return (self.s, self.zl * 2 + 1 - self.core)

    def partner(self):
        return (lax.rem(self.s + 16, 32), self.r)

    def up(self, k):
        z = lax.rem(self.z + k, 8)
        return ((z // 4) * 16 + self.x * 4 + self.y, lax.rem(z, 4) * 2 + self.core)

    def xy_neighbours(self):
        return [self.dev(0, 1, 0), self.dev(0, -1, 0), self.dev(0, 0, 1), self.dev(0, 0, -1)]


def greet(devices):
    barrier = pltpu.get_barrier_semaphore()
    for device in devices:
        pl.semaphore_signal(barrier, inc=1, device_id=device, device_id_type=MESH)
    pl.semaphore_wait(barrier, len(devices))


class Wire:
    def __init__(self, send_sems, recv_sems, canvas, device):
        self.send_sems, self.recv_sems = send_sems, recv_sems
        self.canvas, self.device = canvas, device
        self.used = 0
        self.sent = []

    def new(self, count=1):
        first = self.used
        self.used += count
        return first

    def copy(self, src, dst, key, device):
        return pltpu.make_async_remote_copy(
            src_ref=src,
            dst_ref=dst,
            send_sem=self.send_sems.at[key],
            recv_sem=self.recv_sems.at[key],
            device_id=device,
            device_id_type=MESH,
        )

    def send(self, src, dst, key, device):
        self.copy(src, dst, key, device).start()
        self.sent.append((src.shape, src.dtype, key))

    def recv(self, ref, key, device):
        self.copy(ref, ref, key, device).wait_recv()

    def drain(self):
        for (rows, cols), dtype, key in self.sent:
            ref = self.canvas[dtype == F32].at[pl.ds(0, rows), pl.ds(0, cols)]
            self.copy(ref, ref, key, self.device).wait_send()
        self.sent = []


SIDES = (1, -1)
RING = (0, 1, -1, 2)
AG_KEYS = 40


def side(d):
    return 0 if d == 1 else 1


def gather_stages(net, wire, own, piece):
    base = wire.new(AG_KEYS)

    def s1(h, d):
        return base + h * 2 + side(d)

    def s2(h, d):
        return base + 4 + h * 2 + side(d)

    def t1(h, da, d):
        return base + 8 + (h * 4 + RING.index(da)) * 2 + side(d)

    def t2(h, da, d):
        return base + 24 + (h * 4 + RING.index(da)) * 2 + side(d)

    def at(h, da, db, part=None):
        return piece(*net.at(h, da, db), h, part)

    def spread(h, da, src):
        for d in SIDES:
            wire.send(src, at(h, da, 0), t1(h, da, d), net.dev(h, 0, d))

    def pass_on(h, da):
        for d in SIDES:
            wire.recv(at(h, da, -d), t1(h, da, d), net.dev(h, 0, -d))
            part = side(d)
            wire.send(at(h, da, -d, part), at(h, da, -d, part), t2(h, da, d), net.dev(h, 0, d))

    def stage_a():
        for h in (0, 1):
            for d in SIDES:
                wire.send(own(h), at(h, 0, 0), s1(h, d), net.dev(h, d, 0))
        for h in (0, 1):
            spread(h, 0, own(h))

    def stage_b():
        for d in SIDES:
            for h in (0, 1):
                wire.recv(at(h, -d, 0), s1(h, d), net.dev(h, -d, 0))
                part = side(d)
                wire.send(at(h, -d, 0, part), at(h, -d, 0, part), s2(h, d), net.dev(h, d, 0))
        for d in SIDES:
            for h in (0, 1):
                spread(h, -d, at(h, -d, 0))

    def stage_c():
        for h in (0, 1):
            pass_on(h, 0)

    def stage_d():
        for h in (0, 1):
            for d in SIDES:
                wire.recv(at(h, 2, 0, side(d)), s2(h, d), net.dev(h, -d, 0))
            spread(h, 2, at(h, 2, 0))

    def stage_e():
        for da in (-1, 1):
            for h in (0, 1):
                pass_on(h, da)

    def stage_f():
        for h in (0, 1):
            pass_on(h, 2)

    def stage_g():
        for da in (0, -1, 1, 2):
            for h in (0, 1):
                for d in SIDES:
                    wire.recv(at(h, da, 2, side(d)), t2(h, da, d), net.dev(h, 0, -d))

    return [stage_a, stage_b, stage_c, stage_d, stage_e, stage_f, stage_g]


def scatter_scratch(rows, cols):
    return [
        pltpu.VMEM((2, 4, 2, rows // 2, cols), BF16),
        pltpu.VMEM((2, 4, 2, rows, cols), BF16),
        pltpu.VMEM((2, 4, 2, rows, cols), BF16),
        pltpu.VMEM((2, 3, rows, cols), F32),
        pltpu.VMEM((2, rows, cols), BF16),
        pltpu.VMEM((2, 2, rows // 2, cols), BF16),
        pltpu.VMEM((2, 2, rows, cols), BF16),
        pltpu.VMEM((2, 2, rows, cols), BF16),
    ]


class Scatter:
    ORDER = (2, 1, -1, 0)

    def __init__(self, net, wire, own, bufs, emit):
        self.net, self.wire, self.own, self.emit = net, wire, own, emit
        self.t2b, self.t1s, self.t1b, self.row_sum, self.s2s, self.s2b, self.s1s, self.s1b = bufs
        self.rows = self.row_sum.shape[2]
        self.half = self.rows // 2
        self.base = wire.new(AG_KEYS)

    def s1(self, h, d):
        return self.base + h * 2 + side(d)

    def s2(self, h, d):
        return self.base + 4 + h * 2 + side(d)

    def t1(self, h, i, d):
        return self.base + 8 + (h * 4 + i) * 2 + side(d)

    def t2(self, h, i, d):
        return self.base + 24 + (h * 4 + i) * 2 + side(d)

    def part(self, p):
        return pl.ds(p * self.half, self.half)

    def load(self, h, da, db, part=None):
        return self.own(*self.net.at(h, da, db), h, part)[...].astype(F32)

    def a(self, h, da):
        i, net = RING.index(da), self.net
        for d in SIDES:
            p = side(d)
            src = self.own(*net.at(h, da, 2), h, p)
            self.wire.send(src, self.t2b.at[h, i, p], self.t2(h, i, d), net.dev(h, 0, d))

    def b(self, h, da, d):
        i, p, net = RING.index(da), side(d), self.net
        self.wire.recv(self.t2b.at[h, i, p], self.t2(h, i, d), net.dev(h, 0, -d))
        added = self.load(h, da, d, p) + self.t2b[h, i, p].astype(F32)
        self.t1s[h, i, p, self.part(p)] = added.astype(BF16)
        self.t1s[h, i, p, self.part(1 - p)] = self.load(h, da, d, 1 - p).astype(BF16)
        self.wire.send(self.t1s.at[h, i, p], self.t1b.at[h, i, p], self.t1(h, i, d), net.dev(h, 0, d))

    def c(self, h, da):
        i, net = RING.index(da), self.net
        for d in SIDES:
            self.wire.recv(self.t1b.at[h, i, side(d)], self.t1(h, i, d), net.dev(h, 0, -d))
        total = self.load(h, da, 0) + self.t1b[h, i, 0].astype(F32) + self.t1b[h, i, 1].astype(F32)
        if da != 2:
            self.row_sum[h, i] = total
            return
        self.s2s[h] = total.astype(BF16)
        for d in SIDES:
            p = side(d)
            self.wire.send(self.s2s.at[h, self.part(p)], self.s2b.at[h, p], self.s2(h, d), net.dev(h, d, 0))

    def d(self, h, d):
        i, p, net = RING.index(d), side(d), self.net
        self.wire.recv(self.s2b.at[h, p], self.s2(h, d), net.dev(h, -d, 0))
        added = self.row_sum[h, i, self.part(p)] + self.s2b[h, p].astype(F32)
        self.s1s[h, p, self.part(p)] = added.astype(BF16)
        self.s1s[h, p, self.part(1 - p)] = self.row_sum[h, i, self.part(1 - p)].astype(BF16)
        self.wire.send(self.s1s.at[h, p], self.s1b.at[h, p], self.s1(h, d), net.dev(h, d, 0))

    def e(self, h):
        for d in SIDES:
            self.wire.recv(self.s1b.at[h, side(d)], self.s1(h, d), self.net.dev(h, -d, 0))
        self.emit(h, self.row_sum[h, 0] + self.s1b[h, 0].astype(F32) + self.s1b[h, 1].astype(F32))

    def all_a(self):
        for da in self.ORDER:
            for h in (0, 1):
                self.a(h, da)

    def all_b(self):
        for da in self.ORDER:
            for h in (0, 1):
                for d in SIDES:
                    self.b(h, da, d)

    def all_c(self):
        for da in self.ORDER:
            for h in (0, 1):
                self.c(h, da)

    def all_d(self):
        for h in (0, 1):
            for d in SIDES:
                self.d(h, d)

    def all_e(self):
        for h in (0, 1):
            self.e(h)


def weight_gather_kernel(qkv_in, out_in, qkv_full, out_full, send_sems, recv_sems, local_sems):
    net = Net()
    wire = Wire(send_sems, recv_sems, (out_full, None), net.sibling())
    core, s = net.core, net.s
    other = 1 - net.zh
    qcols = pl.ds(pl.multiple_of(core * 768, 128), 768)

    def ocols(h):
        return pl.ds(pl.multiple_of(core * 1024 + h * 512, 128), 512)

    def qkv_piece(group):
        def piece(gx, gy, h, part):
            row = (group * 16 + gx * 4 + gy) * 64 + h * 32
            if part is None:
                return qkv_full.at[pl.ds(pl.multiple_of(row, 16), 32), qcols]
            return qkv_full.at[pl.ds(pl.multiple_of(row + part * 16, 16), 16), qcols]

        return piece

    def out_piece(group):
        def piece(gx, gy, h, part):
            row = (group * 16 + gx * 4 + gy) * 32
            if part is None:
                return out_full.at[pl.ds(pl.multiple_of(row, 16), 32), ocols(h)]
            return out_full.at[pl.ds(pl.multiple_of(row + part * 16, 16), 16), ocols(h)]

        return piece

    greet(net.xy_neighbours() + [net.sibling(), net.partner()])

    ohalf = pl.ds(pl.multiple_of(core * 1024, 128), 1024)
    qrow = pl.ds(pl.multiple_of(s * 64, 64), 64)
    orow = pl.ds(pl.multiple_of(s * 32, 32), 32)
    zkey = wire.new(2)
    wire.send(qkv_in.at[:, qcols], qkv_full.at[qrow, qcols], zkey, net.partner())
    wire.send(out_in.at[:, ohalf], out_full.at[orow, ohalf], zkey + 1, net.partner())
    own_q = gather_stages(net, wire, lambda h: qkv_in.at[pl.ds(h * 32, 32), qcols], qkv_piece(net.zh))
    own_o = gather_stages(net, wire, lambda h: out_in.at[:, ocols(h)], out_piece(net.zh))
    for a, b in zip(own_q[:1], own_o[:1]):
        a()
        b()
    keep_q = pltpu.make_async_copy(qkv_in.at[:, qcols], qkv_full.at[qrow, qcols], local_sems.at[0])
    keep_o = pltpu.make_async_copy(out_in.at[:, ohalf], out_full.at[orow, ohalf], local_sems.at[1])
    keep_q.start()
    keep_o.start()
    for a, b in zip(own_q[1:6], own_o[1:6]):
        a()
        b()
    far = lax.rem(s + 16, 32)
    far_q = qkv_full.at[pl.ds(pl.multiple_of(far * 64, 64), 64), qcols]
    far_o = out_full.at[pl.ds(pl.multiple_of(far * 32, 32), 32), ohalf]
    wire.recv(far_q, zkey, net.partner())
    wire.recv(far_o, zkey + 1, net.partner())
    far_qp, far_op = qkv_piece(other), out_piece(other)
    two_q = gather_stages(net, wire, lambda h: far_qp(net.x, net.y, h, None), far_qp)
    two_o = gather_stages(net, wire, lambda h: far_op(net.x, net.y, h, None), far_op)
    two_q[0]()
    two_o[0]()
    own_q[6]()
    own_o[6]()
    keep_q.wait()
    keep_o.wait()

    dkey = wire.new(4)

    def sides_of(group, which):
        cols = pl.ds(pl.multiple_of(which * 768, 128), 768)
        cols_o = pl.ds(pl.multiple_of(which * 1024, 128), 1024)
        return (
            qkv_full.at[pl.ds(pl.multiple_of(group * 1024, 64), 1024), cols],
            out_full.at[pl.ds(pl.multiple_of(group * 512, 32), 512), cols_o],
        )

    def share(group, key):
        for i, ref in enumerate(sides_of(group, core)):
            wire.send(ref, ref, key + i, net.sibling())

    share(net.zh, dkey)
    for a, b in zip(two_q[1:], two_o[1:]):
        a()
        b()
    share(other, dkey + 2)
    for group, key in ((net.zh, dkey), (other, dkey + 2)):
        for i, ref in enumerate(sides_of(group, 1 - core)):
            wire.recv(ref, key + i, net.sibling())
    wire.drain()


def gather_weights(qkv_weight, out_weight):
    keys = 4 * AG_KEYS + 6
    return pl.pallas_call(
        weight_gather_kernel,
        out_shape=(
            jax.ShapeDtypeStruct((2048, 1536), BF16),
            jax.ShapeDtypeStruct((1024, 2048), BF16),
        ),
        in_specs=[pl.BlockSpec(memory_space=pl.ANY)] * 2,
        out_specs=[pl.BlockSpec(memory_space=pl.ANY)] * 2,
        scratch_shapes=[
            pltpu.SemaphoreType.DMA((keys,)),
            pltpu.SemaphoreType.DMA((keys,)),
            pltpu.SemaphoreType.DMA((2,)),
        ],
        compiler_params=pltpu.CompilerParams(collective_id=0, has_side_effects=True),
        name="gather_weights",
    )(qkv_weight, out_weight)


BLOCK = 512


def spread_heads(rows_t, padded, natural):
    padded[...] = jnp.zeros_like(padded)
    for g in range(4):
        for k in range(4):
            head = 4 * g + k
            padded[g, g * 64 : g * 64 + 64, k * 128 : k * 128 + 128] = rows_t[head * 64 : head * 64 + 64]
        natural[g * 512 : g * 512 + 512] = padded[g].T


def attend_kernel(
    q_ref,
    kv_in,
    cot_ref,
    out_hbm,
    cos_ref,
    sin_ref,
    gp_ref,
    block_ref,
    parts_o,
    kv_ref,
    out_full,
    kvg_ref,
    terms,
    qt,
    qn,
    dot_,
    don,
    probs,
    peaks,
    peak,
    total,
    acc,
    dqt,
    dots,
    att_t,
    do_sib,
    sib_o,
    sum_o,
    far_out,
    far_in,
    send_sems,
    recv_sems,
    local_sem,
    *bufs,
):
    net = Net()
    wire = Wire(send_sems, recv_sems, (sum_o, None), net.sibling())
    s, x, zh, core = net.s, net.x, net.zh, net.core
    other = 1 - zh

    def kv_place(ref, group):
        def piece(gx, gy, h, part):
            row = (group * 16 + gx * 4 + gy) * 128 + h * 64
            if part is None:
                return ref.at[pl.ds(pl.multiple_of(row, 32), 64)]
            return ref.at[pl.ds(pl.multiple_of(row + part * 32, 32), 32)]

        return piece

    def kv_rows(shard):
        return kv_ref.at[pl.ds(pl.multiple_of(shard * 128, 128), 128)]

    far_shard = lax.rem(s + 16, 32)
    half_cols = pl.ds(pl.multiple_of(core * 1024, 128), 1024)

    greet(net.xy_neighbours() + [net.sibling(), net.partner()])

    fetch = pltpu.make_async_copy(out_hbm, out_full, local_sem)
    fetch.start()
    zkey = wire.new(1)
    wire.send(kv_in, kv_rows(s), zkey, net.partner())
    near = gather_stages(net, wire, lambda h: kv_in.at[pl.ds(h * 64, 64)], kv_place(kv_ref, zh))
    near[0]()
    kv_ref[pl.ds(pl.multiple_of(s * 128, 128), 128)] = kv_in[...]
    peak[...] = jnp.full_like(peak, NEG_FILL)
    total[...] = jnp.zeros_like(total)
    acc[...] = jnp.zeros_like(acc)
    dqt[...] = jnp.zeros_like(dqt)
    spread_heads(q_ref[...].T, qt, qn)
    near[1]()
    near[2]()
    fetch.wait()
    grad_t = lax.dot_general(
        out_full[...], cot_ref[...], (((1,), (1,)), ((), ())), preferred_element_type=F32
    ).astype(BF16)
    near[3]()
    near[4]()
    spread_heads(grad_t, dot_, don)
    near[5]()
    wire.recv(kv_rows(far_shard), zkey, net.partner())
    far_place = kv_place(kv_ref, other)
    far = gather_stages(net, wire, lambda h: far_place(net.x, net.y, h, None), far_place)
    far[0]()
    near[6]()

    def rows_of(j):
        return pl.ds(pl.multiple_of(j * BLOCK, BLOCK), BLOCK)

    def forward(j, masked):
        keys = kv_ref[rows_of(j), 0:256]
        values_t = kv_ref[rows_of(j), 256:512].T
        if masked:
            key_at = lax.broadcasted_iota(jnp.int32, (BLOCK, 512), 0) + j * BLOCK
            query_at = lax.rem(lax.broadcasted_iota(jnp.int32, (BLOCK, 512), 1), 128) + s * 128
            visible = key_at <= query_at
        ahead = jnp.dot(keys, qt[0], preferred_element_type=F32)
        for g in range(4):
            scores = ahead
            if g < 3:
                ahead = jnp.dot(keys, qt[g + 1], preferred_element_type=F32)
            if masked:
                scores = jnp.where(visible, scores, NEG_FILL)
            before = peak[g]
            now = jnp.maximum(before, jnp.max(scores, axis=0, keepdims=True))
            fade = jnp.exp(before - now)
            e = jnp.exp(scores - now)
            total[g] = total[g] * fade + jnp.sum(e, axis=0, keepdims=True)
            e = e.astype(BF16)
            probs[g, j] = e
            peaks[g, j] = now
            peak[g] = now
            acc[g] = acc[g] * fade + jnp.dot(values_t[g * 64 : g * 64 + 64], e, preferred_element_type=F32)

    def in_turn(plans, i):
        for k, plan in enumerate(plans):

            @pl.when(i == k)
            def _():
                for stage in plan:
                    stage()

    def near_forward(i, carry):
        in_turn([[far[1]], [far[2]], [far[3]], [far[4]]], i)

        @pl.when(i < x)
        def _():
            forward(zh * 4 + i, False)

        @pl.when(i == x)
        def _():
            forward(zh * 4 + i, True)

        return carry

    lax.fori_loop(0, 4, near_forward, 0)
    far[5]()
    far[6]()

    @pl.when(zh == 1)
    def _():
        def far_forward(i, carry):
            forward(i, False)
            return carry

        lax.fori_loop(0, 4, far_forward, 0)

    for g in range(4):
        attended = (acc[g] / total[g]).astype(BF16)
        for k in range(4):
            head = 4 * g + k
            att_t[head * 64 : head * 64 + 64] = attended[:, k * 128 : k * 128 + 128]
    core_key = wire.new(2)
    for g in (0, 1):
        rows = slice(g * 512, g * 512 + 512)
        sib_cols = pl.ds(pl.multiple_of((1 - core) * 1024, 128), 1024)
        do_sib[rows] = jnp.dot(att_t[rows], cot_ref[:, sib_cols], preferred_element_type=F32).astype(BF16)
        wire.send(do_sib.at[pl.ds(g * 512, 512)], sib_o.at[pl.ds(g * 512, 512)], core_key + g, net.sibling())
    for g in range(4):
        for k in range(4):
            head = 4 * g + k
            rows = slice(head * 64, head * 64 + 64)
            both = att_t[rows].astype(F32) * dot_[g, g * 64 : g * 64 + 64, k * 128 : k * 128 + 128].astype(F32)
            dots[g, :, k * 128 : k * 128 + 128] = jnp.sum(both, axis=0, keepdims=True)
        peak[g] = peak[g] + jnp.log(total[g])

    def out_own(group):
        def piece(gx, gy, h, part):
            row = (group * 16 + gx * 4 + gy) * 32
            if part is None:
                return sum_o.at[pl.ds(pl.multiple_of(row, 16), 32), pl.ds(h * 512, 512)]
            return sum_o.at[pl.ds(pl.multiple_of(row + part * 16, 16), 16), pl.ds(h * 512, 512)]

        return piece

    def out_emit(group):
        def emit(h, result):
            for part in (0, 1):
                parts_o[group, 2 * h + part] = result[:, part * 256 : part * 256 + 256]

        return emit

    scat_o = [Scatter(net, wire, out_own(g), bufs[16 + 8 * g : 24 + 8 * g], out_emit(g)) for g in (0, 1)]

    def add_cores(g):
        def run():
            rows = slice(g * 512, g * 512 + 512)
            wire.recv(sib_o.at[pl.ds(g * 512, 512)], core_key + g, net.sibling())
            own = jnp.dot(att_t[rows], cot_ref[:, half_cols], preferred_element_type=F32)
            sum_o[rows] = (own + sib_o[rows].astype(F32)).astype(BF16)
            scat_o[g].all_a()

        return run

    def backward(j):
        keys_t = kv_ref[rows_of(j), 0:256].T
        values = kv_ref[rows_of(j), 256:512]
        ahead = jnp.dot(values, dot_[0], preferred_element_type=F32)
        dk = dv = None
        for g in range(4):
            grads = ahead
            if g < 3:
                ahead = jnp.dot(values, dot_[g + 1], preferred_element_type=F32)
            p = probs[g, j].astype(F32) * jnp.exp(peaks[g, j] - peak[g])
            ds = (p * (grads - dots[g])).astype(BF16)
            p = p.astype(BF16)
            dqt[g] += jnp.dot(keys_t[g * 64 : g * 64 + 64], ds, preferred_element_type=F32)
            rows = slice(g * 512, g * 512 + 512)
            dk_g = jnp.dot(ds, qn[rows], preferred_element_type=F32)
            dv_g = jnp.dot(p, don[rows], preferred_element_type=F32)
            dk = dk_g if g == 0 else dk + dk_g
            dv = dv_g if g == 0 else dv + dv_g
        terms[rows_of(j), 0:256] = dk.astype(BF16)
        terms[rows_of(j), 256:512] = dv.astype(BF16)

    zback = wire.new(2)

    def emit_far(h, result):
        far_out[h] = result.astype(BF16)
        wire.send(far_out.at[h], far_in.at[h], zback + h, net.partner())

    def emit_near(h, result):
        kvg_ref[pl.ds(h * 64, 64)] = result

    scat_far = Scatter(net, wire, kv_place(terms, other), bufs[0:8], emit_far)
    scat_near = Scatter(net, wire, kv_place(terms, zh), bufs[8:16], emit_near)

    def after(scat):
        one = functools.partial

        def plan0():
            scat.a(0, 2)
            for da in scat.ORDER:
                scat.a(1, da)

        def plan1():
            scat.a(0, 1)
            for da in scat.ORDER:
                scat.b(1, da, 1)
            for d in SIDES:
                scat.b(0, 2, d)

        def plan2():
            scat.a(0, -1)
            for da in scat.ORDER:
                scat.b(1, da, -1)
            for d in SIDES:
                scat.b(0, 1, d)
            scat.c(0, 2)

        def plan3():
            scat.a(0, 0)
            for d in SIDES:
                scat.b(0, -1, d)
            scat.c(1, 2)
            scat.c(0, 1)

        return [[plan0], [plan1], [plan2], [plan3]]

    def late1(scat):
        def run():
            for d in SIDES:
                scat.b(0, 0, d)
            for da in (1, -1, 0):
                scat.c(1, da)
            scat.c(0, -1)

        return run

    def late2(scat):
        def run():
            scat.c(0, 0)
            scat.all_d()

        return run

    def block_loop(group, plans):
        def step(i, carry):
            turn = lax.rem(18 - i + 3 * ((i * (i - 1)) // 2), 4)
            j = group * 4 + lax.rem(x + turn, 4)

            @pl.when(j <= s // 4)
            def _():
                backward(j)

            @pl.when(j > s // 4)
            def _():
                terms[rows_of(j)] = jnp.zeros((BLOCK, 512), BF16)

            in_turn(plans, i)
            return carry

        lax.fori_loop(0, 4, step, 0)

    plans = after(scat_far)
    plans[1].append(add_cores(0))
    plans[2].append(add_cores(1))
    plans[3].append(scat_o[0].all_b)
    block_loop(other, plans)
    plans = after(scat_near)
    plans[0] = [late1(scat_far)] + plans[0] + [scat_o[1].all_b]
    plans[1] = [late2(scat_far)] + plans[1] + [scat_o[0].all_c]
    plans[2] = [scat_far.all_e] + plans[2] + [scat_o[1].all_c, scat_o[0].all_d]
    plans[3] = plans[3] + [scat_o[1].all_d, scat_o[0].all_e]
    block_loop(zh, plans)
    late1(scat_near)()
    attended = att_t[...].T
    for c in range(4):
        cols = slice(c * 512, c * 512 + 512)
        block_ref[:, cols] = jnp.dot(attended, out_full[:, cols], preferred_element_type=F32).astype(BF16)
    late2(scat_near)()
    cos, sin = cos_ref[...], sin_ref[...]

    def turn_back(rows_t):
        a, b = rows_t[0:32], rows_t[32:64]
        return jnp.concatenate([a * cos + b * sin, b * cos - a * sin], axis=0)

    for g in range(4):
        for k in range(0, 4, 2):
            head = 4 * g + k
            pair = [turn_back(dqt[g, :, c * 128 : c * 128 + 128] * 0.125) for c in (k, k + 1)]
            gp_ref[:, head * 64 : head * 64 + 128] = jnp.concatenate(pair, axis=0).T.astype(BF16)
    scat_o[1].all_e()
    scat_near.all_e()
    for h in (0, 1):
        wire.recv(far_in.at[h], zback + h, net.partner())
        kvg_ref[pl.ds(h * 64, 64)] += far_in[h].astype(F32)
    for c in range(2):
        keys_t = kvg_ref[:, c * 128 : c * 128 + 128].T
        pair = [turn_back(keys_t[0:64]), turn_back(keys_t[64:128])]
        gp_ref[:, 1024 + c * 128 : 1152 + c * 128] = jnp.concatenate(pair, axis=0).T.astype(BF16)
    gp_ref[:, 1280:1536] = kvg_ref[:, 256:512].astype(BF16)
    wire.drain()


def attend(queries, kv, cotangent, out_full, cos_t, sin_t):
    keys = 6 * AG_KEYS + 5
    return pl.pallas_call(
        attend_kernel,
        out_shape=(
            jax.ShapeDtypeStruct((128, 1536), BF16),
            jax.ShapeDtypeStruct((128, 2048), BF16),
            jax.ShapeDtypeStruct((2, 4, 32, 256), F32),
        ),
        in_specs=[pl.BlockSpec(memory_space=pltpu.VMEM)] * 3
        + [pl.BlockSpec(memory_space=pl.ANY)]
        + [pl.BlockSpec(memory_space=pltpu.VMEM)] * 2,
        out_specs=[pl.BlockSpec(memory_space=pltpu.VMEM)] * 3,
        scratch_shapes=[
            pltpu.VMEM((4096, 512), BF16),
            pltpu.VMEM((1024, 2048), BF16),
            pltpu.VMEM((128, 512), F32),
            pltpu.VMEM((4096, 512), BF16),
            pltpu.VMEM((4, 256, 512), BF16),
            pltpu.VMEM((2048, 256), BF16),
            pltpu.VMEM((4, 256, 512), BF16),
            pltpu.VMEM((2048, 256), BF16),
            pltpu.VMEM((4, 8, BLOCK, 512), BF16),
            pltpu.VMEM((4, 8, 1, 512), F32),
            pltpu.VMEM((4, 1, 512), F32),
            pltpu.VMEM((4, 1, 512), F32),
            pltpu.VMEM((4, 64, 512), F32),
            pltpu.VMEM((4, 64, 512), F32),
            pltpu.VMEM((4, 1, 512), F32),
            pltpu.VMEM((1024, 128), BF16),
            pltpu.VMEM((1024, 1024), BF16),
            pltpu.VMEM((1024, 1024), BF16),
            pltpu.VMEM((1024, 1024), BF16),
            pltpu.VMEM((2, 64, 512), BF16),
            pltpu.VMEM((2, 64, 512), BF16),
            pltpu.SemaphoreType.DMA((keys,)),
            pltpu.SemaphoreType.DMA((keys,)),
            pltpu.SemaphoreType.DMA,
            *scatter_scratch(64, 512),
            *scatter_scratch(64, 512),
            *scatter_scratch(32, 512),
            *scatter_scratch(32, 512),
        ],
        compiler_params=pltpu.CompilerParams(
            collective_id=1, has_side_effects=True, vmem_limit_bytes=VMEM_BYTES
        ),
        name="attend",
    )(queries, kv, cotangent, out_full, cos_t, sin_t)


def weight_grad_kernel(
    scale,
    x_ref,
    gp_ref,
    w_ref,
    parts_o,
    tg_ref,
    out_q,
    out_o,
    xt,
    do_sib,
    sib_q,
    sum_q,
    zs_q,
    zs_o,
    zr_q,
    zr_o,
    keep_q,
    fin_q,
    fin_o,
    got_q,
    got_o,
    canvas,
    send_sems,
    recv_sems,
    *bufs,
):
    net = Net()
    wire = Wire(send_sems, recv_sems, (canvas, None), net.sibling())
    core = net.core
    cols_q = [pl.ds(pl.multiple_of(c * 768, 128), 768) for c in (core, 1 - core)]
    cols_o = [pl.ds(pl.multiple_of(c * 1024, 128), 1024) for c in (core, 1 - core)]
    greet(net.xy_neighbours() + [net.sibling()] + [net.up(k) for k in range(1, 8)])

    z1 = wire.new(14)

    def z_send(k, staged, slots, key):
        target = lax.rem(net.z + k, 8)
        wire.send(staged.at[target // 4, lax.rem(target, 4)], slots.at[k - 1], key + k - 1, net.up(k))

    for g in (0, 1):
        for l in range(4):
            zs_o[g, l] = parts_o[g, l].astype(BF16)
    for k in range(1, 8):
        z_send(k, zs_o, zr_o, z1)

    xt[...] = x_ref[...].T
    ckey = wire.new(2)

    def product(rows, cols):
        return jnp.dot(xt[rows], gp_ref[:, cols], preferred_element_type=F32)

    def make_sibling(g):
        def step(i, carry):
            rows = pl.ds(pl.multiple_of(g * 1024 + i * 256, 256), 256)
            do_sib[rows] = product(rows, cols_q[1]).astype(BF16)
            return carry

        lax.fori_loop(0, 4, step, 0)
        rows = pl.ds(g * 1024, 1024)
        wire.send(do_sib.at[rows], sib_q.at[rows], ckey + g, net.sibling())

    def add_cores(g):
        wire.recv(sib_q.at[pl.ds(g * 1024, 1024)], ckey + g, net.sibling())

        def step(i, carry):
            rows = pl.ds(pl.multiple_of(g * 1024 + i * 256, 256), 256)
            sum_q[rows] = (product(rows, cols_q[0]) + sib_q[rows].astype(F32)).astype(BF16)
            return carry

        lax.fori_loop(0, 4, step, 0)

    def own_q(g):
        def piece(gx, gy, h, part):
            row = (g * 16 + gx * 4 + gy) * 64 + h * 32
            if part is None:
                return sum_q.at[pl.ds(pl.multiple_of(row, 16), 32)]
            return sum_q.at[pl.ds(pl.multiple_of(row + part * 16, 16), 16)]

        return piece

    def emit_q(g):
        def emit(h, result):
            for part in (0, 1):
                rows = result[part * 16 : part * 16 + 16]
                keep_q[g, 2 * h + part] = rows
                zs_q[g, 2 * h + part] = rows.astype(BF16)

        return emit

    runs = [Scatter(net, wire, own_q(g), bufs[8 * g : 8 * g + 8], emit_q(g)) for g in (0, 1)]

    def tokens_grad(c):
        rows = slice(c * 512, c * 512 + 512)
        tg_ref[:, rows] = lax.dot_general(
            gp_ref[...], w_ref[rows], (((1,), (1,)), ((), ())), preferred_element_type=F32
        ).astype(BF16)

    make_sibling(0)
    make_sibling(1)
    add_cores(0)
    runs[0].all_a()
    add_cores(1)
    runs[1].all_a()
    tokens_grad(0)
    runs[0].all_b()
    runs[1].all_b()
    tokens_grad(1)
    runs[0].all_c()
    runs[1].all_c()
    tokens_grad(2)
    runs[0].all_d()
    runs[1].all_d()
    tokens_grad(3)
    runs[0].all_e()
    runs[1].all_e()

    z1q = z1 + 7
    for k in range(1, 8):
        z_send(k, zs_q, zr_q, z1q)

    def place(l):
        return (
            got_q.at[pl.ds(pl.multiple_of(l * 16, 16), 16), cols_q[0]],
            got_o.at[:, pl.ds(pl.multiple_of(core * 1024 + l * 256, 128), 256)],
        )

    def level(k):
        l = lax.rem(net.zl + k, 4)
        return l, (net.s, l * 2 + core)

    z2 = wire.new(6)
    mine = place(net.zl)

    def z_sum(first, slots, key):
        result = first
        for k in range(1, 8):
            wire.recv(slots.at[k - 1], key + k - 1, net.up(8 - k))
            result = result + slots[k - 1].astype(F32)
        return (result * scale).astype(BF16)

    def z_spread(which, ref, key):
        for k in (1, 2, 3):
            wire.send(ref, mine[which], key + k - 1, level(k)[1])

    fin_o[...] = z_sum(parts_o[net.zh, net.zl], zr_o, z1)
    z_spread(1, fin_o, z2)
    got_o[:, pl.ds(pl.multiple_of(core * 1024 + net.zl * 256, 128), 256)] = fin_o[...]
    fin_q[...] = z_sum(keep_q[net.zh, net.zl], zr_q, z1q)
    z_spread(0, fin_q, z2 + 3)
    got_q[pl.ds(pl.multiple_of(net.zl * 16, 16), 16), cols_q[0]] = fin_q[...]
    last = wire.new(2)
    for k in (1, 2, 3):
        l, device = level(4 - k)
        wire.recv(place(l)[1], z2 + k - 1, device)
    wire.send(got_o.at[:, cols_o[0]], got_o.at[:, cols_o[0]], last, net.sibling())
    for k in (1, 2, 3):
        l, device = level(4 - k)
        wire.recv(place(l)[0], z2 + 3 + k - 1, device)
    wire.send(got_q.at[:, cols_q[0]], got_q.at[:, cols_q[0]], last + 1, net.sibling())
    wire.recv(got_o.at[:, cols_o[1]], last, net.sibling())
    wire.recv(got_q.at[:, cols_q[1]], last + 1, net.sibling())
    out_o[...] = got_o[...].astype(F32)
    out_q[...] = got_q[...].astype(F32)
    wire.drain()


def weight_grads(inputs, grad_proj, qkv_full, parts_o, scale):
    keys = 2 * AG_KEYS + 14 + 2 + 6 + 2
    return pl.pallas_call(
        functools.partial(weight_grad_kernel, scale),
        out_shape=(
            jax.ShapeDtypeStruct((128, 2048), BF16),
            jax.ShapeDtypeStruct((64, 1536), F32),
            jax.ShapeDtypeStruct((32, 2048), F32),
        ),
        in_specs=[pl.BlockSpec(memory_space=pltpu.VMEM)] * 4,
        out_specs=[pl.BlockSpec(memory_space=pltpu.VMEM)] * 3,
        scratch_shapes=[
            pltpu.VMEM((2048, 128), BF16),
            pltpu.VMEM((2048, 768), BF16),
            pltpu.VMEM((2048, 768), BF16),
            pltpu.VMEM((2048, 768), BF16),
            pltpu.VMEM((2, 4, 16, 768), BF16),
            pltpu.VMEM((2, 4, 32, 256), BF16),
            pltpu.VMEM((7, 16, 768), BF16),
            pltpu.VMEM((7, 32, 256), BF16),
            pltpu.VMEM((2, 4, 16, 768), F32),
            pltpu.VMEM((16, 768), BF16),
            pltpu.VMEM((32, 256), BF16),
            pltpu.VMEM((64, 1536), BF16),
            pltpu.VMEM((32, 2048), BF16),
            pltpu.VMEM((1024, 1024), BF16),
            pltpu.SemaphoreType.DMA((keys,)),
            pltpu.SemaphoreType.DMA((keys,)),
            *scatter_scratch(32, 768),
            *scatter_scratch(32, 768),
        ],
        compiler_params=pltpu.CompilerParams(
            collective_id=2, has_side_effects=True, vmem_limit_bytes=VMEM_BYTES
        ),
        name="weight_grads",
    )(inputs, grad_proj, qkv_full, parts_o)


def finish_kernel(*refs):
    for i in range(4):
        refs[i + 4][...] = refs[i][...]


def finish(*results):
    return pl.pallas_call(
        finish_kernel,
        out_shape=tuple(jax.ShapeDtypeStruct(r.shape, r.dtype) for r in results),
        in_specs=[pl.BlockSpec(memory_space=pltpu.VMEM)] * 4,
        out_specs=[pl.BlockSpec(memory_space=pltpu.VMEM)] * 4,
        name="finish",
    )(*results)


def tables(positions, head_size):
    halves = head_size // 2
    frequency = ROPE_BASE ** (-(jnp.arange(halves, dtype=jnp.float32) * 2.0) / head_size)
    angles = positions.astype(jnp.float32)[:, None] * frequency[None, :]
    return (jnp.cos(angles), jnp.sin(angles))


def rotate(matrix, cos_rows, sin_rows, head_count):
    row_count = matrix.shape[0]
    head_size = matrix.shape[1] // head_count
    halves = head_size // 2
    pieces = matrix.reshape(row_count, head_count, 2, halves)
    lower_half = pieces[:, :, 0]
    upper_half = pieces[:, :, 1]
    cos_part = cos_rows[:, None, :]
    sin_part = sin_rows[:, None, :]
    turned = jnp.stack(
        [
            lower_half * cos_part - upper_half * sin_part,
            upper_half * cos_part + lower_half * sin_part,
        ],
        axis=2,
    )
    return turned.reshape(row_count, head_count * head_size)


def body(tokens, qkv_weight, out_weight, cotangent):
    inner_width = HEADS * HEAD_DIM
    kv_width = KV_HEADS * HEAD_DIM
    logit_scale = HEAD_DIM ** (-0.5)
    inputs = tokens[0]
    grad_output = cotangent[0]
    tok_count = inputs.shape[0]
    qkv_full, out_full = gather_weights(qkv_weight, out_weight)
    positions = lax.axis_index("shard") * tok_count + jnp.arange(tok_count, dtype=jnp.int32)
    cosine, sine = tables(positions, HEAD_DIM)
    projected = jnp.dot(inputs, qkv_full, preferred_element_type=F32)
    queries = rotate(projected[:, :inner_width], cosine, sine, HEADS).astype(BF16)
    key_rows = rotate(projected[:, inner_width : inner_width + kv_width], cosine, sine, KV_HEADS).astype(BF16)
    value_rows = projected[:, inner_width + kv_width :].astype(BF16)
    grad_proj, block_output, parts_o = attend(
        queries * BF16(logit_scale),
        jnp.concatenate([key_rows, value_rows], axis=1),
        grad_output,
        out_full,
        cosine.T,
        sine.T,
    )
    norm_factor = 1.0 / math.sqrt(lax.axis_size("rep") * lax.axis_size("shard") * tok_count)
    tokens_grad, qkv_grad, out_grad = weight_grads(inputs, grad_proj, qkv_full, parts_o, norm_factor)
    block_output, tokens_grad, qkv_grad, out_grad = finish(block_output, tokens_grad, qkv_grad, out_grad)
    return (block_output[None], tokens_grad[None], qkv_grad, out_grad)


def solution(mesh):
    return jax.shard_map(
        body,
        mesh=mesh,
        in_specs=(
            P("rep", "shard", None),
            P("shard", None),
            P("shard", None),
            P("rep", "shard", None),
        ),
        out_specs=(
            P("rep", "shard", None),
            P("rep", "shard", None),
            P("shard", None),
            P("shard", None),
        ),
        check_vma=False,
    )
```

```python
import functools
import math

import jax
import jax.numpy as jnp
from jax import lax
from jax.experimental import pallas as pl
from jax.experimental.pallas import tpu as pltpu
from jax.sharding import PartitionSpec as P

HEADS = 16
KV_HEADS = 4
HEAD_DIM = 64

ROPE_BASE = 500000.0
NEG_FILL = -1e30
MESH = pl.DeviceIdType.MESH
BF16 = jnp.bfloat16
F32 = jnp.float32
VMEM_BYTES = 62 * 1024 * 1024


class Net:
    def __init__(self):
        self.s = lax.axis_index("shard")
        self.r = lax.axis_index("rep")
        self.zh = self.s // 16
        self.x = lax.rem(self.s // 4, 4)
        self.y = lax.rem(self.s, 4)
        self.zl = self.r // 2
        self.core = lax.rem(self.r, 2)
        self.z = self.zh * 4 + self.zl

    def at(self, h, da, db):
        dx, dy = (da, db) if h == 0 else (db, da)
        return lax.rem(self.x + (dx + 4), 4), lax.rem(self.y + (dy + 4), 4)

    def dev(self, h, da, db):
        gx, gy = self.at(h, da, db)
        return (self.zh * 16 + gx * 4 + gy, self.r)

    def sibling(self):
        return (self.s, self.zl * 2 + 1 - self.core)

    def partner(self):
        return (lax.rem(self.s + 16, 32), self.r)

    def up(self, k):
        z = lax.rem(self.z + k, 8)
        return ((z // 4) * 16 + self.x * 4 + self.y, lax.rem(z, 4) * 2 + self.core)

    def xy_neighbours(self):
        return [self.dev(0, 1, 0), self.dev(0, -1, 0), self.dev(0, 0, 1), self.dev(0, 0, -1)]


def greet(devices):
    barrier = pltpu.get_barrier_semaphore()
    for device in devices:
        pl.semaphore_signal(barrier, inc=1, device_id=device, device_id_type=MESH)
    pl.semaphore_wait(barrier, len(devices))


class Wire:
    def __init__(self, send_sems, recv_sems, canvas, device):
        self.send_sems, self.recv_sems = send_sems, recv_sems
        self.canvas, self.device = canvas, device
        self.used = 0
        self.sent = []

    def new(self, count=1):
        first = self.used
        self.used += count
        return first

    def copy(self, src, dst, key, device):
        return pltpu.make_async_remote_copy(
            src_ref=src,
            dst_ref=dst,
            send_sem=self.send_sems.at[key],
            recv_sem=self.recv_sems.at[key],
            device_id=device,
            device_id_type=MESH,
        )

    def send(self, src, dst, key, device):
        self.copy(src, dst, key, device).start()
        self.sent.append((src.shape, src.dtype, key))

    def recv(self, ref, key, device):
        self.copy(ref, ref, key, device).wait_recv()

    def taken(self):
        sent, self.sent = self.sent, []
        return sent

    def drain(self, sent=None):
        for shape, dtype, key in self.taken() if sent is None else sent:
            cols = shape[1] if len(shape) == 2 else 1024 if len(shape) == 4 else 256
            rows = math.prod(shape) // cols
            ref = self.canvas[dtype == F32].at[pl.ds(0, rows), pl.ds(0, cols)]
            self.copy(ref, ref, key, self.device).wait_send()


SIDES = (1, -1)
RING = (0, 1, -1, 2)
AG_KEYS = 40


def side(d):
    return 0 if d == 1 else 1


class Stages(list):
    def __init__(self, base, stages):
        super().__init__(stages)
        self.base = base


def gather_stages(net, wire, own, piece):
    base = wire.new(AG_KEYS)

    def s1(h, d):
        return base + h * 2 + side(d)

    def s2(h, d):
        return base + 4 + h * 2 + side(d)

    def t1(h, da, d):
        return base + 8 + (h * 4 + RING.index(da)) * 2 + side(d)

    def t2(h, da, d):
        return base + 24 + (h * 4 + RING.index(da)) * 2 + side(d)

    def at(h, da, db, part=None):
        return piece(*net.at(h, da, db), h, part)

    def spread(h, da, src):
        for d in SIDES:
            wire.send(src, at(h, da, 0), t1(h, da, d), net.dev(h, 0, d))

    def pass_on(h, da):
        for d in SIDES:
            wire.recv(at(h, da, -d), t1(h, da, d), net.dev(h, 0, -d))
            part = side(d)
            wire.send(at(h, da, -d, part), at(h, da, -d, part), t2(h, da, d), net.dev(h, 0, d))

    def stage_a():
        for h in (0, 1):
            for d in SIDES:
                wire.send(own(h), at(h, 0, 0), s1(h, d), net.dev(h, d, 0))
        for h in (0, 1):
            spread(h, 0, own(h))

    def stage_b():
        for d in SIDES:
            for h in (0, 1):
                wire.recv(at(h, -d, 0), s1(h, d), net.dev(h, -d, 0))
                part = side(d)
                wire.send(at(h, -d, 0, part), at(h, -d, 0, part), s2(h, d), net.dev(h, d, 0))
        for d in SIDES:
            for h in (0, 1):
                spread(h, -d, at(h, -d, 0))

    def stage_c():
        for h in (0, 1):
            pass_on(h, 0)

    def stage_d():
        for h in (0, 1):
            for d in SIDES:
                wire.recv(at(h, 2, 0, side(d)), s2(h, d), net.dev(h, -d, 0))
            spread(h, 2, at(h, 2, 0))

    def stage_e():
        for da in (-1, 1):
            for h in (0, 1):
                pass_on(h, da)

    def stage_f():
        for h in (0, 1):
            pass_on(h, 2)

    def stage_g():
        for da in (0, -1, 1, 2):
            for h in (0, 1):
                for d in SIDES:
                    wire.recv(at(h, da, 2, side(d)), t2(h, da, d), net.dev(h, 0, -d))

    return Stages(base, [stage_a, stage_b, stage_c, stage_d, stage_e, stage_f, stage_g])


def scatter_scratch(rows, cols):
    return [
        pltpu.VMEM((2, 4, 2, rows // 2, cols), BF16),
        pltpu.VMEM((2, 4, 2, rows, cols), BF16),
        pltpu.VMEM((2, 4, 2, rows, cols), BF16),
        pltpu.VMEM((2, 3, rows, cols), F32),
        pltpu.VMEM((2, rows, cols), BF16),
        pltpu.VMEM((2, 2, rows // 2, cols), BF16),
        pltpu.VMEM((2, 2, rows, cols), BF16),
        pltpu.VMEM((2, 2, rows, cols), BF16),
    ]


class Scatter:
    ORDER = (2, 1, -1, 0)

    def __init__(self, net, wire, own, bufs, emit):
        self.net, self.wire, self.own, self.emit = net, wire, own, emit
        self.t2b, self.t1s, self.t1b, self.row_sum, self.s2s, self.s2b, self.s1s, self.s1b = bufs
        self.rows = self.row_sum.shape[2]
        self.half = self.rows // 2
        self.base = wire.new(AG_KEYS)

    def s1(self, h, d):
        return self.base + h * 2 + side(d)

    def s2(self, h, d):
        return self.base + 4 + h * 2 + side(d)

    def t1(self, h, i, d):
        return self.base + 8 + (h * 4 + i) * 2 + side(d)

    def t2(self, h, i, d):
        return self.base + 24 + (h * 4 + i) * 2 + side(d)

    def part(self, p):
        return pl.ds(p * self.half, self.half)

    def load(self, h, da, db, part=None):
        return self.own(*self.net.at(h, da, db), h, part)[...].astype(F32)

    def a(self, h, da):
        i, net = RING.index(da), self.net
        for d in SIDES:
            p = side(d)
            src = self.own(*net.at(h, da, 2), h, p)
            self.wire.send(src, self.t2b.at[h, i, p], self.t2(h, i, d), net.dev(h, 0, d))

    def b(self, h, da, d):
        i, p, net = RING.index(da), side(d), self.net
        self.wire.recv(self.t2b.at[h, i, p], self.t2(h, i, d), net.dev(h, 0, -d))
        added = self.load(h, da, d, p) + self.t2b[h, i, p].astype(F32)
        self.t1s[h, i, p, self.part(p)] = added.astype(BF16)
        self.t1s[h, i, p, self.part(1 - p)] = self.load(h, da, d, 1 - p).astype(BF16)
        self.wire.send(self.t1s.at[h, i, p], self.t1b.at[h, i, p], self.t1(h, i, d), net.dev(h, 0, d))

    def c(self, h, da):
        i, net = RING.index(da), self.net
        for d in SIDES:
            self.wire.recv(self.t1b.at[h, i, side(d)], self.t1(h, i, d), net.dev(h, 0, -d))
        total = self.load(h, da, 0) + self.t1b[h, i, 0].astype(F32) + self.t1b[h, i, 1].astype(F32)
        if da != 2:
            self.row_sum[h, i] = total
            return
        self.s2s[h] = total.astype(BF16)
        for d in SIDES:
            p = side(d)
            self.wire.send(self.s2s.at[h, self.part(p)], self.s2b.at[h, p], self.s2(h, d), net.dev(h, d, 0))

    def d(self, h, d):
        i, p, net = RING.index(d), side(d), self.net
        self.wire.recv(self.s2b.at[h, p], self.s2(h, d), net.dev(h, -d, 0))
        added = self.row_sum[h, i, self.part(p)] + self.s2b[h, p].astype(F32)
        self.s1s[h, p, self.part(p)] = added.astype(BF16)
        self.s1s[h, p, self.part(1 - p)] = self.row_sum[h, i, self.part(1 - p)].astype(BF16)
        self.wire.send(self.s1s.at[h, p], self.s1b.at[h, p], self.s1(h, d), net.dev(h, d, 0))

    def e(self, h):
        for d in SIDES:
            self.wire.recv(self.s1b.at[h, side(d)], self.s1(h, d), self.net.dev(h, -d, 0))
        self.emit(h, self.row_sum[h, 0] + self.s1b[h, 0].astype(F32) + self.s1b[h, 1].astype(F32))

    def all_a(self):
        for da in self.ORDER:
            for h in (0, 1):
                self.a(h, da)

    def all_b(self):
        for da in self.ORDER:
            for h in (0, 1):
                for d in SIDES:
                    self.b(h, da, d)

    def all_c(self):
        for da in self.ORDER:
            for h in (0, 1):
                self.c(h, da)

    def all_d(self):
        for h in (0, 1):
            for d in SIDES:
                self.d(h, d)

    def all_e(self):
        for h in (0, 1):
            self.e(h)


BLOCK = 512


def spread_heads(rows_t, padded, natural):
    padded[...] = jnp.zeros_like(padded)
    for g in range(4):
        for k in range(4):
            head = 4 * g + k
            padded[g, g * 64 : g * 64 + 64, k * 128 : k * 128 + 128] = rows_t[head * 64 : head * 64 + 64]
        natural[g * 512 : g * 512 + 512] = padded[g].T


def attend_kernel(
    x_ref,
    qkv_in,
    out_in,
    cot_ref,
    cos_ref,
    sin_ref,
    gp_ref,
    block_ref,
    parts_o,
    qkv_hbm,
    qkv_own,
    proj,
    kv_in,
    kv_ref,
    out_full,
    kvg_ref,
    terms,
    qt,
    qn,
    dot_,
    don,
    probs,
    peaks,
    peak,
    total,
    acc,
    dqt,
    dots,
    att_t,
    do_sib,
    sib_o,
    sum_o,
    far_out,
    far_in,
    send_sems,
    recv_sems,
    local_sems,
    *bufs,
):
    net = Net()
    wire = Wire(send_sems, recv_sems, (sum_o, None), net.sibling())
    s, x, zh, core = net.s, net.x, net.zh, net.core
    other = 1 - zh

    def kv_place(ref, group):
        def piece(gx, gy, h, part):
            row = (group * 16 + gx * 4 + gy) * 128 + h * 64
            if part is None:
                return ref.at[pl.ds(pl.multiple_of(row, 32), 64)]
            return ref.at[pl.ds(pl.multiple_of(row + part * 32, 32), 32)]

        return piece

    def kv_rows(shard):
        return kv_ref.at[pl.ds(pl.multiple_of(shard * 128, 128), 128)]

    far_shard = lax.rem(s + 16, 32)
    half_cols = pl.ds(pl.multiple_of(core * 1024, 128), 1024)
    panels = pl.ds(core * 3, 3)

    def qkv_at(which, row, count):
        return probs.at[which, row // 512, pl.ds(pl.multiple_of(lax.rem(row, 512), 16), count)]

    def qkv_place(group):
        def piece(gx, gy, h, part):
            row = (group * 16 + gx * 4 + gy) * 64 + h * 32
            return qkv_at(panels, row, 32) if part is None else qkv_at(panels, row + part * 16, 16)

        return piece

    def qkv_half(group, which):
        return probs.at[pl.ds(which * 3, 3), pl.ds(group * 2, 2)]

    def out_cols(h):
        return pl.ds(pl.multiple_of(core * 1024 + h * 512, 128), 512)

    def out_place(group):
        def piece(gx, gy, h, part):
            row = (group * 16 + gx * 4 + gy) * 32
            if part is None:
                return out_full.at[pl.ds(pl.multiple_of(row, 16), 32), out_cols(h)]
            return out_full.at[pl.ds(pl.multiple_of(row + part * 16, 16), 16), out_cols(h)]

        return piece

    def out_half(group, which):
        columns = pl.ds(pl.multiple_of(which * 1024, 128), 1024)
        return out_full.at[pl.ds(pl.multiple_of(group * 512, 32), 512), columns]

    def out_rows(shard):
        return out_full.at[pl.ds(pl.multiple_of(shard * 32, 32), 32), half_cols]

    for p in range(6):
        qkv_own[p] = qkv_in[:, p * 256 : p * 256 + 256]
    greet(net.xy_neighbours() + [net.sibling(), net.partner()])

    zq = wire.new(1)
    wire.send(qkv_own.at[panels], qkv_at(panels, s * 64, 64), zq, net.partner())
    near_q = gather_stages(net, wire, lambda h: qkv_own.at[panels, pl.ds(h * 32, 32)], qkv_place(zh))
    near_q[0]()
    probs[panels, (s * 64) // 512, pl.ds(pl.multiple_of(lax.rem(s * 64, 512), 64), 64)] = qkv_own[panels]
    out_full[pl.ds(pl.multiple_of(s * 32, 32), 32), half_cols] = out_in[:, half_cols]
    peak[...] = jnp.full_like(peak, NEG_FILL)
    total[...] = jnp.zeros_like(total)
    acc[...] = jnp.zeros_like(acc)
    dqt[...] = jnp.zeros_like(dqt)
    for stage in near_q[1:6]:
        stage()
    wire.recv(qkv_at(panels, far_shard * 64, 64), zq, net.partner())
    zo = wire.new(1)
    wire.send(out_in.at[:, half_cols], out_rows(s), zo, net.partner())
    far_qp = qkv_place(other)
    far_q = gather_stages(net, wire, lambda h: far_qp(net.x, net.y, h, None), far_qp)
    far_q[0]()
    near_q[6]()
    share_q = wire.new(2)
    wire.send(qkv_half(zh, core), qkv_half(zh, core), share_q, net.sibling())
    for stage in far_q[1:3]:
        stage()

    def project(group, first):
        def step(p, carry):
            columns = pl.ds(pl.multiple_of(p * 256, 256), 256)
            result = jnp.zeros((128, 256), F32) if first else proj[:, columns]
            for b in (0, 1):
                rows = pl.ds(pl.multiple_of(group * 1024 + b * 512, 512), 512)
                result = result + jnp.dot(x_ref[:, rows], probs[p, group * 2 + b], preferred_element_type=F32)
            proj[:, columns] = result
            return carry

        lax.fori_loop(0, 6, step, 0)

    for stage in far_q[3:5]:
        stage()
    wire.recv(qkv_half(zh, 1 - core), share_q, net.sibling())
    project(zh, True)
    for stage in far_q[5:]:
        stage()
    wire.send(qkv_half(other, core), qkv_half(other, core), share_q + 1, net.sibling())
    early = wire.taken()
    near_o = gather_stages(net, wire, lambda h: out_in.at[:, out_cols(h)], out_place(zh))
    near_o[0]()
    wire.recv(qkv_half(other, 1 - core), share_q + 1, net.sibling())
    keep = []
    for p in range(6):
        for b in range(4):
            place = qkv_hbm.at[pl.ds(b * 512, 512), pl.ds(p * 256, 256)]
            keep.append(pltpu.make_async_copy(probs.at[p, b], place, local_sems.at[p * 4 + b]))
    for made in keep:
        made.start()
    project(other, False)
    cos, sin = cos_ref[...], sin_ref[...]

    def turn(rows_t):
        a, b = rows_t[0:32], rows_t[32:64]
        return [a * cos - b * sin, b * cos + a * sin]

    for c in (0, 1):
        keys_t = proj[:, 1024 + c * 128 : 1152 + c * 128].T
        pair = turn(keys_t[0:64]) + turn(keys_t[64:128])
        kv_in[:, c * 128 : c * 128 + 128] = jnp.concatenate(pair, axis=0).astype(BF16).T
    kv_in[:, 256:512] = proj[:, 1280:1536].astype(BF16)

    zkey = wire.new(1)
    wire.send(kv_in, kv_rows(s), zkey, net.partner())
    near = gather_stages(net, wire, lambda h: kv_in.at[pl.ds(h * 64, 64)], kv_place(kv_ref, zh))
    near[0]()
    near_o[1]()
    kv_ref[pl.ds(pl.multiple_of(s * 128, 128), 128)] = kv_in[...]
    pieces = []
    for c in range(8):
        queries_t = proj[:, c * 128 : c * 128 + 128].T
        pieces += turn(queries_t[0:64]) + turn(queries_t[64:128])
    spread_heads((jnp.concatenate(pieces, axis=0).astype(BF16).astype(F32) * 0.125).astype(BF16), qt, qn)
    near[1]()
    near_o[2]()
    near[2]()
    near_o[3]()
    near[3]()
    near[4]()
    near_o[4]()
    near[5]()
    near_o[5]()
    wire.recv(kv_rows(far_shard), zkey, net.partner())
    far_place = kv_place(kv_ref, other)
    far = gather_stages(net, wire, lambda h: far_place(net.x, net.y, h, None), far_place)
    far[0]()
    wire.recv(out_rows(far_shard), zo, net.partner())
    far_op = out_place(other)
    far_o = gather_stages(net, wire, lambda h: far_op(net.x, net.y, h, None), far_op)
    far_o[0]()
    near[6]()
    near_o[6]()
    share_o = wire.new(2)
    wire.send(out_half(zh, core), out_half(zh, core), share_o, net.sibling())
    for made in keep:
        made.wait()
    wire.drain(early)

    def rows_of(j):
        return pl.ds(pl.multiple_of(j * BLOCK, BLOCK), BLOCK)

    def forward(j, masked):
        keys = kv_ref[rows_of(j), 0:256]
        values_t = kv_ref[rows_of(j), 256:512].T
        if masked:
            key_at = lax.broadcasted_iota(jnp.int32, (BLOCK, 512), 0) + j * BLOCK
            query_at = lax.rem(lax.broadcasted_iota(jnp.int32, (BLOCK, 512), 1), 128) + s * 128
            visible = key_at <= query_at
        ahead = jnp.dot(keys, qt[0], preferred_element_type=F32)
        for g in range(4):
            scores = ahead
            if g < 3:
                ahead = jnp.dot(keys, qt[g + 1], preferred_element_type=F32)
            if masked:
                scores = jnp.where(visible, scores, NEG_FILL)
            before = peak[g]
            now = jnp.maximum(before, jnp.max(scores, axis=0, keepdims=True))
            fade = jnp.exp(before - now)
            e = jnp.exp(scores - now)
            total[g] = total[g] * fade + jnp.sum(e, axis=0, keepdims=True)
            e = e.astype(BF16)
            for c in (0, 1):
                probs[4 * g + j // 2, lax.rem(j, 2) * 2 + c] = e[:, c * 256 : c * 256 + 256]
            peaks[g, j] = now
            peak[g] = now
            acc[g] = acc[g] * fade + jnp.dot(values_t[g * 64 : g * 64 + 64], e, preferred_element_type=F32)

    def in_turn(plans, i):
        for k, plan in enumerate(plans):

            @pl.when(i == k)
            def _():
                for stage in plan:
                    stage()

    def near_forward(i, carry):
        in_turn([[far[1], far_o[1]], [far[2], far_o[2]], [far[3], far_o[3]], [far[4], far_o[4]]], i)

        @pl.when(i < x)
        def _():
            forward(zh * 4 + i, False)

        @pl.when(i == x)
        def _():
            forward(zh * 4 + i, True)

        return carry

    lax.fori_loop(0, 4, near_forward, 0)
    far[5]()
    far_o[5]()

    def landed(h, da, d):
        key = far.base + 24 + (h * 4 + RING.index(da)) * 2 + side(d)
        wire.recv(far_place(*net.at(h, da, 2), h, side(d)), key, net.dev(h, 0, -d))

    def far_forward(i, carry):
        for k, da in enumerate((0, 1, -1, 2)):

            @pl.when(i == k)
            def _(da=da):
                for d in SIDES:
                    landed(0, da, d)
                if da == 2:
                    for db in RING:
                        for d in SIDES:
                            landed(1, db, d)

        @pl.when(zh == 1)
        def _():
            forward(lax.rem(x + lax.rem(8 + i - 3 * ((i * (i - 1)) // 2) + 4 * i, 4), 4), False)

        return carry

    lax.fori_loop(0, 4, far_forward, 0)
    far_o[6]()
    wire.send(out_half(other, core), out_half(other, core), share_o + 1, net.sibling())

    for g in range(4):
        attended = (acc[g] / total[g]).astype(BF16)
        for k in range(4):
            head = 4 * g + k
            att_t[head * 64 : head * 64 + 64] = attended[:, k * 128 : k * 128 + 128]
    core_key = wire.new(2)
    for g in (0, 1):
        rows = slice(g * 512, g * 512 + 512)
        sib_cols = pl.ds(pl.multiple_of((1 - core) * 1024, 128), 1024)
        do_sib[rows] = jnp.dot(att_t[rows], cot_ref[:, sib_cols], preferred_element_type=F32).astype(BF16)
        wire.send(do_sib.at[pl.ds(g * 512, 512)], sib_o.at[pl.ds(g * 512, 512)], core_key + g, net.sibling())
    wire.recv(out_half(zh, 1 - core), share_o, net.sibling())
    wire.recv(out_half(other, 1 - core), share_o + 1, net.sibling())
    grad_t = lax.dot_general(
        out_full[...], cot_ref[...], (((1,), (1,)), ((), ())), preferred_element_type=F32
    ).astype(BF16)
    spread_heads(grad_t, dot_, don)
    for g in range(4):
        for k in range(4):
            head = 4 * g + k
            rows = slice(head * 64, head * 64 + 64)
            both = att_t[rows].astype(F32) * dot_[g, g * 64 : g * 64 + 64, k * 128 : k * 128 + 128].astype(F32)
            dots[g, :, k * 128 : k * 128 + 128] = jnp.sum(both, axis=0, keepdims=True)
        peak[g] = peak[g] + jnp.log(total[g])

    def out_own(group):
        def piece(gx, gy, h, part):
            row = (group * 16 + gx * 4 + gy) * 32
            if part is None:
                return sum_o.at[pl.ds(pl.multiple_of(row, 16), 32), pl.ds(h * 512, 512)]
            return sum_o.at[pl.ds(pl.multiple_of(row + part * 16, 16), 16), pl.ds(h * 512, 512)]

        return piece

    def out_emit(group):
        def emit(h, result):
            for part in (0, 1):
                parts_o[group, 2 * h + part] = result[:, part * 256 : part * 256 + 256]

        return emit

    scat_o = [Scatter(net, wire, out_own(g), bufs[16 + 8 * g : 24 + 8 * g], out_emit(g)) for g in (0, 1)]

    def add_cores(g):
        def run():
            rows = slice(g * 512, g * 512 + 512)
            wire.recv(sib_o.at[pl.ds(g * 512, 512)], core_key + g, net.sibling())
            own = jnp.dot(att_t[rows], cot_ref[:, half_cols], preferred_element_type=F32)
            sum_o[rows] = (own + sib_o[rows].astype(F32)).astype(BF16)
            scat_o[g].all_a()

        return run

    def backward(j):
        keys_t = kv_ref[rows_of(j), 0:256].T
        values = kv_ref[rows_of(j), 256:512]
        ahead = jnp.dot(values, dot_[0], preferred_element_type=F32)
        dk = dv = None
        for g in range(4):
            grads = ahead
            if g < 3:
                ahead = jnp.dot(values, dot_[g + 1], preferred_element_type=F32)
            e = jnp.concatenate([probs[4 * g + j // 2, lax.rem(j, 2) * 2 + c] for c in (0, 1)], axis=1)
            p = e.astype(F32) * jnp.exp(peaks[g, j] - peak[g])
            ds = (p * (grads - dots[g])).astype(BF16)
            p = p.astype(BF16)
            dqt[g] += jnp.dot(keys_t[g * 64 : g * 64 + 64], ds, preferred_element_type=F32)
            rows = slice(g * 512, g * 512 + 512)
            dk_g = jnp.dot(ds, qn[rows], preferred_element_type=F32)
            dv_g = jnp.dot(p, don[rows], preferred_element_type=F32)
            dk = dk_g if g == 0 else dk + dk_g
            dv = dv_g if g == 0 else dv + dv_g
        terms[rows_of(j), 0:256] = dk.astype(BF16)
        terms[rows_of(j), 256:512] = dv.astype(BF16)

    zback = wire.new(2)

    def emit_far(h, result):
        far_out[h] = result.astype(BF16)
        wire.send(far_out.at[h], far_in.at[h], zback + h, net.partner())

    def emit_near(h, result):
        kvg_ref[pl.ds(h * 64, 64)] = result

    scat_far = Scatter(net, wire, kv_place(terms, other), bufs[0:8], emit_far)
    scat_near = Scatter(net, wire, kv_place(terms, zh), bufs[8:16], emit_near)

    def after(scat):
        one = functools.partial

        def plan0():
            scat.a(0, 2)
            for da in scat.ORDER:
                scat.a(1, da)

        def plan1():
            scat.a(0, 1)
            for da in scat.ORDER:
                scat.b(1, da, 1)
            for d in SIDES:
                scat.b(0, 2, d)

        def plan2():
            scat.a(0, -1)
            for da in scat.ORDER:
                scat.b(1, da, -1)
            for d in SIDES:
                scat.b(0, 1, d)
            scat.c(0, 2)

        def plan3():
            scat.a(0, 0)
            for d in SIDES:
                scat.b(0, -1, d)
            scat.c(1, 2)
            scat.c(0, 1)

        return [[plan0], [plan1], [plan2], [plan3]]

    def late1(scat):
        def run():
            for d in SIDES:
                scat.b(0, 0, d)
            for da in (1, -1, 0):
                scat.c(1, da)
            scat.c(0, -1)

        return run

    def late2(scat):
        def run():
            scat.c(0, 0)
            scat.all_d()

        return run

    def block_loop(group, plans):
        def step(i, carry):
            turn = lax.rem(18 - i + 3 * ((i * (i - 1)) // 2), 4)
            j = group * 4 + lax.rem(x + turn, 4)

            @pl.when(j <= s // 4)
            def _():
                backward(j)

            @pl.when(j > s // 4)
            def _():
                terms[rows_of(j)] = jnp.zeros((BLOCK, 512), BF16)

            in_turn(plans, i)
            return carry

        lax.fori_loop(0, 4, step, 0)

    plans = after(scat_far)
    plans[1].append(add_cores(0))
    plans[2].append(add_cores(1))
    plans[3].append(scat_o[0].all_b)
    block_loop(other, plans)
    plans = after(scat_near)
    plans[0] = [late1(scat_far)] + plans[0] + [scat_o[1].all_b]
    plans[1] = [late2(scat_far)] + plans[1] + [scat_o[0].all_c]
    plans[2] = [scat_far.all_e] + plans[2] + [scat_o[1].all_c, scat_o[0].all_d]
    plans[3] = plans[3] + [scat_o[1].all_d, scat_o[0].all_e]
    block_loop(zh, plans)
    late1(scat_near)()
    attended = att_t[...].T
    for c in range(4):
        cols = slice(c * 512, c * 512 + 512)
        block_ref[:, cols] = jnp.dot(attended, out_full[:, cols], preferred_element_type=F32).astype(BF16)
    late2(scat_near)()
    def turn_back(rows_t):
        a, b = rows_t[0:32], rows_t[32:64]
        return jnp.concatenate([a * cos + b * sin, b * cos - a * sin], axis=0)

    for g in range(4):
        for k in range(0, 4, 2):
            head = 4 * g + k
            pair = [turn_back(dqt[g, :, c * 128 : c * 128 + 128] * 0.125) for c in (k, k + 1)]
            gp_ref[:, head * 64 : head * 64 + 128] = jnp.concatenate(pair, axis=0).T.astype(BF16)
    scat_o[1].all_e()
    scat_near.all_e()
    for h in (0, 1):
        wire.recv(far_in.at[h], zback + h, net.partner())
        kvg_ref[pl.ds(h * 64, 64)] += far_in[h].astype(F32)
    for c in range(2):
        keys_t = kvg_ref[:, c * 128 : c * 128 + 128].T
        pair = [turn_back(keys_t[0:64]), turn_back(keys_t[64:128])]
        gp_ref[:, 1024 + c * 128 : 1152 + c * 128] = jnp.concatenate(pair, axis=0).T.astype(BF16)
    gp_ref[:, 1280:1536] = kvg_ref[:, 256:512].astype(BF16)
    wire.drain()


def attend(inputs, qkv_weight, out_weight, cotangent, cos_t, sin_t):
    keys = 10 * AG_KEYS + 11
    return pl.pallas_call(
        attend_kernel,
        out_shape=(
            jax.ShapeDtypeStruct((128, 1536), BF16),
            jax.ShapeDtypeStruct((128, 2048), BF16),
            jax.ShapeDtypeStruct((2, 4, 32, 256), F32),
            jax.ShapeDtypeStruct((2048, 1536), BF16),
        ),
        in_specs=[pl.BlockSpec(memory_space=pltpu.VMEM)] * 6,
        out_specs=[pl.BlockSpec(memory_space=pltpu.VMEM)] * 3 + [pl.BlockSpec(memory_space=pl.ANY)],
        scratch_shapes=[
            pltpu.VMEM((6, 64, 256), BF16),
            pltpu.VMEM((128, 1536), F32),
            pltpu.VMEM((128, 512), BF16),
            pltpu.VMEM((4096, 512), BF16),
            pltpu.VMEM((1024, 2048), BF16),
            pltpu.VMEM((128, 512), F32),
            pltpu.VMEM((4096, 512), BF16),
            pltpu.VMEM((4, 256, 512), BF16),
            pltpu.VMEM((2048, 256), BF16),
            pltpu.VMEM((4, 256, 512), BF16),
            pltpu.VMEM((2048, 256), BF16),
            pltpu.VMEM((16, 4, BLOCK, 256), BF16),
            pltpu.VMEM((4, 8, 1, 512), F32),
            pltpu.VMEM((4, 1, 512), F32),
            pltpu.VMEM((4, 1, 512), F32),
            pltpu.VMEM((4, 64, 512), F32),
            pltpu.VMEM((4, 64, 512), F32),
            pltpu.VMEM((4, 1, 512), F32),
            pltpu.VMEM((1024, 128), BF16),
            pltpu.VMEM((1024, 1024), BF16),
            pltpu.VMEM((1024, 1024), BF16),
            pltpu.VMEM((1024, 1024), BF16),
            pltpu.VMEM((2, 64, 512), BF16),
            pltpu.VMEM((2, 64, 512), BF16),
            pltpu.SemaphoreType.DMA((keys,)),
            pltpu.SemaphoreType.DMA((keys,)),
            pltpu.SemaphoreType.DMA((24,)),
            *scatter_scratch(64, 512),
            *scatter_scratch(64, 512),
            *scatter_scratch(32, 512),
            *scatter_scratch(32, 512),
        ],
        compiler_params=pltpu.CompilerParams(
            collective_id=0, has_side_effects=True, vmem_limit_bytes=VMEM_BYTES
        ),
        name="attend",
    )(inputs, qkv_weight, out_weight, cotangent, cos_t, sin_t)


def weight_grad_kernel(
    scale,
    x_ref,
    gp_ref,
    w_ref,
    parts_o,
    tg_ref,
    out_q,
    out_o,
    xt,
    do_sib,
    sib_q,
    sum_q,
    zs_q,
    zs_o,
    zr_q,
    zr_o,
    keep_q,
    fin_q,
    fin_o,
    got_q,
    got_o,
    canvas,
    send_sems,
    recv_sems,
    *bufs,
):
    net = Net()
    wire = Wire(send_sems, recv_sems, (canvas, None), net.sibling())
    core = net.core
    cols_q = [pl.ds(pl.multiple_of(c * 768, 128), 768) for c in (core, 1 - core)]
    cols_o = [pl.ds(pl.multiple_of(c * 1024, 128), 1024) for c in (core, 1 - core)]
    greet(net.xy_neighbours() + [net.sibling()] + [net.up(k) for k in range(1, 8)])

    z1 = wire.new(14)

    def z_send(k, staged, slots, key):
        target = lax.rem(net.z + k, 8)
        wire.send(staged.at[target // 4, lax.rem(target, 4)], slots.at[k - 1], key + k - 1, net.up(k))

    for g in (0, 1):
        for l in range(4):
            zs_o[g, l] = parts_o[g, l].astype(BF16)
    for k in range(1, 8):
        z_send(k, zs_o, zr_o, z1)

    xt[...] = x_ref[...].T
    ckey = wire.new(2)

    def product(rows, cols):
        return jnp.dot(xt[rows], gp_ref[:, cols], preferred_element_type=F32)

    def make_sibling(g):
        def step(i, carry):
            rows = pl.ds(pl.multiple_of(g * 1024 + i * 256, 256), 256)
            do_sib[rows] = product(rows, cols_q[1]).astype(BF16)
            return carry

        lax.fori_loop(0, 4, step, 0)
        rows = pl.ds(g * 1024, 1024)
        wire.send(do_sib.at[rows], sib_q.at[rows], ckey + g, net.sibling())

    def add_cores(g):
        wire.recv(sib_q.at[pl.ds(g * 1024, 1024)], ckey + g, net.sibling())

        def step(i, carry):
            rows = pl.ds(pl.multiple_of(g * 1024 + i * 256, 256), 256)
            sum_q[rows] = (product(rows, cols_q[0]) + sib_q[rows].astype(F32)).astype(BF16)
            return carry

        lax.fori_loop(0, 4, step, 0)

    def own_q(g):
        def piece(gx, gy, h, part):
            row = (g * 16 + gx * 4 + gy) * 64 + h * 32
            if part is None:
                return sum_q.at[pl.ds(pl.multiple_of(row, 16), 32)]
            return sum_q.at[pl.ds(pl.multiple_of(row + part * 16, 16), 16)]

        return piece

    def emit_q(g):
        def emit(h, result):
            for part in (0, 1):
                rows = result[part * 16 : part * 16 + 16]
                keep_q[g, 2 * h + part] = rows
                zs_q[g, 2 * h + part] = rows.astype(BF16)

        return emit

    runs = [Scatter(net, wire, own_q(g), bufs[8 * g : 8 * g + 8], emit_q(g)) for g in (0, 1)]

    def tokens_grad(c):
        rows = slice(c * 512, c * 512 + 512)
        tg_ref[:, rows] = lax.dot_general(
            gp_ref[...], w_ref[rows], (((1,), (1,)), ((), ())), preferred_element_type=F32
        ).astype(BF16)

    make_sibling(0)
    make_sibling(1)
    add_cores(0)
    runs[0].all_a()
    add_cores(1)
    runs[1].all_a()
    tokens_grad(0)
    runs[0].all_b()
    runs[1].all_b()
    tokens_grad(1)
    runs[0].all_c()
    runs[1].all_c()
    tokens_grad(2)
    runs[0].all_d()
    runs[1].all_d()
    tokens_grad(3)
    runs[0].all_e()
    runs[1].all_e()

    z1q = z1 + 7
    for k in range(1, 8):
        z_send(k, zs_q, zr_q, z1q)

    def place(l):
        return (
            got_q.at[pl.ds(pl.multiple_of(l * 16, 16), 16), cols_q[0]],
            got_o.at[:, pl.ds(pl.multiple_of(core * 1024 + l * 256, 128), 256)],
        )

    def level(k):
        l = lax.rem(net.zl + k, 4)
        return l, (net.s, l * 2 + core)

    z2 = wire.new(6)
    mine = place(net.zl)

    def z_sum(first, slots, key):
        result = first
        for k in range(1, 8):
            wire.recv(slots.at[k - 1], key + k - 1, net.up(8 - k))
            result = result + slots[k - 1].astype(F32)
        return (result * scale).astype(BF16)

    def z_spread(which, ref, key):
        for k in (1, 2, 3):
            wire.send(ref, mine[which], key + k - 1, level(k)[1])

    fin_o[...] = z_sum(parts_o[net.zh, net.zl], zr_o, z1)
    z_spread(1, fin_o, z2)
    got_o[:, pl.ds(pl.multiple_of(core * 1024 + net.zl * 256, 128), 256)] = fin_o[...]
    fin_q[...] = z_sum(keep_q[net.zh, net.zl], zr_q, z1q)
    z_spread(0, fin_q, z2 + 3)
    got_q[pl.ds(pl.multiple_of(net.zl * 16, 16), 16), cols_q[0]] = fin_q[...]
    last = wire.new(2)
    for k in (1, 2, 3):
        l, device = level(4 - k)
        wire.recv(place(l)[1], z2 + k - 1, device)
    wire.send(got_o.at[:, cols_o[0]], got_o.at[:, cols_o[0]], last, net.sibling())
    for k in (1, 2, 3):
        l, device = level(4 - k)
        wire.recv(place(l)[0], z2 + 3 + k - 1, device)
    wire.send(got_q.at[:, cols_q[0]], got_q.at[:, cols_q[0]], last + 1, net.sibling())
    wire.recv(got_o.at[:, cols_o[1]], last, net.sibling())
    wire.recv(got_q.at[:, cols_q[1]], last + 1, net.sibling())
    out_o[...] = got_o[...].astype(F32)
    out_q[...] = got_q[...].astype(F32)
    wire.drain()


def weight_grads(inputs, grad_proj, qkv_full, parts_o, scale):
    keys = 2 * AG_KEYS + 14 + 2 + 6 + 2
    return pl.pallas_call(
        functools.partial(weight_grad_kernel, scale),
        out_shape=(
            jax.ShapeDtypeStruct((128, 2048), BF16),
            jax.ShapeDtypeStruct((64, 1536), F32),
            jax.ShapeDtypeStruct((32, 2048), F32),
        ),
        in_specs=[pl.BlockSpec(memory_space=pltpu.VMEM)] * 4,
        out_specs=[pl.BlockSpec(memory_space=pltpu.VMEM)] * 3,
        scratch_shapes=[
            pltpu.VMEM((2048, 128), BF16),
            pltpu.VMEM((2048, 768), BF16),
            pltpu.VMEM((2048, 768), BF16),
            pltpu.VMEM((2048, 768), BF16),
            pltpu.VMEM((2, 4, 16, 768), BF16),
            pltpu.VMEM((2, 4, 32, 256), BF16),
            pltpu.VMEM((7, 16, 768), BF16),
            pltpu.VMEM((7, 32, 256), BF16),
            pltpu.VMEM((2, 4, 16, 768), F32),
            pltpu.VMEM((16, 768), BF16),
            pltpu.VMEM((32, 256), BF16),
            pltpu.VMEM((64, 1536), BF16),
            pltpu.VMEM((32, 2048), BF16),
            pltpu.VMEM((1024, 1024), BF16),
            pltpu.SemaphoreType.DMA((keys,)),
            pltpu.SemaphoreType.DMA((keys,)),
            *scatter_scratch(32, 768),
            *scatter_scratch(32, 768),
        ],
        compiler_params=pltpu.CompilerParams(
            collective_id=2, has_side_effects=True, vmem_limit_bytes=VMEM_BYTES
        ),
        name="weight_grads",
    )(inputs, grad_proj, qkv_full, parts_o)


def finish_kernel(*refs):
    for i in range(4):
        refs[i + 4][...] = refs[i][...]


def finish(*results):
    return pl.pallas_call(
        finish_kernel,
        out_shape=tuple(jax.ShapeDtypeStruct(r.shape, r.dtype) for r in results),
        in_specs=[pl.BlockSpec(memory_space=pltpu.VMEM)] * 4,
        out_specs=[pl.BlockSpec(memory_space=pltpu.VMEM)] * 4,
        name="finish",
    )(*results)


def tables(positions, head_size):
    halves = head_size // 2
    frequency = ROPE_BASE ** (-(jnp.arange(halves, dtype=jnp.float32) * 2.0) / head_size)
    angles = positions.astype(jnp.float32)[:, None] * frequency[None, :]
    return (jnp.cos(angles), jnp.sin(angles))


def rotate(matrix, cos_rows, sin_rows, head_count):
    row_count = matrix.shape[0]
    head_size = matrix.shape[1] // head_count
    halves = head_size // 2
    pieces = matrix.reshape(row_count, head_count, 2, halves)
    lower_half = pieces[:, :, 0]
    upper_half = pieces[:, :, 1]
    cos_part = cos_rows[:, None, :]
    sin_part = sin_rows[:, None, :]
    turned = jnp.stack(
        [
            lower_half * cos_part - upper_half * sin_part,
            upper_half * cos_part + lower_half * sin_part,
        ],
        axis=2,
    )
    return turned.reshape(row_count, head_count * head_size)


def body(tokens, qkv_weight, out_weight, cotangent):
    inputs = tokens[0]
    tok_count = inputs.shape[0]
    positions = lax.axis_index("shard") * tok_count + jnp.arange(tok_count, dtype=jnp.int32)
    cosine, sine = tables(positions, HEAD_DIM)
    grad_proj, block_output, parts_o, qkv_full = attend(
        inputs, qkv_weight, out_weight, cotangent[0], cosine.T, sine.T
    )
    norm_factor = 1.0 / math.sqrt(lax.axis_size("rep") * lax.axis_size("shard") * tok_count)
    tokens_grad, qkv_grad, out_grad = weight_grads(inputs, grad_proj, qkv_full, parts_o, norm_factor)
    block_output, tokens_grad, qkv_grad, out_grad = finish(block_output, tokens_grad, qkv_grad, out_grad)
    return (block_output[None], tokens_grad[None], qkv_grad, out_grad)


def solution(mesh):
    return jax.shard_map(
        body,
        mesh=mesh,
        in_specs=(
            P("rep", "shard", None),
            P("shard", None),
            P("shard", None),
            P("rep", "shard", None),
        ),
        out_specs=(
            P("rep", "shard", None),
            P("rep", "shard", None),
            P("shard", None),
            P("shard", None),
        ),
        check_vma=False,
    )
```

```python
import functools
import math

import jax
import jax.numpy as jnp
from jax import lax
from jax.experimental import pallas as pl
from jax.experimental.pallas import tpu as pltpu
from jax.sharding import PartitionSpec as P

HEADS = 16
KV_HEADS = 4
HEAD_DIM = 64

ROPE_BASE = 500000.0
NEG_FILL = -1e30
MESH = pl.DeviceIdType.MESH
BF16 = jnp.bfloat16
F32 = jnp.float32
VMEM_BYTES = 62 * 1024 * 1024


class Net:
    def __init__(self):
        self.s = lax.axis_index("shard")
        self.r = lax.axis_index("rep")
        self.zh = self.s // 16
        self.x = lax.rem(self.s // 4, 4)
        self.y = lax.rem(self.s, 4)
        self.zl = self.r // 2
        self.core = lax.rem(self.r, 2)
        self.z = self.zh * 4 + self.zl

    def at(self, h, da, db):
        dx, dy = (da, db) if h == 0 else (db, da)
        return lax.rem(self.x + (dx + 4), 4), lax.rem(self.y + (dy + 4), 4)

    def dev(self, h, da, db):
        gx, gy = self.at(h, da, db)
        return (self.zh * 16 + gx * 4 + gy, self.r)

    def sibling(self):
        return (self.s, self.zl * 2 + 1 - self.core)

    def partner(self):
        return (lax.rem(self.s + 16, 32), self.r)

    def up(self, k):
        z = lax.rem(self.z + k, 8)
        return ((z // 4) * 16 + self.x * 4 + self.y, lax.rem(z, 4) * 2 + self.core)

    def xy_neighbours(self):
        return [self.dev(0, 1, 0), self.dev(0, -1, 0), self.dev(0, 0, 1), self.dev(0, 0, -1)]


def greet(devices):
    barrier = pltpu.get_barrier_semaphore()
    for device in devices:
        pl.semaphore_signal(barrier, inc=1, device_id=device, device_id_type=MESH)
    pl.semaphore_wait(barrier, len(devices))


class Wire:
    def __init__(self, send_sems, recv_sems, canvas, device):
        self.send_sems, self.recv_sems = send_sems, recv_sems
        self.canvas, self.device = canvas, device
        self.used = 0
        self.sent = []

    def new(self, count=1):
        first = self.used
        self.used += count
        return first

    def copy(self, src, dst, key, device):
        return pltpu.make_async_remote_copy(
            src_ref=src,
            dst_ref=dst,
            send_sem=self.send_sems.at[key],
            recv_sem=self.recv_sems.at[key],
            device_id=device,
            device_id_type=MESH,
        )

    def send(self, src, dst, key, device):
        self.copy(src, dst, key, device).start()
        self.sent.append((src.shape, src.dtype, key))

    def recv(self, ref, key, device):
        self.copy(ref, ref, key, device).wait_recv()

    def taken(self):
        sent, self.sent = self.sent, []
        return sent

    def drain(self, sent=None):
        for shape, dtype, key in self.taken() if sent is None else sent:
            cols = shape[1] if len(shape) == 2 else 1024 if len(shape) == 4 else 256
            rows = math.prod(shape) // cols
            ref = self.canvas[dtype == F32].at[pl.ds(0, rows), pl.ds(0, cols)]
            self.copy(ref, ref, key, self.device).wait_send()


SIDES = (1, -1)
RING = (0, 1, -1, 2)
AG_KEYS = 40


def side(d):
    return 0 if d == 1 else 1


class Stages(list):
    def __init__(self, base, stages):
        super().__init__(stages)
        self.base = base


def gather_stages(net, wire, own, piece):
    base = wire.new(AG_KEYS)

    def s1(h, d):
        return base + h * 2 + side(d)

    def s2(h, d):
        return base + 4 + h * 2 + side(d)

    def t1(h, da, d):
        return base + 8 + (h * 4 + RING.index(da)) * 2 + side(d)

    def t2(h, da, d):
        return base + 24 + (h * 4 + RING.index(da)) * 2 + side(d)

    def at(h, da, db, part=None):
        return piece(*net.at(h, da, db), h, part)

    def spread(h, da, src):
        for d in SIDES:
            wire.send(src, at(h, da, 0), t1(h, da, d), net.dev(h, 0, d))

    def pass_on(h, da):
        for d in SIDES:
            wire.recv(at(h, da, -d), t1(h, da, d), net.dev(h, 0, -d))
            part = side(d)
            wire.send(at(h, da, -d, part), at(h, da, -d, part), t2(h, da, d), net.dev(h, 0, d))

    def stage_a():
        for h in (0, 1):
            for d in SIDES:
                wire.send(own(h), at(h, 0, 0), s1(h, d), net.dev(h, d, 0))
        for h in (0, 1):
            spread(h, 0, own(h))

    def stage_b():
        for d in SIDES:
            for h in (0, 1):
                wire.recv(at(h, -d, 0), s1(h, d), net.dev(h, -d, 0))
                part = side(d)
                wire.send(at(h, -d, 0, part), at(h, -d, 0, part), s2(h, d), net.dev(h, d, 0))
        for d in SIDES:
            for h in (0, 1):
                spread(h, -d, at(h, -d, 0))

    def stage_c():
        for h in (0, 1):
            pass_on(h, 0)

    def stage_d():
        for h in (0, 1):
            for d in SIDES:
                wire.recv(at(h, 2, 0, side(d)), s2(h, d), net.dev(h, -d, 0))
            spread(h, 2, at(h, 2, 0))

    def stage_e():
        for da in (-1, 1):
            for h in (0, 1):
                pass_on(h, da)

    def stage_f():
        for h in (0, 1):
            pass_on(h, 2)

    def stage_g():
        for da in (0, -1, 1, 2):
            for h in (0, 1):
                for d in SIDES:
                    wire.recv(at(h, da, 2, side(d)), t2(h, da, d), net.dev(h, 0, -d))

    return Stages(base, [stage_a, stage_b, stage_c, stage_d, stage_e, stage_f, stage_g])


def scatter_scratch(rows, cols):
    return [
        pltpu.VMEM((2, 4, 2, rows // 2, cols), BF16),
        pltpu.VMEM((2, 4, 2, rows, cols), BF16),
        pltpu.VMEM((2, 4, 2, rows, cols), BF16),
        pltpu.VMEM((2, 3, rows, cols), F32),
        pltpu.VMEM((2, rows, cols), BF16),
        pltpu.VMEM((2, 2, rows // 2, cols), BF16),
        pltpu.VMEM((2, 2, rows, cols), BF16),
        pltpu.VMEM((2, 2, rows, cols), BF16),
    ]


class Scatter:
    ORDER = (2, 1, -1, 0)

    def __init__(self, net, wire, own, bufs, emit):
        self.net, self.wire, self.own, self.emit = net, wire, own, emit
        self.t2b, self.t1s, self.t1b, self.row_sum, self.s2s, self.s2b, self.s1s, self.s1b = bufs
        self.rows = self.row_sum.shape[2]
        self.half = self.rows // 2
        self.base = wire.new(AG_KEYS)

    def s1(self, h, d):
        return self.base + h * 2 + side(d)

    def s2(self, h, d):
        return self.base + 4 + h * 2 + side(d)

    def t1(self, h, i, d):
        return self.base + 8 + (h * 4 + i) * 2 + side(d)

    def t2(self, h, i, d):
        return self.base + 24 + (h * 4 + i) * 2 + side(d)

    def part(self, p):
        return pl.ds(p * self.half, self.half)

    def load(self, h, da, db, part=None):
        return self.own(*self.net.at(h, da, db), h, part)[...].astype(F32)

    def a(self, h, da):
        i, net = RING.index(da), self.net
        for d in SIDES:
            p = side(d)
            src = self.own(*net.at(h, da, 2), h, p)
            self.wire.send(src, self.t2b.at[h, i, p], self.t2(h, i, d), net.dev(h, 0, d))

    def b(self, h, da, d):
        i, p, net = RING.index(da), side(d), self.net
        self.wire.recv(self.t2b.at[h, i, p], self.t2(h, i, d), net.dev(h, 0, -d))
        added = self.load(h, da, d, p) + self.t2b[h, i, p].astype(F32)
        self.t1s[h, i, p, self.part(p)] = added.astype(BF16)
        self.t1s[h, i, p, self.part(1 - p)] = self.load(h, da, d, 1 - p).astype(BF16)
        self.wire.send(self.t1s.at[h, i, p], self.t1b.at[h, i, p], self.t1(h, i, d), net.dev(h, 0, d))

    def c(self, h, da):
        i, net = RING.index(da), self.net
        for d in SIDES:
            self.wire.recv(self.t1b.at[h, i, side(d)], self.t1(h, i, d), net.dev(h, 0, -d))
        total = self.load(h, da, 0) + self.t1b[h, i, 0].astype(F32) + self.t1b[h, i, 1].astype(F32)
        if da != 2:
            self.row_sum[h, i] = total
            return
        self.s2s[h] = total.astype(BF16)
        for d in SIDES:
            p = side(d)
            self.wire.send(self.s2s.at[h, self.part(p)], self.s2b.at[h, p], self.s2(h, d), net.dev(h, d, 0))

    def d(self, h, d):
        i, p, net = RING.index(d), side(d), self.net
        self.wire.recv(self.s2b.at[h, p], self.s2(h, d), net.dev(h, -d, 0))
        added = self.row_sum[h, i, self.part(p)] + self.s2b[h, p].astype(F32)
        self.s1s[h, p, self.part(p)] = added.astype(BF16)
        self.s1s[h, p, self.part(1 - p)] = self.row_sum[h, i, self.part(1 - p)].astype(BF16)
        self.wire.send(self.s1s.at[h, p], self.s1b.at[h, p], self.s1(h, d), net.dev(h, d, 0))

    def e(self, h):
        for d in SIDES:
            self.wire.recv(self.s1b.at[h, side(d)], self.s1(h, d), self.net.dev(h, -d, 0))
        self.emit(h, self.row_sum[h, 0] + self.s1b[h, 0].astype(F32) + self.s1b[h, 1].astype(F32))

    def all_a(self):
        for da in self.ORDER:
            for h in (0, 1):
                self.a(h, da)

    def all_b(self):
        for da in self.ORDER:
            for h in (0, 1):
                for d in SIDES:
                    self.b(h, da, d)

    def all_c(self):
        for da in self.ORDER:
            for h in (0, 1):
                self.c(h, da)

    def all_d(self):
        for h in (0, 1):
            for d in SIDES:
                self.d(h, d)

    def all_e(self):
        for h in (0, 1):
            self.e(h)


BLOCK = 512


def spread_heads(rows_t, padded, natural):
    padded[...] = jnp.zeros_like(padded)
    for g in range(4):
        for k in range(4):
            head = 4 * g + k
            padded[g, g * 64 : g * 64 + 64, k * 128 : k * 128 + 128] = rows_t[head * 64 : head * 64 + 64]
        natural[g * 512 : g * 512 + 512] = padded[g].T


def attend_kernel(
    x_ref,
    qkv_in,
    out_in,
    cot_ref,
    cos_ref,
    sin_ref,
    gp_ref,
    block_ref,
    parts_o,
    qkv_hbm,
    qkv_own,
    proj,
    kv_in,
    kv_ref,
    out_full,
    kvg_ref,
    terms,
    qt,
    qn,
    dot_,
    don,
    probs,
    peaks,
    peak,
    total,
    acc,
    dqt,
    dots,
    att_t,
    do_sib,
    sib_o,
    sum_o,
    far_out,
    far_in,
    send_sems,
    recv_sems,
    local_sems,
    *bufs,
):
    net = Net()
    wire = Wire(send_sems, recv_sems, (sum_o, None), net.sibling())
    s, x, zh, core = net.s, net.x, net.zh, net.core
    other = 1 - zh

    def kv_place(ref, group):
        def piece(gx, gy, h, part):
            row = (group * 16 + gx * 4 + gy) * 128 + h * 64
            if part is None:
                return ref.at[pl.ds(pl.multiple_of(row, 32), 64)]
            return ref.at[pl.ds(pl.multiple_of(row + part * 32, 32), 32)]

        return piece

    def kv_rows(shard):
        return kv_ref.at[pl.ds(pl.multiple_of(shard * 128, 128), 128)]

    far_shard = lax.rem(s + 16, 32)
    half_cols = pl.ds(pl.multiple_of(core * 1024, 128), 1024)
    panels = pl.ds(core * 3, 3)

    def qkv_at(which, row, count):
        return probs.at[which, row // 512, pl.ds(pl.multiple_of(lax.rem(row, 512), 16), count)]

    def qkv_place(group):
        def piece(gx, gy, h, part):
            row = (group * 16 + gx * 4 + gy) * 64 + h * 32
            return qkv_at(panels, row, 32) if part is None else qkv_at(panels, row + part * 16, 16)

        return piece

    def qkv_half(group, which):
        return probs.at[pl.ds(which * 3, 3), pl.ds(group * 2, 2)]

    def out_cols(h):
        return pl.ds(pl.multiple_of(core * 1024 + h * 512, 128), 512)

    def out_place(group):
        def piece(gx, gy, h, part):
            row = (group * 16 + gx * 4 + gy) * 32
            if part is None:
                return out_full.at[pl.ds(pl.multiple_of(row, 16), 32), out_cols(h)]
            return out_full.at[pl.ds(pl.multiple_of(row + part * 16, 16), 16), out_cols(h)]

        return piece

    def out_half(group, which):
        columns = pl.ds(pl.multiple_of(which * 1024, 128), 1024)
        return out_full.at[pl.ds(pl.multiple_of(group * 512, 32), 512), columns]

    def out_rows(shard):
        return out_full.at[pl.ds(pl.multiple_of(shard * 32, 32), 32), half_cols]

    for p in range(6):
        qkv_own[p] = qkv_in[:, p * 256 : p * 256 + 256]
    greet(net.xy_neighbours() + [net.sibling(), net.partner()])

    zq = wire.new(1)
    wire.send(qkv_own.at[panels], qkv_at(panels, s * 64, 64), zq, net.partner())
    near_q = gather_stages(net, wire, lambda h: qkv_own.at[panels, pl.ds(h * 32, 32)], qkv_place(zh))
    near_q[0]()
    probs[panels, (s * 64) // 512, pl.ds(pl.multiple_of(lax.rem(s * 64, 512), 64), 64)] = qkv_own[panels]
    out_full[pl.ds(pl.multiple_of(s * 32, 32), 32), half_cols] = out_in[:, half_cols]
    peak[...] = jnp.full_like(peak, NEG_FILL)
    total[...] = jnp.zeros_like(total)
    acc[...] = jnp.zeros_like(acc)
    dqt[...] = jnp.zeros_like(dqt)
    for stage in near_q[1:6]:
        stage()
    wire.recv(qkv_at(panels, far_shard * 64, 64), zq, net.partner())
    zo = wire.new(1)
    wire.send(out_in.at[:, half_cols], out_rows(s), zo, net.partner())
    far_qp = qkv_place(other)
    far_q = gather_stages(net, wire, lambda h: far_qp(net.x, net.y, h, None), far_qp)
    far_q[0]()
    near_q[6]()
    share_q = wire.new(2)
    wire.send(qkv_half(zh, core), qkv_half(zh, core), share_q, net.sibling())
    for stage in far_q[1:3]:
        stage()

    def project(group, first):
        def step(p, carry):
            columns = pl.ds(pl.multiple_of(p * 256, 256), 256)
            result = jnp.zeros((128, 256), F32) if first else proj[:, columns]
            for b in (0, 1):
                rows = pl.ds(pl.multiple_of(group * 1024 + b * 512, 512), 512)
                result = result + jnp.dot(x_ref[:, rows], probs[p, group * 2 + b], preferred_element_type=F32)
            proj[:, columns] = result
            return carry

        lax.fori_loop(0, 6, step, 0)

    for stage in far_q[3:5]:
        stage()
    wire.recv(qkv_half(zh, 1 - core), share_q, net.sibling())
    project(zh, True)
    for stage in far_q[5:]:
        stage()
    wire.send(qkv_half(other, core), qkv_half(other, core), share_q + 1, net.sibling())
    early = wire.taken()
    near_o = gather_stages(net, wire, lambda h: out_in.at[:, out_cols(h)], out_place(zh))
    near_o[0]()
    wire.recv(qkv_half(other, 1 - core), share_q + 1, net.sibling())
    keep = []
    for p in range(6):
        for b in range(4):
            place = qkv_hbm.at[pl.ds(b * 512, 512), pl.ds(p * 256, 256)]
            keep.append(pltpu.make_async_copy(probs.at[p, b], place, local_sems.at[p * 4 + b]))
    for made in keep:
        made.start()
    project(other, False)
    cos, sin = cos_ref[...], sin_ref[...]

    def turn(rows_t):
        a, b = rows_t[0:32], rows_t[32:64]
        return [a * cos - b * sin, b * cos + a * sin]

    for c in (0, 1):
        keys_t = proj[:, 1024 + c * 128 : 1152 + c * 128].T
        pair = turn(keys_t[0:64]) + turn(keys_t[64:128])
        kv_in[:, c * 128 : c * 128 + 128] = jnp.concatenate(pair, axis=0).astype(BF16).T
    kv_in[:, 256:512] = proj[:, 1280:1536].astype(BF16)

    zkey = wire.new(1)
    wire.send(kv_in, kv_rows(s), zkey, net.partner())
    near = gather_stages(net, wire, lambda h: kv_in.at[pl.ds(h * 64, 64)], kv_place(kv_ref, zh))
    near[0]()
    near_o[1]()
    kv_ref[pl.ds(pl.multiple_of(s * 128, 128), 128)] = kv_in[...]
    pieces = []
    for c in range(8):
        queries_t = proj[:, c * 128 : c * 128 + 128].T
        pieces += turn(queries_t[0:64]) + turn(queries_t[64:128])
    spread_heads((jnp.concatenate(pieces, axis=0).astype(BF16).astype(F32) * 0.125).astype(BF16), qt, qn)
    near[1]()
    near_o[2]()
    near[2]()
    near_o[3]()
    near[3]()
    near[4]()
    near_o[4]()
    near[5]()
    near_o[5]()
    wire.recv(kv_rows(far_shard), zkey, net.partner())
    far_place = kv_place(kv_ref, other)
    far = gather_stages(net, wire, lambda h: far_place(net.x, net.y, h, None), far_place)
    far[0]()
    wire.recv(out_rows(far_shard), zo, net.partner())
    far_op = out_place(other)
    far_o = gather_stages(net, wire, lambda h: far_op(net.x, net.y, h, None), far_op)
    far_o[0]()
    near[6]()
    near_o[6]()
    share_o = wire.new(2)
    wire.send(out_half(zh, core), out_half(zh, core), share_o, net.sibling())
    for made in keep:
        made.wait()
    wire.drain(early)

    def rows_of(j):
        return pl.ds(pl.multiple_of(j * BLOCK, BLOCK), BLOCK)

    def forward(j, masked):
        keys = kv_ref[rows_of(j), 0:256]
        values_t = kv_ref[rows_of(j), 256:512].T
        if masked:
            key_at = lax.broadcasted_iota(jnp.int32, (BLOCK, 512), 0) + j * BLOCK
            query_at = lax.rem(lax.broadcasted_iota(jnp.int32, (BLOCK, 512), 1), 128) + s * 128
            visible = key_at <= query_at
        ahead = jnp.dot(keys, qt[0], preferred_element_type=F32)
        for g in range(4):
            scores = ahead
            if g < 3:
                ahead = jnp.dot(keys, qt[g + 1], preferred_element_type=F32)
            if masked:
                scores = jnp.where(visible, scores, NEG_FILL)
            before = peak[g]
            now = jnp.maximum(before, jnp.max(scores, axis=0, keepdims=True))
            fade = jnp.exp(before - now)
            e = jnp.exp(scores - now)
            total[g] = total[g] * fade + jnp.sum(e, axis=0, keepdims=True)
            e = e.astype(BF16)
            for c in (0, 1):
                probs[4 * g + j // 2, lax.rem(j, 2) * 2 + c] = e[:, c * 256 : c * 256 + 256]
            peaks[g, j] = now
            peak[g] = now
            acc[g] = acc[g] * fade + jnp.dot(values_t[g * 64 : g * 64 + 64], e, preferred_element_type=F32)

    def in_turn(plans, i):
        for k, plan in enumerate(plans):

            @pl.when(i == k)
            def _():
                for stage in plan:
                    stage()

    def near_forward(i, carry):
        in_turn([[far[1], far_o[1]], [far[2], far_o[2]], [far[3], far_o[3]], [far[4], far_o[4]]], i)

        @pl.when(i < x)
        def _():
            forward(zh * 4 + i, False)

        @pl.when(i == x)
        def _():
            forward(zh * 4 + i, True)

        return carry

    lax.fori_loop(0, 4, near_forward, 0)
    far[5]()
    far_o[5]()

    def landed(h, da, d):
        key = far.base + 24 + (h * 4 + RING.index(da)) * 2 + side(d)
        wire.recv(far_place(*net.at(h, da, 2), h, side(d)), key, net.dev(h, 0, -d))

    def far_forward(i, carry):
        for k, da in enumerate((0, 1, -1, 2)):

            @pl.when(i == k)
            def _(da=da):
                for d in SIDES:
                    landed(0, da, d)
                if da == 2:
                    for db in RING:
                        for d in SIDES:
                            landed(1, db, d)

        @pl.when(zh == 1)
        def _():
            forward(lax.rem(x + lax.rem(8 + i - 3 * ((i * (i - 1)) // 2) + 4 * i, 4), 4), False)

        return carry

    lax.fori_loop(0, 4, far_forward, 0)
    far_o[6]()
    wire.send(out_half(other, core), out_half(other, core), share_o + 1, net.sibling())

    for g in range(4):
        attended = (acc[g] / total[g]).astype(BF16)
        for k in range(4):
            head = 4 * g + k
            att_t[head * 64 : head * 64 + 64] = attended[:, k * 128 : k * 128 + 128]
    core_key = wire.new(2)
    for g in (0, 1):
        rows = slice(g * 512, g * 512 + 512)
        sib_cols = pl.ds(pl.multiple_of((1 - core) * 1024, 128), 1024)
        do_sib[rows] = jnp.dot(att_t[rows], cot_ref[:, sib_cols], preferred_element_type=F32).astype(BF16)
        wire.send(do_sib.at[pl.ds(g * 512, 512)], sib_o.at[pl.ds(g * 512, 512)], core_key + g, net.sibling())
    wire.recv(out_half(zh, 1 - core), share_o, net.sibling())
    wire.recv(out_half(other, 1 - core), share_o + 1, net.sibling())
    grad_t = lax.dot_general(
        out_full[...], cot_ref[...], (((1,), (1,)), ((), ())), preferred_element_type=F32
    ).astype(BF16)
    spread_heads(grad_t, dot_, don)
    for g in range(4):
        for k in range(4):
            head = 4 * g + k
            rows = slice(head * 64, head * 64 + 64)
            both = att_t[rows].astype(F32) * dot_[g, g * 64 : g * 64 + 64, k * 128 : k * 128 + 128].astype(F32)
            dots[g, :, k * 128 : k * 128 + 128] = jnp.sum(both, axis=0, keepdims=True)
        peak[g] = peak[g] + jnp.log(total[g])

    def out_own(group):
        def piece(gx, gy, h, part):
            row = (group * 16 + gx * 4 + gy) * 32
            if part is None:
                return sum_o.at[pl.ds(pl.multiple_of(row, 16), 32), pl.ds(h * 512, 512)]
            return sum_o.at[pl.ds(pl.multiple_of(row + part * 16, 16), 16), pl.ds(h * 512, 512)]

        return piece

    def out_emit(group):
        def emit(h, result):
            for part in (0, 1):
                parts_o[group, 2 * h + part] = result[:, part * 256 : part * 256 + 256]

        return emit

    scat_o = [Scatter(net, wire, out_own(g), bufs[16 + 8 * g : 24 + 8 * g], out_emit(g)) for g in (0, 1)]

    def add_cores(g):
        def run():
            rows = slice(g * 512, g * 512 + 512)
            wire.recv(sib_o.at[pl.ds(g * 512, 512)], core_key + g, net.sibling())
            own = jnp.dot(att_t[rows], cot_ref[:, half_cols], preferred_element_type=F32)
            sum_o[rows] = (own + sib_o[rows].astype(F32)).astype(BF16)
            scat_o[g].all_a()

        return run

    def backward(j):
        keys_t = kv_ref[rows_of(j), 0:256].T
        values = kv_ref[rows_of(j), 256:512]
        ahead = jnp.dot(values, dot_[0], preferred_element_type=F32)
        dk = dv = None
        for g in range(4):
            grads = ahead
            if g < 3:
                ahead = jnp.dot(values, dot_[g + 1], preferred_element_type=F32)
            e = jnp.concatenate([probs[4 * g + j // 2, lax.rem(j, 2) * 2 + c] for c in (0, 1)], axis=1)
            p = e.astype(F32) * jnp.exp(peaks[g, j] - peak[g])
            ds = (p * (grads - dots[g])).astype(BF16)
            p = p.astype(BF16)
            dqt[g] += jnp.dot(keys_t[g * 64 : g * 64 + 64], ds, preferred_element_type=F32)
            rows = slice(g * 512, g * 512 + 512)
            dk_g = jnp.dot(ds, qn[rows], preferred_element_type=F32)
            dv_g = jnp.dot(p, don[rows], preferred_element_type=F32)
            dk = dk_g if g == 0 else dk + dk_g
            dv = dv_g if g == 0 else dv + dv_g
        terms[rows_of(j), 0:256] = dk.astype(BF16)
        terms[rows_of(j), 256:512] = dv.astype(BF16)

    zback = wire.new(2)

    def emit_far(h, result):
        far_out[h] = result.astype(BF16)
        wire.send(far_out.at[h], far_in.at[h], zback + h, net.partner())

    def emit_near(h, result):
        kvg_ref[pl.ds(h * 64, 64)] = result

    scat_far = Scatter(net, wire, kv_place(terms, other), bufs[0:8], emit_far)
    scat_near = Scatter(net, wire, kv_place(terms, zh), bufs[8:16], emit_near)

    def after(scat):
        one = functools.partial

        def plan0():
            scat.a(0, 2)
            for da in scat.ORDER:
                scat.a(1, da)

        def plan1():
            scat.a(0, 1)
            for da in scat.ORDER:
                scat.b(1, da, 1)
            for d in SIDES:
                scat.b(0, 2, d)

        def plan2():
            scat.a(0, -1)
            for da in scat.ORDER:
                scat.b(1, da, -1)
            for d in SIDES:
                scat.b(0, 1, d)
            scat.c(0, 2)

        def plan3():
            scat.a(0, 0)
            scat.c(1, 2)
            for d in SIDES:
                scat.b(0, -1, d)
            scat.c(0, 1)

        return [[plan0], [plan1], [plan2], [plan3]]

    def late1(scat):
        def run():
            scat.c(1, 1)
            scat.c(1, -1)
            for d in SIDES:
                scat.b(0, 0, d)
            for d in SIDES:
                scat.d(1, d)
            scat.c(0, -1)
            for d in SIDES:
                scat.d(0, d)

        return run

    def late2(scat):
        def run():
            scat.c(1, 0)
            scat.c(0, 0)

        return run

    def block_loop(group, plans):
        def step(i, carry):
            turn = lax.rem(18 - i + 3 * ((i * (i - 1)) // 2), 4)
            j = group * 4 + lax.rem(x + turn, 4)

            @pl.when(j <= s // 4)
            def _():
                backward(j)

            @pl.when(j > s // 4)
            def _():
                terms[rows_of(j)] = jnp.zeros((BLOCK, 512), BF16)

            in_turn(plans, i)
            return carry

        lax.fori_loop(0, 4, step, 0)

    plans = after(scat_far)
    plans[1].append(add_cores(0))
    plans[2].append(add_cores(1))
    plans[3].append(scat_o[0].all_b)
    block_loop(other, plans)
    plans = after(scat_near)
    plans[0] = [late1(scat_far)] + plans[0] + [scat_o[1].all_b]
    plans[1] = [late2(scat_far)] + plans[1] + [scat_o[0].all_c]
    plans[2] = [scat_far.all_e] + plans[2] + [scat_o[1].all_c, scat_o[0].all_d]
    plans[3] = plans[3] + [scat_o[1].all_d, scat_o[0].all_e]
    block_loop(zh, plans)
    late1(scat_near)()
    attended = att_t[...].T
    for c in range(4):
        cols = slice(c * 512, c * 512 + 512)
        block_ref[:, cols] = jnp.dot(attended, out_full[:, cols], preferred_element_type=F32).astype(BF16)
    def turn_back(rows_t):
        a, b = rows_t[0:32], rows_t[32:64]
        return jnp.concatenate([a * cos + b * sin, b * cos - a * sin], axis=0)

    for g in range(4):
        for k in range(0, 4, 2):
            head = 4 * g + k
            pair = [turn_back(dqt[g, :, c * 128 : c * 128 + 128] * 0.125) for c in (k, k + 1)]
            gp_ref[:, head * 64 : head * 64 + 128] = jnp.concatenate(pair, axis=0).T.astype(BF16)
    scat_o[1].all_e()
    late2(scat_near)()
    scat_near.all_e()
    for h in (0, 1):
        wire.recv(far_in.at[h], zback + h, net.partner())
        kvg_ref[pl.ds(h * 64, 64)] += far_in[h].astype(F32)
    for c in range(2):
        keys_t = kvg_ref[:, c * 128 : c * 128 + 128].T
        pair = [turn_back(keys_t[0:64]), turn_back(keys_t[64:128])]
        gp_ref[:, 1024 + c * 128 : 1152 + c * 128] = jnp.concatenate(pair, axis=0).T.astype(BF16)
    gp_ref[:, 1280:1536] = kvg_ref[:, 256:512].astype(BF16)
    wire.drain()


def attend(inputs, qkv_weight, out_weight, cotangent, cos_t, sin_t):
    keys = 10 * AG_KEYS + 11
    return pl.pallas_call(
        attend_kernel,
        out_shape=(
            jax.ShapeDtypeStruct((128, 1536), BF16),
            jax.ShapeDtypeStruct((128, 2048), BF16),
            jax.ShapeDtypeStruct((2, 4, 32, 256), F32),
            jax.ShapeDtypeStruct((2048, 1536), BF16),
        ),
        in_specs=[pl.BlockSpec(memory_space=pltpu.VMEM)] * 6,
        out_specs=[pl.BlockSpec(memory_space=pltpu.VMEM)] * 3 + [pl.BlockSpec(memory_space=pl.ANY)],
        scratch_shapes=[
            pltpu.VMEM((6, 64, 256), BF16),
            pltpu.VMEM((128, 1536), F32),
            pltpu.VMEM((128, 512), BF16),
            pltpu.VMEM((4096, 512), BF16),
            pltpu.VMEM((1024, 2048), BF16),
            pltpu.VMEM((128, 512), F32),
            pltpu.VMEM((4096, 512), BF16),
            pltpu.VMEM((4, 256, 512), BF16),
            pltpu.VMEM((2048, 256), BF16),
            pltpu.VMEM((4, 256, 512), BF16),
            pltpu.VMEM((2048, 256), BF16),
            pltpu.VMEM((16, 4, BLOCK, 256), BF16),
            pltpu.VMEM((4, 8, 1, 512), F32),
            pltpu.VMEM((4, 1, 512), F32),
            pltpu.VMEM((4, 1, 512), F32),
            pltpu.VMEM((4, 64, 512), F32),
            pltpu.VMEM((4, 64, 512), F32),
            pltpu.VMEM((4, 1, 512), F32),
            pltpu.VMEM((1024, 128), BF16),
            pltpu.VMEM((1024, 1024), BF16),
            pltpu.VMEM((1024, 1024), BF16),
            pltpu.VMEM((1024, 1024), BF16),
            pltpu.VMEM((2, 64, 512), BF16),
            pltpu.VMEM((2, 64, 512), BF16),
            pltpu.SemaphoreType.DMA((keys,)),
            pltpu.SemaphoreType.DMA((keys,)),
            pltpu.SemaphoreType.DMA((24,)),
            *scatter_scratch(64, 512),
            *scatter_scratch(64, 512),
            *scatter_scratch(32, 512),
            *scatter_scratch(32, 512),
        ],
        compiler_params=pltpu.CompilerParams(
            collective_id=0, has_side_effects=True, vmem_limit_bytes=VMEM_BYTES
        ),
        name="attend",
    )(inputs, qkv_weight, out_weight, cotangent, cos_t, sin_t)


def weight_grad_kernel(
    scale,
    x_ref,
    gp_ref,
    w_ref,
    parts_o,
    tg_ref,
    out_q,
    out_o,
    xt,
    do_sib,
    sib_q,
    sum_q,
    zs_q,
    zs_o,
    zr_q,
    zr_o,
    keep_q,
    fin_q,
    fin_o,
    got_q,
    got_o,
    canvas,
    send_sems,
    recv_sems,
    *bufs,
):
    net = Net()
    wire = Wire(send_sems, recv_sems, (canvas, None), net.sibling())
    core = net.core
    cols_q = [pl.ds(pl.multiple_of(c * 768, 128), 768) for c in (core, 1 - core)]
    cols_o = [pl.ds(pl.multiple_of(c * 1024, 128), 1024) for c in (core, 1 - core)]
    greet(net.xy_neighbours() + [net.sibling()] + [net.up(k) for k in range(1, 8)])

    z1 = wire.new(14)

    def z_send(k, staged, slots, key):
        target = lax.rem(net.z + k, 8)
        wire.send(staged.at[target // 4, lax.rem(target, 4)], slots.at[k - 1], key + k - 1, net.up(k))

    for g in (0, 1):
        for l in range(4):
            zs_o[g, l] = parts_o[g, l].astype(BF16)
    for k in range(1, 8):
        z_send(k, zs_o, zr_o, z1)

    xt[...] = x_ref[...].T
    ckey = wire.new(2)

    def product(rows, cols):
        return jnp.dot(xt[rows], gp_ref[:, cols], preferred_element_type=F32)

    def make_sibling(g):
        def step(i, carry):
            rows = pl.ds(pl.multiple_of(g * 1024 + i * 256, 256), 256)
            do_sib[rows] = product(rows, cols_q[1]).astype(BF16)
            return carry

        lax.fori_loop(0, 4, step, 0)
        rows = pl.ds(g * 1024, 1024)
        wire.send(do_sib.at[rows], sib_q.at[rows], ckey + g, net.sibling())

    def add_cores(g):
        wire.recv(sib_q.at[pl.ds(g * 1024, 1024)], ckey + g, net.sibling())

        def step(i, carry):
            rows = pl.ds(pl.multiple_of(g * 1024 + i * 256, 256), 256)
            sum_q[rows] = (product(rows, cols_q[0]) + sib_q[rows].astype(F32)).astype(BF16)
            return carry

        lax.fori_loop(0, 4, step, 0)

    def own_q(g):
        def piece(gx, gy, h, part):
            row = (g * 16 + gx * 4 + gy) * 64 + h * 32
            if part is None:
                return sum_q.at[pl.ds(pl.multiple_of(row, 16), 32)]
            return sum_q.at[pl.ds(pl.multiple_of(row + part * 16, 16), 16)]

        return piece

    def emit_q(g):
        def emit(h, result):
            for part in (0, 1):
                rows = result[part * 16 : part * 16 + 16]
                keep_q[g, 2 * h + part] = rows
                zs_q[g, 2 * h + part] = rows.astype(BF16)

        return emit

    runs = [Scatter(net, wire, own_q(g), bufs[8 * g : 8 * g + 8], emit_q(g)) for g in (0, 1)]

    def tokens_grad(c):
        rows = slice(c * 512, c * 512 + 512)
        tg_ref[:, rows] = lax.dot_general(
            gp_ref[...], w_ref[rows], (((1,), (1,)), ((), ())), preferred_element_type=F32
        ).astype(BF16)

    make_sibling(0)
    make_sibling(1)
    add_cores(0)
    runs[0].all_a()
    add_cores(1)
    runs[1].all_a()
    tokens_grad(0)
    runs[0].all_b()
    runs[1].all_b()
    tokens_grad(1)
    runs[0].all_c()
    runs[1].all_c()
    tokens_grad(2)
    runs[0].all_d()
    runs[1].all_d()
    tokens_grad(3)
    runs[0].all_e()
    runs[1].all_e()

    z1q = z1 + 7
    for k in range(1, 8):
        z_send(k, zs_q, zr_q, z1q)

    def place(l):
        return (
            got_q.at[pl.ds(pl.multiple_of(l * 16, 16), 16), cols_q[0]],
            got_o.at[:, pl.ds(pl.multiple_of(core * 1024 + l * 256, 128), 256)],
        )

    def level(k):
        l = lax.rem(net.zl + k, 4)
        return l, (net.s, l * 2 + core)

    z2 = wire.new(6)
    mine = place(net.zl)

    def z_sum(first, slots, key):
        result = first
        for k in range(1, 8):
            wire.recv(slots.at[k - 1], key + k - 1, net.up(8 - k))
            result = result + slots[k - 1].astype(F32)
        return (result * scale).astype(BF16)

    def z_spread(which, ref, key):
        for k in (1, 2, 3):
            wire.send(ref, mine[which], key + k - 1, level(k)[1])

    fin_o[...] = z_sum(parts_o[net.zh, net.zl], zr_o, z1)
    z_spread(1, fin_o, z2)
    got_o[:, pl.ds(pl.multiple_of(core * 1024 + net.zl * 256, 128), 256)] = fin_o[...]
    fin_q[...] = z_sum(keep_q[net.zh, net.zl], zr_q, z1q)
    z_spread(0, fin_q, z2 + 3)
    got_q[pl.ds(pl.multiple_of(net.zl * 16, 16), 16), cols_q[0]] = fin_q[...]
    last = wire.new(2)
    for k in (1, 2, 3):
        l, device = level(4 - k)
        wire.recv(place(l)[1], z2 + k - 1, device)
    wire.send(got_o.at[:, cols_o[0]], got_o.at[:, cols_o[0]], last, net.sibling())
    for k in (1, 2, 3):
        l, device = level(4 - k)
        wire.recv(place(l)[0], z2 + 3 + k - 1, device)
    wire.send(got_q.at[:, cols_q[0]], got_q.at[:, cols_q[0]], last + 1, net.sibling())
    wire.recv(got_o.at[:, cols_o[1]], last, net.sibling())
    wire.recv(got_q.at[:, cols_q[1]], last + 1, net.sibling())
    out_o[...] = got_o[...].astype(F32)
    out_q[...] = got_q[...].astype(F32)
    wire.drain()


def weight_grads(inputs, grad_proj, qkv_full, parts_o, scale):
    keys = 2 * AG_KEYS + 14 + 2 + 6 + 2
    return pl.pallas_call(
        functools.partial(weight_grad_kernel, scale),
        out_shape=(
            jax.ShapeDtypeStruct((128, 2048), BF16),
            jax.ShapeDtypeStruct((64, 1536), F32),
            jax.ShapeDtypeStruct((32, 2048), F32),
        ),
        in_specs=[pl.BlockSpec(memory_space=pltpu.VMEM)] * 4,
        out_specs=[pl.BlockSpec(memory_space=pltpu.VMEM)] * 3,
        scratch_shapes=[
            pltpu.VMEM((2048, 128), BF16),
            pltpu.VMEM((2048, 768), BF16),
            pltpu.VMEM((2048, 768), BF16),
            pltpu.VMEM((2048, 768), BF16),
            pltpu.VMEM((2, 4, 16, 768), BF16),
            pltpu.VMEM((2, 4, 32, 256), BF16),
            pltpu.VMEM((7, 16, 768), BF16),
            pltpu.VMEM((7, 32, 256), BF16),
            pltpu.VMEM((2, 4, 16, 768), F32),
            pltpu.VMEM((16, 768), BF16),
            pltpu.VMEM((32, 256), BF16),
            pltpu.VMEM((64, 1536), BF16),
            pltpu.VMEM((32, 2048), BF16),
            pltpu.VMEM((1024, 1024), BF16),
            pltpu.SemaphoreType.DMA((keys,)),
            pltpu.SemaphoreType.DMA((keys,)),
            *scatter_scratch(32, 768),
            *scatter_scratch(32, 768),
        ],
        compiler_params=pltpu.CompilerParams(
            collective_id=2, has_side_effects=True, vmem_limit_bytes=VMEM_BYTES
        ),
        name="weight_grads",
    )(inputs, grad_proj, qkv_full, parts_o)


def finish_kernel(*refs):
    for i in range(4):
        refs[i + 4][...] = refs[i][...]


def finish(*results):
    return pl.pallas_call(
        finish_kernel,
        out_shape=tuple(jax.ShapeDtypeStruct(r.shape, r.dtype) for r in results),
        in_specs=[pl.BlockSpec(memory_space=pltpu.VMEM)] * 4,
        out_specs=[pl.BlockSpec(memory_space=pltpu.VMEM)] * 4,
        name="finish",
    )(*results)


def tables(positions, head_size):
    halves = head_size // 2
    frequency = ROPE_BASE ** (-(jnp.arange(halves, dtype=jnp.float32) * 2.0) / head_size)
    angles = positions.astype(jnp.float32)[:, None] * frequency[None, :]
    return (jnp.cos(angles), jnp.sin(angles))


def rotate(matrix, cos_rows, sin_rows, head_count):
    row_count = matrix.shape[0]
    head_size = matrix.shape[1] // head_count
    halves = head_size // 2
    pieces = matrix.reshape(row_count, head_count, 2, halves)
    lower_half = pieces[:, :, 0]
    upper_half = pieces[:, :, 1]
    cos_part = cos_rows[:, None, :]
    sin_part = sin_rows[:, None, :]
    turned = jnp.stack(
        [
            lower_half * cos_part - upper_half * sin_part,
            upper_half * cos_part + lower_half * sin_part,
        ],
        axis=2,
    )
    return turned.reshape(row_count, head_count * head_size)


def body(tokens, qkv_weight, out_weight, cotangent):
    inputs = tokens[0]
    tok_count = inputs.shape[0]
    positions = lax.axis_index("shard") * tok_count + jnp.arange(tok_count, dtype=jnp.int32)
    cosine, sine = tables(positions, HEAD_DIM)
    grad_proj, block_output, parts_o, qkv_full = attend(
        inputs, qkv_weight, out_weight, cotangent[0], cosine.T, sine.T
    )
    norm_factor = 1.0 / math.sqrt(lax.axis_size("rep") * lax.axis_size("shard") * tok_count)
    tokens_grad, qkv_grad, out_grad = weight_grads(inputs, grad_proj, qkv_full, parts_o, norm_factor)
    block_output, tokens_grad, qkv_grad, out_grad = finish(block_output, tokens_grad, qkv_grad, out_grad)
    return (block_output[None], tokens_grad[None], qkv_grad, out_grad)


def solution(mesh):
    return jax.shard_map(
        body,
        mesh=mesh,
        in_specs=(
            P("rep", "shard", None),
            P("shard", None),
            P("shard", None),
            P("rep", "shard", None),
        ),
        out_specs=(
            P("rep", "shard", None),
            P("rep", "shard", None),
            P("shard", None),
            P("shard", None),
        ),
        check_vma=False,
    )
```

```python
import functools
import math

import jax
import jax.numpy as jnp
from jax import lax
from jax.experimental import pallas as pl
from jax.experimental.pallas import tpu as pltpu
from jax.sharding import PartitionSpec as P

HEADS = 16
KV_HEADS = 4
HEAD_DIM = 64

ROPE_BASE = 500000.0
NEG_FILL = -1e30
MESH = pl.DeviceIdType.MESH
BF16 = jnp.bfloat16
F32 = jnp.float32
VMEM_BYTES = 62 * 1024 * 1024


class Net:
    def __init__(self):
        self.s = lax.axis_index("shard")
        self.r = lax.axis_index("rep")
        self.zh = self.s // 16
        self.x = lax.rem(self.s // 4, 4)
        self.y = lax.rem(self.s, 4)
        self.zl = self.r // 2
        self.core = lax.rem(self.r, 2)
        self.z = self.zh * 4 + self.zl

    def at(self, h, da, db):
        dx, dy = (da, db) if h == 0 else (db, da)
        return lax.rem(self.x + (dx + 4), 4), lax.rem(self.y + (dy + 4), 4)

    def dev(self, h, da, db):
        gx, gy = self.at(h, da, db)
        return (self.zh * 16 + gx * 4 + gy, self.r)

    def sibling(self):
        return (self.s, self.zl * 2 + 1 - self.core)

    def partner(self):
        return (lax.rem(self.s + 16, 32), self.r)

    def up(self, k):
        z = lax.rem(self.z + k, 8)
        return ((z // 4) * 16 + self.x * 4 + self.y, lax.rem(z, 4) * 2 + self.core)

    def xy_neighbours(self):
        return [self.dev(0, 1, 0), self.dev(0, -1, 0), self.dev(0, 0, 1), self.dev(0, 0, -1)]


def greet(devices):
    barrier = pltpu.get_barrier_semaphore()
    for device in devices:
        pl.semaphore_signal(barrier, inc=1, device_id=device, device_id_type=MESH)
    pl.semaphore_wait(barrier, len(devices))


class Wire:
    def __init__(self, send_sems, recv_sems, canvas, device):
        self.send_sems, self.recv_sems = send_sems, recv_sems
        self.canvas, self.device = canvas, device
        self.used = 0
        self.sent = []

    def new(self, count=1):
        first = self.used
        self.used += count
        return first

    def copy(self, src, dst, key, device):
        return pltpu.make_async_remote_copy(
            src_ref=src,
            dst_ref=dst,
            send_sem=self.send_sems.at[key],
            recv_sem=self.recv_sems.at[key],
            device_id=device,
            device_id_type=MESH,
        )

    def send(self, src, dst, key, device):
        self.copy(src, dst, key, device).start()
        self.sent.append((src.shape, src.dtype, key))

    def recv(self, ref, key, device):
        self.copy(ref, ref, key, device).wait_recv()

    def taken(self):
        sent, self.sent = self.sent, []
        return sent

    def drain(self, sent=None):
        for shape, dtype, key in self.taken() if sent is None else sent:
            cols = shape[1] if len(shape) == 2 else 1024 if len(shape) == 4 else 256
            rows = math.prod(shape) // cols
            ref = self.canvas[dtype == F32].at[pl.ds(0, rows), pl.ds(0, cols)]
            self.copy(ref, ref, key, self.device).wait_send()


SIDES = (1, -1)
RING = (0, 1, -1, 2)
AG_KEYS = 40


def side(d):
    return 0 if d == 1 else 1


class Stages(list):
    def __init__(self, base, stages):
        super().__init__(stages)
        self.base = base


def gather_stages(net, wire, own, piece):
    base = wire.new(AG_KEYS)

    def s1(h, d):
        return base + h * 2 + side(d)

    def s2(h, d):
        return base + 4 + h * 2 + side(d)

    def t1(h, da, d):
        return base + 8 + (h * 4 + RING.index(da)) * 2 + side(d)

    def t2(h, da, d):
        return base + 24 + (h * 4 + RING.index(da)) * 2 + side(d)

    def at(h, da, db, part=None):
        return piece(*net.at(h, da, db), h, part)

    def spread(h, da, src):
        for d in SIDES:
            wire.send(src, at(h, da, 0), t1(h, da, d), net.dev(h, 0, d))

    def pass_on(h, da):
        for d in SIDES:
            wire.recv(at(h, da, -d), t1(h, da, d), net.dev(h, 0, -d))
            part = side(d)
            wire.send(at(h, da, -d, part), at(h, da, -d, part), t2(h, da, d), net.dev(h, 0, d))

    def stage_a():
        for h in (0, 1):
            for d in SIDES:
                wire.send(own(h), at(h, 0, 0), s1(h, d), net.dev(h, d, 0))
        for h in (0, 1):
            spread(h, 0, own(h))

    def stage_b():
        for d in SIDES:
            for h in (0, 1):
                wire.recv(at(h, -d, 0), s1(h, d), net.dev(h, -d, 0))
                part = side(d)
                wire.send(at(h, -d, 0, part), at(h, -d, 0, part), s2(h, d), net.dev(h, d, 0))
        for d in SIDES:
            for h in (0, 1):
                spread(h, -d, at(h, -d, 0))

    def stage_c():
        for h in (0, 1):
            pass_on(h, 0)

    def stage_d():
        for h in (0, 1):
            for d in SIDES:
                wire.recv(at(h, 2, 0, side(d)), s2(h, d), net.dev(h, -d, 0))
            spread(h, 2, at(h, 2, 0))

    def stage_e():
        for da in (-1, 1):
            for h in (0, 1):
                pass_on(h, da)

    def stage_f():
        for h in (0, 1):
            pass_on(h, 2)

    def stage_g():
        for da in (0, -1, 1, 2):
            for h in (0, 1):
                for d in SIDES:
                    wire.recv(at(h, da, 2, side(d)), t2(h, da, d), net.dev(h, 0, -d))

    return Stages(base, [stage_a, stage_b, stage_c, stage_d, stage_e, stage_f, stage_g])


def scatter_scratch(rows, cols):
    return [
        pltpu.VMEM((2, 4, 2, rows // 2, cols), BF16),
        pltpu.VMEM((2, 4, 2, rows, cols), BF16),
        pltpu.VMEM((2, 4, 2, rows, cols), BF16),
        pltpu.VMEM((2, 3, rows, cols), F32),
        pltpu.VMEM((2, rows, cols), BF16),
        pltpu.VMEM((2, 2, rows // 2, cols), BF16),
        pltpu.VMEM((2, 2, rows, cols), BF16),
        pltpu.VMEM((2, 2, rows, cols), BF16),
    ]


class Scatter:
    ORDER = (2, 1, -1, 0)

    def __init__(self, net, wire, own, bufs, emit):
        self.net, self.wire, self.own, self.emit = net, wire, own, emit
        self.t2b, self.t1s, self.t1b, self.row_sum, self.s2s, self.s2b, self.s1s, self.s1b = bufs
        self.rows = self.row_sum.shape[2]
        self.half = self.rows // 2
        self.base = wire.new(AG_KEYS)

    def s1(self, h, d):
        return self.base + h * 2 + side(d)

    def s2(self, h, d):
        return self.base + 4 + h * 2 + side(d)

    def t1(self, h, i, d):
        return self.base + 8 + (h * 4 + i) * 2 + side(d)

    def t2(self, h, i, d):
        return self.base + 24 + (h * 4 + i) * 2 + side(d)

    def part(self, p):
        return pl.ds(p * self.half, self.half)

    def load(self, h, da, db, part=None):
        return self.own(*self.net.at(h, da, db), h, part)[...].astype(F32)

    def a(self, h, da):
        i, net = RING.index(da), self.net
        for d in SIDES:
            p = side(d)
            src = self.own(*net.at(h, da, 2), h, p)
            self.wire.send(src, self.t2b.at[h, i, p], self.t2(h, i, d), net.dev(h, 0, d))

    def b(self, h, da, d):
        i, p, net = RING.index(da), side(d), self.net
        self.wire.recv(self.t2b.at[h, i, p], self.t2(h, i, d), net.dev(h, 0, -d))
        added = self.load(h, da, d, p) + self.t2b[h, i, p].astype(F32)
        self.t1s[h, i, p, self.part(p)] = added.astype(BF16)
        self.t1s[h, i, p, self.part(1 - p)] = self.load(h, da, d, 1 - p).astype(BF16)
        self.wire.send(self.t1s.at[h, i, p], self.t1b.at[h, i, p], self.t1(h, i, d), net.dev(h, 0, d))

    def c(self, h, da):
        i, net = RING.index(da), self.net
        for d in SIDES:
            self.wire.recv(self.t1b.at[h, i, side(d)], self.t1(h, i, d), net.dev(h, 0, -d))
        total = self.load(h, da, 0) + self.t1b[h, i, 0].astype(F32) + self.t1b[h, i, 1].astype(F32)
        if da != 2:
            self.row_sum[h, i] = total
            return
        self.s2s[h] = total.astype(BF16)
        for d in SIDES:
            p = side(d)
            self.wire.send(self.s2s.at[h, self.part(p)], self.s2b.at[h, p], self.s2(h, d), net.dev(h, d, 0))

    def d(self, h, d):
        i, p, net = RING.index(d), side(d), self.net
        self.wire.recv(self.s2b.at[h, p], self.s2(h, d), net.dev(h, -d, 0))
        added = self.row_sum[h, i, self.part(p)] + self.s2b[h, p].astype(F32)
        self.s1s[h, p, self.part(p)] = added.astype(BF16)
        self.s1s[h, p, self.part(1 - p)] = self.row_sum[h, i, self.part(1 - p)].astype(BF16)
        self.wire.send(self.s1s.at[h, p], self.s1b.at[h, p], self.s1(h, d), net.dev(h, d, 0))

    def e(self, h):
        for d in SIDES:
            self.wire.recv(self.s1b.at[h, side(d)], self.s1(h, d), self.net.dev(h, -d, 0))
        self.emit(h, self.row_sum[h, 0] + self.s1b[h, 0].astype(F32) + self.s1b[h, 1].astype(F32))

    def all_a(self):
        for da in self.ORDER:
            for h in (0, 1):
                self.a(h, da)

    def all_b(self):
        for da in self.ORDER:
            for h in (0, 1):
                for d in SIDES:
                    self.b(h, da, d)

    def all_c(self):
        for da in self.ORDER:
            for h in (0, 1):
                self.c(h, da)

    def all_d(self):
        for h in (0, 1):
            for d in SIDES:
                self.d(h, d)

    def all_e(self):
        for h in (0, 1):
            self.e(h)


BLOCK = 512


def spread_heads(rows_t, padded, natural):
    padded[...] = jnp.zeros_like(padded)
    for g in range(4):
        for k in range(4):
            head = 4 * g + k
            padded[g, g * 64 : g * 64 + 64, k * 128 : k * 128 + 128] = rows_t[head * 64 : head * 64 + 64]
        natural[g * 512 : g * 512 + 512] = padded[g].T


def attend_kernel(
    x_ref,
    qkv_in,
    out_in,
    cot_ref,
    cos_ref,
    sin_ref,
    gp_ref,
    block_ref,
    parts_o,
    qkv_hbm,
    qkv_own,
    proj,
    kv_in,
    kv_ref,
    out_full,
    kvg_ref,
    terms,
    qt,
    qn,
    dot_,
    don,
    probs,
    peaks,
    peak,
    total,
    acc,
    dqt,
    dots,
    att_t,
    do_sib,
    sib_o,
    sum_o,
    far_out,
    far_in,
    send_sems,
    recv_sems,
    local_sems,
    *bufs,
):
    net = Net()
    wire = Wire(send_sems, recv_sems, (sum_o, None), net.sibling())
    s, x, zh, core = net.s, net.x, net.zh, net.core
    other = 1 - zh

    def kv_place(ref, group):
        def piece(gx, gy, h, part):
            row = (group * 16 + gx * 4 + gy) * 128 + h * 64
            if part is None:
                return ref.at[pl.ds(pl.multiple_of(row, 32), 64)]
            return ref.at[pl.ds(pl.multiple_of(row + part * 32, 32), 32)]

        return piece

    def kv_rows(shard):
        return kv_ref.at[pl.ds(pl.multiple_of(shard * 128, 128), 128)]

    far_shard = lax.rem(s + 16, 32)
    half_cols = pl.ds(pl.multiple_of(core * 1024, 128), 1024)
    panels = pl.ds(core * 3, 3)

    def qkv_at(which, row, count):
        return probs.at[which, row // 512, pl.ds(pl.multiple_of(lax.rem(row, 512), 16), count)]

    def qkv_place(group):
        def piece(gx, gy, h, part):
            row = (group * 16 + gx * 4 + gy) * 64 + h * 32
            return qkv_at(panels, row, 32) if part is None else qkv_at(panels, row + part * 16, 16)

        return piece

    def qkv_half(group, which):
        return probs.at[pl.ds(which * 3, 3), pl.ds(group * 2, 2)]

    def out_cols(h):
        return pl.ds(pl.multiple_of(core * 1024 + h * 512, 128), 512)

    def out_place(group):
        def piece(gx, gy, h, part):
            row = (group * 16 + gx * 4 + gy) * 32
            if part is None:
                return out_full.at[pl.ds(pl.multiple_of(row, 16), 32), out_cols(h)]
            return out_full.at[pl.ds(pl.multiple_of(row + part * 16, 16), 16), out_cols(h)]

        return piece

    def out_half(group, which):
        columns = pl.ds(pl.multiple_of(which * 1024, 128), 1024)
        return out_full.at[pl.ds(pl.multiple_of(group * 512, 32), 512), columns]

    def out_rows(shard):
        return out_full.at[pl.ds(pl.multiple_of(shard * 32, 32), 32), half_cols]

    for p in range(6):
        qkv_own[p] = qkv_in[:, p * 256 : p * 256 + 256]
    greet(net.xy_neighbours() + [net.sibling(), net.partner()])

    zq = wire.new(1)
    wire.send(qkv_own.at[panels], qkv_at(panels, s * 64, 64), zq, net.partner())
    near_q = gather_stages(net, wire, lambda h: qkv_own.at[panels, pl.ds(h * 32, 32)], qkv_place(zh))
    near_q[0]()
    probs[panels, (s * 64) // 512, pl.ds(pl.multiple_of(lax.rem(s * 64, 512), 64), 64)] = qkv_own[panels]
    out_full[pl.ds(pl.multiple_of(s * 32, 32), 32), half_cols] = out_in[:, half_cols]
    peak[...] = jnp.full_like(peak, NEG_FILL)
    total[...] = jnp.zeros_like(total)
    acc[...] = jnp.zeros_like(acc)
    dqt[...] = jnp.zeros_like(dqt)
    for stage in near_q[1:6]:
        stage()
    wire.recv(qkv_at(panels, far_shard * 64, 64), zq, net.partner())
    zo = wire.new(1)
    wire.send(out_in.at[:, half_cols], out_rows(s), zo, net.partner())
    far_qp = qkv_place(other)
    far_q = gather_stages(net, wire, lambda h: far_qp(net.x, net.y, h, None), far_qp)
    far_q[0]()
    near_q[6]()
    share_q = wire.new(2)
    wire.send(qkv_half(zh, core), qkv_half(zh, core), share_q, net.sibling())
    for stage in far_q[1:3]:
        stage()

    def project(group, first):
        def step(p, carry):
            columns = pl.ds(pl.multiple_of(p * 256, 256), 256)
            result = jnp.zeros((128, 256), F32) if first else proj[:, columns]
            for b in (0, 1):
                rows = pl.ds(pl.multiple_of(group * 1024 + b * 512, 512), 512)
                result = result + jnp.dot(x_ref[:, rows], probs[p, group * 2 + b], preferred_element_type=F32)
            proj[:, columns] = result
            return carry

        lax.fori_loop(0, 6, step, 0)

    for stage in far_q[3:5]:
        stage()
    wire.recv(qkv_half(zh, 1 - core), share_q, net.sibling())
    project(zh, True)
    for stage in far_q[5:]:
        stage()
    wire.send(qkv_half(other, core), qkv_half(other, core), share_q + 1, net.sibling())
    early = wire.taken()
    near_o = gather_stages(net, wire, lambda h: out_in.at[:, out_cols(h)], out_place(zh))
    near_o[0]()
    wire.recv(qkv_half(other, 1 - core), share_q + 1, net.sibling())
    keep = []
    for p in range(6):
        for b in range(4):
            place = qkv_hbm.at[pl.ds(b * 512, 512), pl.ds(p * 256, 256)]
            keep.append(pltpu.make_async_copy(probs.at[p, b], place, local_sems.at[p * 4 + b]))
    for made in keep:
        made.start()
    project(other, False)
    cos, sin = cos_ref[...], sin_ref[...]

    def turn(rows_t):
        a, b = rows_t[0:32], rows_t[32:64]
        return [a * cos - b * sin, b * cos + a * sin]

    for c in (0, 1):
        keys_t = proj[:, 1024 + c * 128 : 1152 + c * 128].T
        pair = turn(keys_t[0:64]) + turn(keys_t[64:128])
        kv_in[:, c * 128 : c * 128 + 128] = jnp.concatenate(pair, axis=0).astype(BF16).T
    kv_in[:, 256:512] = proj[:, 1280:1536].astype(BF16)

    zkey = wire.new(1)
    wire.send(kv_in, kv_rows(s), zkey, net.partner())
    near = gather_stages(net, wire, lambda h: kv_in.at[pl.ds(h * 64, 64)], kv_place(kv_ref, zh))
    near[0]()
    near_o[1]()
    kv_ref[pl.ds(pl.multiple_of(s * 128, 128), 128)] = kv_in[...]
    pieces = []
    for c in range(8):
        queries_t = proj[:, c * 128 : c * 128 + 128].T
        pieces += turn(queries_t[0:64]) + turn(queries_t[64:128])
    spread_heads((jnp.concatenate(pieces, axis=0).astype(BF16).astype(F32) * 0.125).astype(BF16), qt, qn)
    near[1]()
    near_o[2]()
    near[2]()
    near_o[3]()
    near[3]()
    near[4]()
    near_o[4]()
    near[5]()
    near_o[5]()
    wire.recv(kv_rows(far_shard), zkey, net.partner())
    far_place = kv_place(kv_ref, other)
    far = gather_stages(net, wire, lambda h: far_place(net.x, net.y, h, None), far_place)
    far[0]()
    wire.recv(out_rows(far_shard), zo, net.partner())
    far_op = out_place(other)
    far_o = gather_stages(net, wire, lambda h: far_op(net.x, net.y, h, None), far_op)
    far_o[0]()
    near[6]()
    near_o[6]()
    share_o = wire.new(2)
    wire.send(out_half(zh, core), out_half(zh, core), share_o, net.sibling())
    for made in keep:
        made.wait()
    wire.drain(early)

    def rows_of(j):
        return pl.ds(pl.multiple_of(j * BLOCK, BLOCK), BLOCK)

    def forward(j, masked):
        keys = kv_ref[rows_of(j), 0:256]
        values_t = kv_ref[rows_of(j), 256:512].T
        if masked:
            key_at = lax.broadcasted_iota(jnp.int32, (BLOCK, 512), 0) + j * BLOCK
            query_at = lax.rem(lax.broadcasted_iota(jnp.int32, (BLOCK, 512), 1), 128) + s * 128
            visible = key_at <= query_at
        ahead = jnp.dot(keys, qt[0], preferred_element_type=F32)
        for g in range(4):
            scores = ahead
            if g < 3:
                ahead = jnp.dot(keys, qt[g + 1], preferred_element_type=F32)
            if masked:
                scores = jnp.where(visible, scores, NEG_FILL)
            before = peak[g]
            now = jnp.maximum(before, jnp.max(scores, axis=0, keepdims=True))
            fade = jnp.exp(before - now)
            e = jnp.exp(scores - now)
            total[g] = total[g] * fade + jnp.sum(e, axis=0, keepdims=True)
            e = e.astype(BF16)
            for c in (0, 1):
                probs[4 * g + j // 2, lax.rem(j, 2) * 2 + c] = e[:, c * 256 : c * 256 + 256]
            peaks[g, j] = now
            peak[g] = now
            acc[g] = acc[g] * fade + jnp.dot(values_t[g * 64 : g * 64 + 64], e, preferred_element_type=F32)

    def in_turn(plans, i):
        for k, plan in enumerate(plans):

            @pl.when(i == k)
            def _():
                for stage in plan:
                    stage()

    def near_forward(i, carry):
        in_turn([[far[1], far_o[1]], [far[2], far_o[2]], [far[3], far_o[3]], [far[4], far_o[4]]], i)

        @pl.when(i < x)
        def _():
            forward(zh * 4 + i, False)

        @pl.when(i == x)
        def _():
            forward(zh * 4 + i, True)

        return carry

    lax.fori_loop(0, 4, near_forward, 0)
    far[5]()
    far_o[5]()

    def landed(h, da, d):
        key = far.base + 24 + (h * 4 + RING.index(da)) * 2 + side(d)
        wire.recv(far_place(*net.at(h, da, 2), h, side(d)), key, net.dev(h, 0, -d))

    def far_forward(i, carry):
        for k, da in enumerate((0, 1, -1, 2)):

            @pl.when(i == k)
            def _(da=da):
                for d in SIDES:
                    landed(0, da, d)
                if da == 2:
                    for db in RING:
                        for d in SIDES:
                            landed(1, db, d)

        @pl.when(zh == 1)
        def _():
            forward(lax.rem(x + lax.rem(8 + i - 3 * ((i * (i - 1)) // 2) + 4 * i, 4), 4), False)

        return carry

    lax.fori_loop(0, 4, far_forward, 0)
    far_o[6]()
    wire.send(out_half(other, core), out_half(other, core), share_o + 1, net.sibling())

    for g in range(4):
        attended = (acc[g] / total[g]).astype(BF16)
        for k in range(4):
            head = 4 * g + k
            att_t[head * 64 : head * 64 + 64] = attended[:, k * 128 : k * 128 + 128]
    core_key = wire.new(2)
    for g in (0, 1):
        rows = slice(g * 512, g * 512 + 512)
        sib_cols = pl.ds(pl.multiple_of((1 - core) * 1024, 128), 1024)
        do_sib[rows] = jnp.dot(att_t[rows], cot_ref[:, sib_cols], preferred_element_type=F32).astype(BF16)
        wire.send(do_sib.at[pl.ds(g * 512, 512)], sib_o.at[pl.ds(g * 512, 512)], core_key + g, net.sibling())
    wire.recv(out_half(zh, 1 - core), share_o, net.sibling())
    wire.recv(out_half(other, 1 - core), share_o + 1, net.sibling())
    grad_t = lax.dot_general(
        out_full[...], cot_ref[...], (((1,), (1,)), ((), ())), preferred_element_type=F32
    ).astype(BF16)
    spread_heads(grad_t, dot_, don)
    for g in range(4):
        for k in range(4):
            head = 4 * g + k
            rows = slice(head * 64, head * 64 + 64)
            both = att_t[rows].astype(F32) * dot_[g, g * 64 : g * 64 + 64, k * 128 : k * 128 + 128].astype(F32)
            dots[g, :, k * 128 : k * 128 + 128] = jnp.sum(both, axis=0, keepdims=True)
        peak[g] = peak[g] + jnp.log(total[g])

    def out_own(group):
        def piece(gx, gy, h, part):
            row = (group * 16 + gx * 4 + gy) * 32
            if part is None:
                return sum_o.at[pl.ds(pl.multiple_of(row, 16), 32), pl.ds(h * 512, 512)]
            return sum_o.at[pl.ds(pl.multiple_of(row + part * 16, 16), 16), pl.ds(h * 512, 512)]

        return piece

    def out_emit(group):
        def emit(h, result):
            for part in (0, 1):
                parts_o[group, 2 * h + part] = result[:, part * 256 : part * 256 + 256]

        return emit

    scat_o = [Scatter(net, wire, out_own(g), bufs[16 + 8 * g : 24 + 8 * g], out_emit(g)) for g in (0, 1)]

    def add_cores(g):
        def run():
            rows = slice(g * 512, g * 512 + 512)
            wire.recv(sib_o.at[pl.ds(g * 512, 512)], core_key + g, net.sibling())
            own = jnp.dot(att_t[rows], cot_ref[:, half_cols], preferred_element_type=F32)
            sum_o[rows] = (own + sib_o[rows].astype(F32)).astype(BF16)
            scat_o[g].all_a()

        return run

    def backward(j):
        keys_t = kv_ref[rows_of(j), 0:256].T
        values = kv_ref[rows_of(j), 256:512]
        ahead = jnp.dot(values, dot_[0], preferred_element_type=F32)
        dk = dv = None
        for g in range(4):
            grads = ahead
            if g < 3:
                ahead = jnp.dot(values, dot_[g + 1], preferred_element_type=F32)
            e = jnp.concatenate([probs[4 * g + j // 2, lax.rem(j, 2) * 2 + c] for c in (0, 1)], axis=1)
            p = e.astype(F32) * jnp.exp(peaks[g, j] - peak[g])
            ds = (p * (grads - dots[g])).astype(BF16)
            p = p.astype(BF16)
            dqt[g] += jnp.dot(keys_t[g * 64 : g * 64 + 64], ds, preferred_element_type=F32)
            rows = slice(g * 512, g * 512 + 512)
            dk_g = jnp.dot(ds, qn[rows], preferred_element_type=F32)
            dv_g = jnp.dot(p, don[rows], preferred_element_type=F32)
            dk = dk_g if g == 0 else dk + dk_g
            dv = dv_g if g == 0 else dv + dv_g
        terms[rows_of(j), 0:256] = dk.astype(BF16)
        terms[rows_of(j), 256:512] = dv.astype(BF16)

    zback = wire.new(2)

    def emit_far(h, result):
        far_out[h] = result.astype(BF16)
        wire.send(far_out.at[h], far_in.at[h], zback + h, net.partner())

    def emit_near(h, result):
        kvg_ref[pl.ds(h * 64, 64)] = result

    scat_far = Scatter(net, wire, kv_place(terms, other), bufs[0:8], emit_far)
    scat_near = Scatter(net, wire, kv_place(terms, zh), bufs[8:16], emit_near)

    def after(scat):
        one = functools.partial

        def plan0():
            scat.a(0, 2)
            for da in scat.ORDER:
                scat.a(1, da)

        def plan1():
            scat.a(0, 1)
            for da in scat.ORDER:
                scat.b(1, da, 1)
            for d in SIDES:
                scat.b(0, 2, d)

        def plan2():
            scat.a(0, -1)
            for da in scat.ORDER:
                scat.b(1, da, -1)
            for d in SIDES:
                scat.b(0, 1, d)
            scat.c(0, 2)

        def plan3():
            scat.a(0, 0)
            scat.c(1, 2)
            for d in SIDES:
                scat.b(0, -1, d)
            scat.c(0, 1)

        return [[plan0], [plan1], [plan2], [plan3]]

    def late1(scat):
        def run():
            scat.c(1, 1)
            scat.c(1, -1)
            for d in SIDES:
                scat.b(0, 0, d)
            for d in SIDES:
                scat.d(1, d)
            scat.c(0, -1)
            for d in SIDES:
                scat.d(0, d)

        return run

    def late2(scat):
        def run():
            scat.c(1, 0)
            scat.c(0, 0)

        return run

    def block_loop(group, plans):
        def step(i, carry):
            turn = lax.rem(18 - i + 3 * ((i * (i - 1)) // 2), 4)
            j = group * 4 + lax.rem(x + turn, 4)

            @pl.when(j <= s // 4)
            def _():
                backward(j)

            @pl.when(j > s // 4)
            def _():
                terms[rows_of(j)] = jnp.zeros((BLOCK, 512), BF16)

            in_turn(plans, i)
            return carry

        lax.fori_loop(0, 4, step, 0)

    plans = after(scat_far)
    plans[1].append(add_cores(0))
    plans[2].append(add_cores(1))
    plans[3].append(scat_o[0].all_b)
    block_loop(other, plans)
    plans = after(scat_near)
    plans[0] = [late1(scat_far)] + plans[0] + [scat_o[1].all_b]
    plans[1] = [late2(scat_far)] + plans[1] + [scat_o[0].all_c]
    plans[2] = [scat_far.all_e] + plans[2] + [scat_o[1].all_c, scat_o[0].all_d]
    plans[3] = plans[3] + [scat_o[1].all_d, scat_o[0].all_e]
    block_loop(zh, plans)
    late1(scat_near)()
    attended = att_t[...].T
    for c in range(4):
        cols = slice(c * 512, c * 512 + 512)
        block_ref[:, cols] = jnp.dot(attended, out_full[:, cols], preferred_element_type=F32).astype(BF16)
    def turn_back(rows_t):
        a, b = rows_t[0:32], rows_t[32:64]
        return jnp.concatenate([a * cos + b * sin, b * cos - a * sin], axis=0)

    for g in range(4):
        for k in range(0, 4, 2):
            head = 4 * g + k
            pair = [turn_back(dqt[g, :, c * 128 : c * 128 + 128] * 0.125) for c in (k, k + 1)]
            gp_ref[:, head * 64 : head * 64 + 128] = jnp.concatenate(pair, axis=0).T.astype(BF16)
    scat_o[1].all_e()
    late2(scat_near)()
    scat_near.all_e()
    for h in (0, 1):
        wire.recv(far_in.at[h], zback + h, net.partner())
        kvg_ref[pl.ds(h * 64, 64)] += far_in[h].astype(F32)
    for c in range(2):
        keys_t = kvg_ref[:, c * 128 : c * 128 + 128].T
        pair = [turn_back(keys_t[0:64]), turn_back(keys_t[64:128])]
        gp_ref[:, 1024 + c * 128 : 1152 + c * 128] = jnp.concatenate(pair, axis=0).T.astype(BF16)
    gp_ref[:, 1280:1536] = kvg_ref[:, 256:512].astype(BF16)
    wire.drain()


def attend(inputs, qkv_weight, out_weight, cotangent, cos_t, sin_t):
    keys = 10 * AG_KEYS + 11
    return pl.pallas_call(
        attend_kernel,
        out_shape=(
            jax.ShapeDtypeStruct((128, 1536), BF16),
            jax.ShapeDtypeStruct((128, 2048), BF16),
            jax.ShapeDtypeStruct((2, 4, 32, 256), F32),
            jax.ShapeDtypeStruct((2048, 1536), BF16),
        ),
        in_specs=[pl.BlockSpec(memory_space=pltpu.VMEM)] * 6,
        out_specs=[pl.BlockSpec(memory_space=pltpu.VMEM)] * 3 + [pl.BlockSpec(memory_space=pl.ANY)],
        scratch_shapes=[
            pltpu.VMEM((6, 64, 256), BF16),
            pltpu.VMEM((128, 1536), F32),
            pltpu.VMEM((128, 512), BF16),
            pltpu.VMEM((4096, 512), BF16),
            pltpu.VMEM((1024, 2048), BF16),
            pltpu.VMEM((128, 512), F32),
            pltpu.VMEM((4096, 512), BF16),
            pltpu.VMEM((4, 256, 512), BF16),
            pltpu.VMEM((2048, 256), BF16),
            pltpu.VMEM((4, 256, 512), BF16),
            pltpu.VMEM((2048, 256), BF16),
            pltpu.VMEM((16, 4, BLOCK, 256), BF16),
            pltpu.VMEM((4, 8, 1, 512), F32),
            pltpu.VMEM((4, 1, 512), F32),
            pltpu.VMEM((4, 1, 512), F32),
            pltpu.VMEM((4, 64, 512), F32),
            pltpu.VMEM((4, 64, 512), F32),
            pltpu.VMEM((4, 1, 512), F32),
            pltpu.VMEM((1024, 128), BF16),
            pltpu.VMEM((1024, 1024), BF16),
            pltpu.VMEM((1024, 1024), BF16),
            pltpu.VMEM((1024, 1024), BF16),
            pltpu.VMEM((2, 64, 512), BF16),
            pltpu.VMEM((2, 64, 512), BF16),
            pltpu.SemaphoreType.DMA((keys,)),
            pltpu.SemaphoreType.DMA((keys,)),
            pltpu.SemaphoreType.DMA((24,)),
            *scatter_scratch(64, 512),
            *scatter_scratch(64, 512),
            *scatter_scratch(32, 512),
            *scatter_scratch(32, 512),
        ],
        compiler_params=pltpu.CompilerParams(
            collective_id=0, has_side_effects=True, vmem_limit_bytes=VMEM_BYTES
        ),
        name="attend",
    )(inputs, qkv_weight, out_weight, cotangent, cos_t, sin_t)


def weight_grad_kernel(
    scale,
    x_ref,
    gp_ref,
    w_ref,
    parts_o,
    tg_ref,
    out_q,
    out_o,
    xt,
    do_sib,
    sib_q,
    sum_q,
    zs_q,
    zs_o,
    zr_q,
    zr_o,
    keep_q,
    fin_q,
    fin_o,
    got_q,
    got_o,
    canvas,
    send_sems,
    recv_sems,
    *bufs,
):
    net = Net()
    wire = Wire(send_sems, recv_sems, (canvas, None), net.sibling())
    core = net.core
    cols_q = [pl.ds(pl.multiple_of(c * 768, 128), 768) for c in (core, 1 - core)]
    cols_o = [pl.ds(pl.multiple_of(c * 1024, 128), 1024) for c in (core, 1 - core)]
    greet(net.xy_neighbours() + [net.sibling()] + [net.up(k) for k in range(1, 8)])

    z1 = wire.new(14)

    def z_send(k, staged, slots, key):
        target = lax.rem(net.z + k, 8)
        wire.send(staged.at[target // 4, lax.rem(target, 4)], slots.at[k - 1], key + k - 1, net.up(k))

    for g in (0, 1):
        for l in range(4):
            zs_o[g, l] = parts_o[g, l].astype(BF16)
    for k in range(1, 8):
        z_send(k, zs_o, zr_o, z1)

    xt[...] = x_ref[...].T
    ckey = wire.new(2)

    def product(rows, cols):
        return jnp.dot(xt[rows], gp_ref[:, cols], preferred_element_type=F32)

    def make_sibling(g):
        def step(i, carry):
            rows = pl.ds(pl.multiple_of(g * 1024 + i * 256, 256), 256)
            do_sib[rows] = product(rows, cols_q[1]).astype(BF16)
            return carry

        lax.fori_loop(0, 4, step, 0)
        rows = pl.ds(g * 1024, 1024)
        wire.send(do_sib.at[rows], sib_q.at[rows], ckey + g, net.sibling())

    def add_cores(g):
        wire.recv(sib_q.at[pl.ds(g * 1024, 1024)], ckey + g, net.sibling())

        def step(i, carry):
            rows = pl.ds(pl.multiple_of(g * 1024 + i * 256, 256), 256)
            sum_q[rows] = (product(rows, cols_q[0]) + sib_q[rows].astype(F32)).astype(BF16)
            return carry

        lax.fori_loop(0, 4, step, 0)

    def own_q(g):
        def piece(gx, gy, h, part):
            row = (g * 16 + gx * 4 + gy) * 64 + h * 32
            if part is None:
                return sum_q.at[pl.ds(pl.multiple_of(row, 16), 32)]
            return sum_q.at[pl.ds(pl.multiple_of(row + part * 16, 16), 16)]

        return piece

    def emit_q(g):
        def emit(h, result):
            for part in (0, 1):
                rows = result[part * 16 : part * 16 + 16]
                keep_q[g, 2 * h + part] = rows
                zs_q[g, 2 * h + part] = rows.astype(BF16)

        return emit

    runs = [Scatter(net, wire, own_q(g), bufs[8 * g : 8 * g + 8], emit_q(g)) for g in (0, 1)]

    def tokens_grad(c):
        rows = slice(c * 512, c * 512 + 512)
        tg_ref[:, rows] = lax.dot_general(
            gp_ref[...], w_ref[rows], (((1,), (1,)), ((), ())), preferred_element_type=F32
        ).astype(BF16)

    make_sibling(0)
    make_sibling(1)
    add_cores(0)
    runs[0].all_a()
    add_cores(1)
    runs[1].all_a()
    tokens_grad(0)
    runs[0].all_b()
    runs[1].all_b()
    tokens_grad(1)
    for run in runs:
        run.c(0, 2)
        run.c(1, 2)
    for run in runs:
        for da in (1, -1):
            run.c(0, da)
            run.c(1, da)
    tokens_grad(2)
    runs[0].all_d()
    runs[1].all_d()
    tokens_grad(3)
    for run in runs:
        run.c(0, 0)
        run.c(1, 0)
    runs[0].all_e()
    runs[1].all_e()

    z1q = z1 + 7
    for k in range(1, 8):
        z_send(k, zs_q, zr_q, z1q)

    def place(l):
        return (
            got_q.at[pl.ds(pl.multiple_of(l * 16, 16), 16), cols_q[0]],
            got_o.at[:, pl.ds(pl.multiple_of(core * 1024 + l * 256, 128), 256)],
        )

    def level(k):
        l = lax.rem(net.zl + k, 4)
        return l, (net.s, l * 2 + core)

    z2 = wire.new(6)
    mine = place(net.zl)

    def z_sum(first, slots, key):
        result = first
        for k in range(1, 8):
            wire.recv(slots.at[k - 1], key + k - 1, net.up(8 - k))
            result = result + slots[k - 1].astype(F32)
        return (result * scale).astype(BF16)

    def z_spread(which, ref, key):
        for k in (1, 2, 3):
            wire.send(ref, mine[which], key + k - 1, level(k)[1])

    fin_o[...] = z_sum(parts_o[net.zh, net.zl], zr_o, z1)
    z_spread(1, fin_o, z2)
    got_o[:, pl.ds(pl.multiple_of(core * 1024 + net.zl * 256, 128), 256)] = fin_o[...]
    fin_q[...] = z_sum(keep_q[net.zh, net.zl], zr_q, z1q)
    z_spread(0, fin_q, z2 + 3)
    got_q[pl.ds(pl.multiple_of(net.zl * 16, 16), 16), cols_q[0]] = fin_q[...]
    last = wire.new(2)
    for k in (1, 2, 3):
        l, device = level(4 - k)
        wire.recv(place(l)[1], z2 + k - 1, device)
    wire.send(got_o.at[:, cols_o[0]], got_o.at[:, cols_o[0]], last, net.sibling())
    for k in (1, 2, 3):
        l, device = level(4 - k)
        wire.recv(place(l)[0], z2 + 3 + k - 1, device)
    wire.send(got_q.at[:, cols_q[0]], got_q.at[:, cols_q[0]], last + 1, net.sibling())
    wire.recv(got_o.at[:, cols_o[1]], last, net.sibling())
    wire.recv(got_q.at[:, cols_q[1]], last + 1, net.sibling())
    out_o[...] = got_o[...].astype(F32)
    out_q[...] = got_q[...].astype(F32)
    wire.drain()


def weight_grads(inputs, grad_proj, qkv_full, parts_o, scale):
    keys = 2 * AG_KEYS + 14 + 2 + 6 + 2
    return pl.pallas_call(
        functools.partial(weight_grad_kernel, scale),
        out_shape=(
            jax.ShapeDtypeStruct((128, 2048), BF16),
            jax.ShapeDtypeStruct((64, 1536), F32),
            jax.ShapeDtypeStruct((32, 2048), F32),
        ),
        in_specs=[pl.BlockSpec(memory_space=pltpu.VMEM)] * 4,
        out_specs=[pl.BlockSpec(memory_space=pltpu.VMEM)] * 3,
        scratch_shapes=[
            pltpu.VMEM((2048, 128), BF16),
            pltpu.VMEM((2048, 768), BF16),
            pltpu.VMEM((2048, 768), BF16),
            pltpu.VMEM((2048, 768), BF16),
            pltpu.VMEM((2, 4, 16, 768), BF16),
            pltpu.VMEM((2, 4, 32, 256), BF16),
            pltpu.VMEM((7, 16, 768), BF16),
            pltpu.VMEM((7, 32, 256), BF16),
            pltpu.VMEM((2, 4, 16, 768), F32),
            pltpu.VMEM((16, 768), BF16),
            pltpu.VMEM((32, 256), BF16),
            pltpu.VMEM((64, 1536), BF16),
            pltpu.VMEM((32, 2048), BF16),
            pltpu.VMEM((1024, 1024), BF16),
            pltpu.SemaphoreType.DMA((keys,)),
            pltpu.SemaphoreType.DMA((keys,)),
            *scatter_scratch(32, 768),
            *scatter_scratch(32, 768),
        ],
        compiler_params=pltpu.CompilerParams(
            collective_id=2, has_side_effects=True, vmem_limit_bytes=VMEM_BYTES
        ),
        name="weight_grads",
    )(inputs, grad_proj, qkv_full, parts_o)


def finish_kernel(*refs):
    for i in range(4):
        refs[i + 4][...] = refs[i][...]


def finish(*results):
    return pl.pallas_call(
        finish_kernel,
        out_shape=tuple(jax.ShapeDtypeStruct(r.shape, r.dtype) for r in results),
        in_specs=[pl.BlockSpec(memory_space=pltpu.VMEM)] * 4,
        out_specs=[pl.BlockSpec(memory_space=pltpu.VMEM)] * 4,
        name="finish",
    )(*results)


def tables(positions, head_size):
    halves = head_size // 2
    frequency = ROPE_BASE ** (-(jnp.arange(halves, dtype=jnp.float32) * 2.0) / head_size)
    angles = positions.astype(jnp.float32)[:, None] * frequency[None, :]
    return (jnp.cos(angles), jnp.sin(angles))


def rotate(matrix, cos_rows, sin_rows, head_count):
    row_count = matrix.shape[0]
    head_size = matrix.shape[1] // head_count
    halves = head_size // 2
    pieces = matrix.reshape(row_count, head_count, 2, halves)
    lower_half = pieces[:, :, 0]
    upper_half = pieces[:, :, 1]
    cos_part = cos_rows[:, None, :]
    sin_part = sin_rows[:, None, :]
    turned = jnp.stack(
        [
            lower_half * cos_part - upper_half * sin_part,
            upper_half * cos_part + lower_half * sin_part,
        ],
        axis=2,
    )
    return turned.reshape(row_count, head_count * head_size)


def body(tokens, qkv_weight, out_weight, cotangent):
    inputs = tokens[0]
    tok_count = inputs.shape[0]
    positions = lax.axis_index("shard") * tok_count + jnp.arange(tok_count, dtype=jnp.int32)
    cosine, sine = tables(positions, HEAD_DIM)
    grad_proj, block_output, parts_o, qkv_full = attend(
        inputs, qkv_weight, out_weight, cotangent[0], cosine.T, sine.T
    )
    norm_factor = 1.0 / math.sqrt(lax.axis_size("rep") * lax.axis_size("shard") * tok_count)
    tokens_grad, qkv_grad, out_grad = weight_grads(inputs, grad_proj, qkv_full, parts_o, norm_factor)
    block_output, tokens_grad, qkv_grad, out_grad = finish(block_output, tokens_grad, qkv_grad, out_grad)
    return (block_output[None], tokens_grad[None], qkv_grad, out_grad)


def solution(mesh):
    return jax.shard_map(
        body,
        mesh=mesh,
        in_specs=(
            P("rep", "shard", None),
            P("shard", None),
            P("shard", None),
            P("rep", "shard", None),
        ),
        out_specs=(
            P("rep", "shard", None),
            P("rep", "shard", None),
            P("shard", None),
            P("shard", None),
        ),
        check_vma=False,
    )
```
